32 devices in a mesh: dp: 8 (over z, y), tensor: 4 (over x, core).
Axes of the slice: x: 2, y: 2, z: 4, core: 2. Of those that a mesh axis runs over, the one named last changes fastest.
Arguments:
- tokens: bfloat16 [12288, 1024], P(('dp', 'tensor')), may hold values from -6 to 6
- encoder: bfloat16 [8, 1024, 1024], P('dp', 'tensor'), may hold values from -6 to 6
- seg_ids: int32 [8, 1536], P('dp'), may hold values from 0 to 3, as said below
- enc_lens: int32 [8], P('dp'), may hold values from 128 to 1024, as said below
- attn_qkv: float32 [3, 1024, 1024], P(None, 'dp', 'tensor'), may hold values from -0.1875 to 0.1875
- attn_out: float32 [1024, 1024], P('tensor', 'dp'), may hold values from -0.5 to 0.5
- cross_q: float32 [1024, 1024], P('dp', 'tensor'), may hold values from -0.1875 to 0.1875
- cross_kv: float32 [2, 1024, 1024], P(None, 'dp', 'tensor'), may hold values from -0.1875 to 0.1875
- cross_out: float32 [1024, 1024], P('tensor', 'dp'), may hold values from -0.75 to 0.75
- ffn_in: float32 [1024, 4096], P('dp', 'tensor'), may hold values from -0.1875 to 0.1875
- ffn_out: float32 [4096, 1024], P('tensor', 'dp'), may hold values from -0.09375 to 0.09375
- norm_gains: float32 [3, 1024], replicated, may hold values from 0.5 to 1.5
- norm_biases: float32 [3, 1024], replicated, may hold values from -1.5 to 1.5
- out_grad: bfloat16 [12288, 1024], P(('dp', 'tensor')), may hold values from -6 to 6
Outputs:
- out_tokens: bfloat16 [12288, 1024], P(('dp', 'tensor'))
- in_grad: float32 [12288, 1024], P(('dp', 'tensor'))
- enc_grad: float32 [8, 1024, 1024], P('dp', 'tensor')
- attn_qkv_grad: float32 [3, 1024, 1024], P(None, 'dp', 'tensor')
- attn_out_grad: float32 [1024, 1024], P('tensor', 'dp')
- cross_q_grad: float32 [1024, 1024], P('dp', 'tensor')
- cross_kv_grad: float32 [2, 1024, 1024], P(None, 'dp', 'tensor')
- cross_out_grad: float32 [1024, 1024], P('tensor', 'dp')
- ffn_in_grad: float32 [1024, 4096], P('dp', 'tensor')
- ffn_out_grad: float32 [4096, 1024], P('tensor', 'dp')
- gain_grad: float32 [3, 1024], replicated
- bias_grad: float32 [3, 1024], replicated
The draws below stay inside these ranges and needn't reach their ends.
Inputs may be any that keep to these rules, and one draw needn't show every extreme that they name: `seg_ids`: in each sequence the document numbers never fall and every number 0 to 3 occurs; a document has 153 to 768 tokens, and one of each sequence has exactly 768. `enc_lens`: some sequence has all 1024 positions valid.
All inputs are finite; a program needn't handle non-finite values.
Results may differ from the reference program's by a relative error of at most 0.019.
Values may be sent and summed in bfloat16 or wider, within the bound.
A program may use at most 128 MiB of HBM per device.

```python
import jax
import jax.numpy as jnp
from jax import lax

D = 1024
HEADS = 16
HD = 64
FF = 4096
DOCS = 4
SEQ = 1536
ENC = 1024
SEQS = 8
TOKENS = 12288


def draw_enc_lens(key, part):
    draw_key, pick_key = jax.random.split(key)
    lengths = jax.random.randint(draw_key, (SEQS,), ENC // 8, ENC + 1, dtype=jnp.int32)
    chosen = jax.random.randint(pick_key, (), 0, SEQS, dtype=jnp.int32)
    return jnp.where(jnp.arange(SEQS, dtype=jnp.int32) == chosen, ENC, lengths).astype(jnp.int32)


def draw_seg_ids(key, part):
    floor_len = SEQ // 10
    most_len = SEQ // 2
    spare_len = SEQ - most_len - (DOCS - 1) * floor_len

    def one_sequence(seq_key):
        cut_key, place_key = jax.random.split(seq_key)
        cut_points = jnp.sort(jax.random.randint(cut_key, (DOCS - 2,), 0, spare_len + 1, dtype=jnp.int32))
        cut_edges = jnp.concatenate([jnp.zeros((1,), jnp.int32), cut_points, jnp.full((1,), spare_len, jnp.int32)])
        other_lens = floor_len + cut_edges[1:] - cut_edges[:-1]
        big_slot = jax.random.randint(place_key, (), 0, DOCS, dtype=jnp.int32)
        slot_ids = jnp.arange(DOCS, dtype=jnp.int32)
        from_slot = jnp.clip(slot_ids - (slot_ids > big_slot).astype(jnp.int32), 0, DOCS - 2)
        doc_lens = jnp.where(slot_ids == big_slot, most_len, other_lens[from_slot]).astype(jnp.int32)
        doc_bounds = jnp.cumsum(doc_lens)[:-1]
        positions = jnp.arange(SEQ, dtype=jnp.int32)
        return jnp.sum((positions[:, None] >= doc_bounds[None, :]).astype(jnp.int32), axis=1)
    return jax.vmap(one_sequence)(jax.random.split(key, SEQS)).astype(jnp.int32)


def raised(values, rng, source, target, shards_of, factor):
    owner, partner = [(jnp.arange(values.shape[axis_at]) // (values.shape[axis_at] // shards_of)).reshape([-1 if axis == axis_at else 1 for axis in range(values.ndim)]) for axis_at in (source, target)]
    chosen = jax.random.permutation(rng, shards_of)[partner]
    strong = (owner == chosen) | (owner == (partner + shards_of // 2) % shards_of)
    return jnp.where(strong, factor * values, values)


def block_levels(own_key, extent, shards, low, largest):
    loudness, own = 1.0, jax.random.fold_in(own_key, 6)
    for position, blocks in shards:
        draws = jnp.exp(jax.random.uniform(jax.random.fold_in(own, position), (blocks,), jnp.float32, low / len(shards), largest / len(shards)))
        loudness = loudness * jnp.repeat(draws, extent[position] // blocks).reshape([-1 if axis == position else 1 for axis in range(len(extent))])
    return loudness


def normal_values(own_key, dims, scale, reach, cuts=(), held_as=jnp.bfloat16):
    gain = block_levels(own_key, dims, cuts, -0.22, 0.18) if cuts else 1.0
    values = jax.random.normal(own_key, dims, jnp.float32) * scale * gain
    return jnp.minimum(jnp.maximum(values, -reach), reach).astype(held_as)


def noise_with(stream_key, shape, deviation, reach, pieces, heavy, kind=jnp.bfloat16):
    array = deviation * jax.random.normal(stream_key, shape, jnp.float32)
    if pieces:
        array = array * block_levels(stream_key, shape, pieces, -0.22, 0.18)
    return jnp.clip(raised(array, jax.random.fold_in(stream_key, 3), *heavy), -reach, reach).astype(kind)


def setup_inputs(seed: int = 0) -> dict:
    splits = jax.random.split(jax.random.key(seed), 15)
    return {
        "tokens": noise_with(splits[0], (TOKENS, D), 1.0, 6.0, ((0, 32),), (0, 1, 32, 2.75)),
        "encoder": normal_values(splits[1], (SEQS, ENC, D), 1.0, 6.0, ((0, 8), (1, 4))),
        "seg_ids": draw_seg_ids(jax.random.fold_in(splits[14], 71), 0),
        "enc_lens": draw_enc_lens(jax.random.fold_in(splits[14], 71), 0),
        "attn_qkv": normal_values(splits[4], (3, D, D), D ** -0.5, 0.1875, ((1, 8), (2, 4)), jnp.float32),
        "attn_out": normal_values(splits[5], (D, D), (D // 8) ** -0.5, 0.5, ((0, 4), (1, 8)), jnp.float32),
        "cross_q": normal_values(splits[6], (D, D), D ** -0.5, 0.1875, ((0, 8), (1, 4)), jnp.float32),
        "cross_kv": normal_values(splits[7], (2, D, D), D ** -0.5, 0.1875, ((1, 8), (2, 4)), jnp.float32),
        "cross_out": normal_values(splits[8], (D, D), (D // 16) ** -0.5, 0.75, ((0, 4), (1, 8)), jnp.float32),
        "ffn_in": normal_values(splits[9], (D, FF), D ** -0.5, 0.1875, ((0, 8), (1, 4)), jnp.float32),
        "ffn_out": normal_values(splits[10], (FF, D), FF ** -0.5, 0.09375, ((0, 4), (1, 8)), jnp.float32),
        "norm_gains": jnp.clip(1.0 + 0.1 * jax.random.normal(splits[11], (3, D), jnp.float32), 0.5, 1.5),
        "norm_biases": normal_values(splits[12], (3, D), 0.3, 1.5, (), jnp.float32),
        "out_grad": noise_with(splits[13], (TOKENS, D), 1.0, 6.0, ((0, 32),), (0, 1, 32, 2.75)),
    }


@jax.custom_vjp
def low(v):
    return lax.optimization_barrier(v.astype(jnp.bfloat16)).astype(jnp.float32)

@jax.custom_vjp
def low_back(v):
    return v

def low_keep(v):
    return (low(v), None)

def low_pass(kept, grad):
    return (grad,)

def back_keep(v):
    return (v, None)

def back_low(kept, grad):
    return (low(grad),)
low.defvjp(low_keep, low_pass)
low_back.defvjp(back_keep, back_low)
epsilon = 1e-05
masked_score = -1e+30

def product(left, right):
    return jnp.dot(left, right, precision=lax.Precision.HIGHEST, preferred_element_type=jnp.float32)

def norm_rows(values_in, gain_row, bias_row):
    average = lax.optimization_barrier(jnp.mean(values_in, axis=-1, keepdims=True))
    centred = values_in - average
    spread = lax.optimization_barrier(jnp.mean(centred * centred, axis=-1, keepdims=True))
    return centred * lax.rsqrt(spread + epsilon) * gain_row + bias_row

def attention(queries, key_rows, value_rows, allowed):
    seq_len = queries.shape[0]
    block_rows = min(512, seq_len)
    score_scale = HD ** (-0.5)

    def one_block(block_index):
        row_start = block_index * block_rows
        query_block = lax.dynamic_slice_in_dim(queries, row_start, block_rows, 0)
        raw_scores = jnp.einsum('qhd,khd->hqk', query_block, key_rows, precision=lax.Precision.HIGHEST)
        scores = low_back(raw_scores) * score_scale
        scores = jnp.where(allowed(row_start, block_rows)[None], scores, masked_score)
        row_peak = lax.optimization_barrier(jnp.max(scores, axis=-1, keepdims=True))
        exponent = jnp.exp(scores - row_peak)
        soft_probs = exponent / lax.optimization_barrier(jnp.sum(exponent, axis=-1, keepdims=True))
        return jnp.einsum('hqk,khd->qhd', low(soft_probs), value_rows, precision=lax.Precision.HIGHEST)
    indices = jnp.arange(seq_len // block_rows, dtype=jnp.int32)
    blocks = lax.map(jax.checkpoint(one_block), indices)
    return blocks.reshape(seq_len, -1)

def forward(inputs, states, qkv_master, out_master, query_master, pair_master, back_master, up_master, down_master, gains, biases, segment, enc_length):
    seq_len = inputs.shape[0]
    enc_count = states.shape[0]
    positions = jnp.arange(seq_len, dtype=jnp.int32)
    enc_positions = jnp.arange(enc_count, dtype=jnp.int32)

    def self_allowed(row_start, block_rows):
        row_ids = row_start + jnp.arange(block_rows, dtype=jnp.int32)
        row_segments = lax.dynamic_slice_in_dim(segment, row_start, block_rows, 0)
        return (row_segments[:, None] == segment[None, :]) & (row_ids[:, None] >= positions[None, :])

    def cross_allowed(row_start, block_rows):
        return jnp.broadcast_to(enc_positions[None, :] < enc_length, (block_rows, enc_count))
    self_weights = low(qkv_master)
    normed_one = low(norm_rows(inputs, gains[0], biases[0]))
    queries = low_back(low(product(normed_one, self_weights[0]))).reshape(seq_len, HEADS, HD)
    key_rows = low_back(low(product(normed_one, self_weights[1]))).reshape(seq_len, HEADS, HD)
    value_rows = low_back(low(product(normed_one, self_weights[2]))).reshape(seq_len, HEADS, HD)
    context_one = low_back(low(attention(queries, key_rows, value_rows, self_allowed)))
    hidden_one = inputs + low_back(product(context_one, low(out_master)))
    normed_two = low(norm_rows(hidden_one, gains[1], biases[1]))
    cross_weights = low(pair_master)
    queries_two = low_back(low(product(normed_two, low(query_master)))).reshape(seq_len, HEADS, HD)
    keys_two = low_back(low(product(states, cross_weights[0]))).reshape(enc_count, HEADS, HD)
    values_two = low_back(low(product(states, cross_weights[1]))).reshape(enc_count, HEADS, HD)
    context_two = low_back(low(attention(queries_two, keys_two, values_two, cross_allowed)))
    hidden_two = hidden_one + low_back(product(context_two, low(back_master)))
    normed_three = low(norm_rows(hidden_two, gains[2], biases[2]))
    inner_pre = low_back(product(normed_three, low(up_master)))
    active = low(jax.nn.silu(inner_pre))
    return hidden_two + low_back(product(active, low(down_master)))

def reference(tokens, encoder, seg_ids, enc_lens, attn_qkv, attn_out, cross_q, cross_kv, cross_out, ffn_in, ffn_out, norm_gains, norm_biases, out_grad):
    seqs = seg_ids.shape[0]
    seq_len = seg_ids.shape[1]
    width = tokens.shape[1]
    params = tuple((weight.astype(jnp.float32) for weight in (attn_qkv, attn_out, cross_q, cross_kv, cross_out, ffn_in, ffn_out, norm_gains, norm_biases)))

    def one_sequence(totals, item):
        row_block, states, segment, enc_length, cotangent = item

        def apply(inputs, enc_states, *weights):
            return forward(inputs, enc_states, *weights, segment, enc_length)
        result, pull = jax.vjp(apply, row_block.astype(jnp.float32), states.astype(jnp.float32), *params)
        grads = pull(cotangent.astype(jnp.float32))
        totals = tuple((first_term + second_term for first_term, second_term in zip(totals, grads[2:])))
        return (totals, (result.astype(jnp.bfloat16), grads[0], grads[1]))
    zeros = tuple((jnp.zeros_like(weight) for weight in params))
    items = (tokens.reshape(seqs, seq_len, width), encoder, seg_ids, enc_lens, out_grad.reshape(seqs, seq_len, width))
    totals, (results, in_grads, enc_grads) = lax.scan(one_sequence, zeros, items)
    return (results.reshape(-1, width), in_grads.reshape(-1, width), enc_grads, totals[0], totals[1], totals[2], totals[3], totals[4], totals[5], totals[6], totals[7], totals[8])
```

```python
import functools

import jax
import jax.numpy as jnp
from jax import lax
from jax.experimental import pallas as pl
from jax.experimental.pallas import tpu as pltpu
from jax.sharding import Mesh
from jax.sharding import PartitionSpec as P

HD = 64
LANES = 128
PAIR = 2 * HD
RING = 4
epsilon = 1e-05
masked_score = -1e30
MESH = pl.DeviceIdType.MESH
low_type = jnp.bfloat16
f32 = jnp.float32
MIB = 1 << 20


def matmul(left, right):
    return jnp.dot(left, right, preferred_element_type=f32)


def inner_rows(left, right):
    return lax.dot_general(left, right, (((0,), (0,)), ((), ())), preferred_element_type=f32)


def outer_cols(left, right):
    return lax.dot_general(left, right, (((1,), (1,)), ((), ())), preferred_element_type=f32)


def norm_forward(values_in, gain_row, bias_row):
    average = jnp.mean(values_in, axis=-1, keepdims=True)
    centred = values_in - average
    inverse = lax.rsqrt(jnp.mean(centred * centred, axis=-1, keepdims=True) + epsilon)
    unit_rows = centred * inverse
    return (unit_rows * gain_row + bias_row, unit_rows, inverse)


def norm_backward(incoming, unit_rows, inverse, gain_row):
    scaled = incoming * gain_row
    first_mean = jnp.mean(scaled, axis=-1, keepdims=True)
    second_mean = jnp.mean(scaled * unit_rows, axis=-1, keepdims=True)
    result = inverse * (scaled - first_mean - unit_rows * second_mean)
    return (result, jnp.sum(incoming * unit_rows, axis=0), jnp.sum(incoming, axis=0))


class Place:
    def __init__(self):
        self.z = lax.axis_index("z")
        self.y = lax.axis_index("y")
        self.x = lax.axis_index("x")
        self.c = lax.axis_index("c")

    def to(self, which):
        if which == "x":
            return {"x": 1 - self.x}
        if which == "y":
            return {"y": 1 - self.y}
        if which == "c":
            return {"c": 1 - self.c}
        if which == "z1":
            return {"z": self.z + 1 - 2 * lax.rem(self.z, 2)}
        if which == "z2":
            return {"z": lax.rem(self.z + 2, RING)}
        if which == "down":
            return {"z": lax.rem(self.z + RING - 1, RING)}
        return {"z": lax.rem(self.z + 1, RING)}

    def ring(self, step):
        return lax.rem(self.z + step, RING)


def greet(place, names):
    barrier = pltpu.get_barrier_semaphore()
    for name in names:
        pl.semaphore_signal(barrier, inc=1, device_id=place.to(name), device_id_type=MESH)
    pl.semaphore_wait(barrier, len(names))


class Copies:
    def __init__(self, send_sems, recv_sems):
        self.send_sems, self.recv_sems = send_sems, recv_sems
        self.made = []

    def start(self, place, src, dst, which):
        at = len(self.made)
        copy = pltpu.make_async_remote_copy(
            src_ref=src,
            dst_ref=dst,
            send_sem=self.send_sems.at[at],
            recv_sem=self.recv_sems.at[at],
            device_id=place.to(which),
            device_id_type=MESH,
        )
        copy.start()
        self.made.append(copy)
        return copy

    def finish(self):
        for copy in self.made:
            copy.wait_send()


GATHER_ORDERS = ("xzy", "yzx", "zyx", "zxy")


def gather_unit(order, place, own, whole, base, rows, cols, copies):
    x, y = place.x, place.y

    def at(step, both_y, both_x):
        first = place.ring(step) * 2
        row = first * rows if both_y else (first + y) * rows
        col = base if both_x else base + x * cols
        return whole.at[
            pl.ds(pl.multiple_of(row, rows), rows * (2 if both_y else 1)),
            pl.ds(pl.multiple_of(col, LANES), cols * (2 if both_x else 1)),
        ]

    def send(where, which):
        return copies.start(place, where, where, which)

    arrived = {}
    mine = at(0, False, False)
    if order in ("xzy", "yzx"):
        axis, last = order[0], order[2]
        wide = dict(both_y=axis == "y", both_x=axis == "x")
        first = copies.start(place, own, mine, axis)
        yield
        first.wait_recv()
        hop = send(at(0, **wide), "down")
        ends = [send(at(0, **wide), last)]
        yield
        for step in range(1, RING):
            hop.wait_recv()
            if step < RING - 1:
                hop = send(at(step, **wide), "down")
            ends.append(send(at(step, **wide), last))
            yield
        for copy in ends:
            copy.wait_recv()
    else:
        mid, last = order[1], order[2]
        wide = dict(both_y=mid == "y", both_x=mid == "x")
        hop = copies.start(place, own, mine, "down")
        mids = [copies.start(place, own, mine, mid)]
        ends = []
        yield
        for step in range(1, RING + 1):
            if step < RING:
                hop.wait_recv()
                if step < RING - 1:
                    hop = send(at(step, False, False), "down")
                mids.append(send(at(step, False, False), mid))
            mids[step - 1].wait_recv()
            ends.append(send(at(step - 1, **wide), last))
            yield
        for copy in ends:
            copy.wait_recv()
    del arrived


def run_staggered(makers, spacing):
    waiting = list(makers)
    running = []
    level = 0
    while waiting or running:
        if waiting and level % spacing == 0:
            running.extend(waiting.pop(0))
        still = []
        for unit in running:
            try:
                next(unit)
                still.append(unit)
            except StopIteration:
                pass
        running = still
        level += 1


N_ROWS_COPIES = 8


def gather_kernel(sizes, *refs):
    rows, cols, units_of = sizes
    n_weights = len(units_of)
    h_own, g_own, enc_own = refs[:3]
    own = refs[3 : 3 + n_weights]
    outs = refs[3 + n_weights :]
    h_all, g_all, enc_all = outs[:3]
    whole = outs[3 : 3 + n_weights]
    send_sems, recv_sems, local_sems = outs[3 + n_weights :]
    place = Place()
    greet(place, ("x", "y", "c", "down", "up"))
    copies = Copies(send_sems, recv_sems)
    x, c = place.x, place.c
    n = h_own.shape[0]
    e = enc_own.shape[0]

    def h_at(xx, cc):
        return h_all.at[pl.ds(pl.multiple_of((xx * 2 + cc) * n, 16), n)]

    def e_at(xx, cc):
        return enc_all.at[pl.ds(pl.multiple_of((xx * 2 + cc) * e, 16), e)]

    g_at = g_all.at[pl.ds(pl.multiple_of(c * n, 16), n)]
    hx = copies.start(place, h_own, h_at(x, c), "x")
    hc = copies.start(place, h_own, h_at(x, c), "c")
    local = []

    def keep(src, dst):
        copy = pltpu.make_async_copy(src, dst, local_sems.at[len(local)])
        copy.start()
        local.append(copy)

    keep(h_own, h_at(x, c))
    keep(g_own, g_at)
    keep(enc_own, e_at(x, c))
    groups, group = [], []
    mine = []
    for which, count in enumerate(units_of):
        for unit in range(count):
            base = unit * 2 * cols
            src = own[which].at[unit]
            dst = whole[which].at[
                pl.ds(pl.multiple_of((place.z * 2 + place.y) * rows, rows), rows),
                pl.ds(pl.multiple_of(base + x * cols, LANES), cols),
            ]
            mine.append((src, dst))
            order = GATHER_ORDERS[len(group)]
            group.append(gather_unit(order, place, src, whole[which], base, rows, cols, copies))
            if len(group) == len(GATHER_ORDERS):
                groups.append(group)
                group = []
    for src, dst in mine:
        keep(src, dst)
    for copy in local:
        copy.wait()
    gc = copies.start(place, g_own, g_at, "c")
    ex = copies.start(place, enc_own, e_at(x, c), "x")
    ec = copies.start(place, enc_own, e_at(x, c), "c")

    def rows_unit():
        yield
        yield
        hx.wait_recv()
        hxc = copies.start(place, h_at(1 - x, c), h_at(1 - x, c), "c")
        ex.wait_recv()
        exc = copies.start(place, e_at(1 - x, c), e_at(1 - x, c), "c")
        yield
        for copy in (hc, gc, ec, hxc, exc):
            copy.wait_recv()

    groups[0].append(rows_unit())
    run_staggered(groups, 3)
    copies.finish()


def gather_weights(h_own, g_own, enc_own, shards):
    units_of = tuple(s.shape[0] for s in shards)
    rows, cols = shards[0].shape[1:]
    depth = rows * RING * 2
    n, e, width = h_own.shape[0], enc_own.shape[0], h_own.shape[1]
    n_units = sum(units_of)
    n_copies = N_ROWS_COPIES + n_units * 11
    any_spec = pl.BlockSpec(memory_space=pl.ANY)
    out_shape = [
        jax.ShapeDtypeStruct((4 * n, width), low_type),
        jax.ShapeDtypeStruct((2 * n, width), low_type),
        jax.ShapeDtypeStruct((4 * e, width), low_type),
    ] + [jax.ShapeDtypeStruct((depth, 2 * cols * k), low_type) for k in units_of]
    return pl.pallas_call(
        functools.partial(gather_kernel, (rows, cols, units_of)),
        out_shape=out_shape,
        in_specs=[any_spec] * (3 + len(shards)),
        out_specs=[any_spec] * len(out_shape),
        scratch_shapes=[
            pltpu.SemaphoreType.DMA((n_copies,)),
            pltpu.SemaphoreType.DMA((n_copies,)),
            pltpu.SemaphoreType.DMA((3 + n_units,)),
        ],
        compiler_params=pltpu.CompilerParams(collective_id=0, has_side_effects=True),
        name="gather_weights",
    )(h_own, g_own, enc_own, *shards)


REDUCE_ORDERS = ("xyz", "xzy", "yxz", "yzx")
CHUNK_ORDER = tuple(range(1, RING)) + (0,)


def reduce_unit(order, place, part, base, rows, cols, recv, out, copies):
    x, y = place.x, place.y

    def at(step, row_of, col_of):
        first = place.ring(step) * 2
        row = first * rows if row_of is None else (first + row_of) * rows
        col = base if col_of is None else base + col_of * cols
        return part.at[
            pl.ds(pl.multiple_of(row, rows), rows * (2 if row_of is None else 1)),
            pl.ds(pl.multiple_of(col, LANES), cols * (2 if col_of is None else 1)),
        ]

    used = [0]

    def landing(shape):
        height = shape[0] * (shape[1] // cols)
        where = [
            recv.at[pl.ds(used[0] + k * shape[0], shape[0])] for k in range(shape[1] // cols)
        ]
        used[0] += height
        return where

    def pieces(where, shape):
        return where

    def add(target, source):
        target[...] = (target[...].astype(f32) + source[...].astype(f32)).astype(low_type)

    def exchange(step, which, mid):
        sent = []
        if which == "x":
            if mid:
                spots = [(at(step, y, 1 - x), at(step, y, x))]
            else:
                spots = [(at(step, None, 1 - x), at(step, None, x))]
        else:
            if mid:
                spots = [(at(step, 1 - y, x), at(step, y, x))]
            else:
                spots = [(at(step, 1 - y, k), at(step, y, k)) for k in range(2)]
        for src, keep_at in spots:
            (land,) = landing((src.shape[0], cols))
            sent.append((copies.start(place, src, land, which), keep_at, land))
        return sent

    def take(sent):
        for copy, keep_at, land in sent:
            copy.wait_recv()
            add(keep_at, land)

    first, middle, last = order
    outer = {s: exchange(s, first, False) for s in CHUNK_ORDER}
    yield
    if last == "z":
        inner = {}
        hop = None
        for k, step in enumerate(CHUNK_ORDER):
            take(outer[step])
            inner[step] = exchange(step, middle, True)
            yield
        for step in CHUNK_ORDER:
            take(inner[step])
            if hop is not None:
                copy, land = hop
                copy.wait_recv()
                if step == 0:
                    total = at(0, y, x)[...].astype(f32) + land[...].astype(f32)
                    out[...] = total
                else:
                    add(at(step, y, x), land)
            if step != 0:
                (land,) = landing((rows, cols))
                hop = (copies.start(place, at(step, y, x), land, "down"), land)
                yield
    else:
        hop = None
        for step in CHUNK_ORDER:
            take(outer[step])
            if first == "x":
                spots = [at(step, None, x)]
            else:
                spots = [at(step, y, k) for k in range(2)]
            if hop is not None:
                for (copy, land), spot in zip(hop, spots):
                    copy.wait_recv()
                    add(spot, land)
            if step != 0:
                hop = []
                for spot in spots:
                    (land,) = landing((spot.shape[0], cols))
                    hop.append((copies.start(place, spot, land, "down"), land))
                yield
        src = at(0, 1 - y, x) if last == "y" else at(0, y, 1 - x)
        (land,) = landing((rows, cols))
        copy = copies.start(place, src, land, last)
        yield
        copy.wait_recv()
        out[...] = at(0, y, x)[...].astype(f32) + land[...].astype(f32)


def reduce_kernel(sizes, *refs):
    rows, cols, units_of = sizes
    n_weights = len(units_of)
    small = refs[0]
    parts = refs[1 : 1 + n_weights]
    outs = refs[1 + n_weights :]
    small_out = outs[0]
    sums = outs[1 : 1 + n_weights]
    recv, small_recv, send_sems, recv_sems = outs[1 + n_weights :]
    place = Place()
    greet(place, ("x", "y", "c", "down", "up", "z2"))
    copies = Copies(send_sems, recv_sems)
    groups, group = [], []
    index = 0
    for which, count in enumerate(units_of):
        for unit in range(count):
            order = REDUCE_ORDERS[len(group)]
            group.append(
                reduce_unit(
                    order,
                    place,
                    parts[which],
                    unit * 2 * cols,
                    rows,
                    cols,
                    recv.at[index],
                    sums[which].at[unit],
                    copies,
                )
            )
            index += 1
            if len(group) == len(REDUCE_ORDERS):
                groups.append(group)
                group = []

    def small_unit():
        small_out[0] = small[...]
        for at, which in enumerate(("c", "x", "y", "z1", "z2")):
            copy = copies.start(place, small_out.at[at], small_recv.at[at], which)
            yield
            copy.wait_recv()
            small_out[at + 1] = small_out[at] + small_recv[at]

    groups[0].append(small_unit())
    run_staggered(groups, 3)
    copies.finish()


def reduce_grads(small, parts, rows, cols):
    units_of = tuple(p.shape[1] // (2 * cols) for p in parts)
    n_units = sum(units_of)
    vmem = pl.BlockSpec(memory_space=pltpu.VMEM)
    out_shape = [jax.ShapeDtypeStruct((6,) + small.shape, f32)] + [
        jax.ShapeDtypeStruct((k, rows, cols), f32) for k in units_of
    ]
    n_copies = 5 + n_units * 15
    return pl.pallas_call(
        functools.partial(reduce_kernel, (rows, cols, units_of)),
        out_shape=out_shape,
        in_specs=[vmem] * (1 + len(parts)),
        out_specs=[vmem] * len(out_shape),
        scratch_shapes=[
            pltpu.VMEM((n_units, rows * 15, cols), low_type),
            pltpu.VMEM((5,) + small.shape, f32),
            pltpu.SemaphoreType.DMA((n_copies,)),
            pltpu.SemaphoreType.DMA((n_copies,)),
        ],
        input_output_aliases={},
        compiler_params=pltpu.CompilerParams(
            collective_id=1, has_side_effects=True, vmem_limit_bytes=52 * MIB
        ),
        name="reduce_grads",
    )(small, *parts)


BLOCK = 256


def split_heads(values_in):
    lane = lax.broadcasted_iota(jnp.int32, values_in.shape, 1)
    zero = jnp.zeros_like(values_in)
    return jnp.concatenate(
        [jnp.where(lane < HD, values_in, zero), jnp.where(lane >= HD, values_in, zero)], axis=0
    )


def window_start(place_ref, window, keys):
    if window == keys:
        return 0
    ends = (place_ref[0] + pl.program_id(1) + 1) * BLOCK
    return pl.multiple_of(jnp.maximum(ends - window, 0), BLOCK)


def key_scores(queries, keys, lows, highs, start):
    scores = outer_cols(keys, queries)
    ids = start + lax.broadcasted_iota(jnp.int32, scores.shape, 0)
    lows = jnp.concatenate([lows, lows], axis=1)
    highs = jnp.concatenate([highs, highs], axis=1)
    return jnp.where((ids >= lows) & (ids <= highs), scores, masked_score)


def attend_kernel(window, place_ref, q_ref, k_ref, v_ref, low_ref, high_ref, o_ref, lse_ref):
    start = window_start(place_ref, window, k_ref.shape[0])
    keys = k_ref[pl.ds(start, window)]
    values = v_ref[pl.ds(start, window)]
    queries = split_heads(q_ref[...] * jnp.asarray(HD**-0.5, low_type))
    scores = key_scores(queries, keys, low_ref[...], high_ref[...], start)
    peak = jnp.max(scores, axis=0, keepdims=True)
    probs = jnp.exp(scores - peak)
    total = jnp.sum(probs, axis=0, keepdims=True)
    lse_ref[0, 0] = peak + jnp.log(total)
    context = inner_rows(values, probs.astype(low_type)) / total
    rows = q_ref.shape[0]
    pair = jnp.concatenate([context[:HD, :rows], context[HD:, rows:]], axis=0)
    o_ref[...] = pair.T.astype(low_type)


def attention_specs(rows, keys):
    def block(i, j, p):
        return (j, i)

    def whole(i, j, p):
        return (0, i)

    def line(i, j, p):
        return (0, j)

    q_spec = pl.BlockSpec((BLOCK, PAIR), block)
    k_spec = pl.BlockSpec((keys, PAIR), whole)
    l_spec = pl.BlockSpec((1, BLOCK), line)
    lse_spec = pl.BlockSpec((1, 1, 1, 2 * BLOCK), lambda i, j, p: (i, j, 0, 0))
    return q_spec, k_spec, l_spec, lse_spec


def attend(place, queries, keys, values, lows, highs, window):
    rows, width = queries.shape
    count = keys.shape[0]
    pairs, blocks = width // PAIR, rows // BLOCK
    q_spec, k_spec, l_spec, lse_spec = attention_specs(rows, count)
    cost = pl.CostEstimate(
        flops=8 * rows * window * width,
        bytes_accessed=2 * width * (2 * rows + 2 * count),
        transcendentals=rows * window * width // HD,
    )
    return pl.pallas_call(
        functools.partial(attend_kernel, window),
        out_shape=[
            jax.ShapeDtypeStruct((rows, width), low_type),
            jax.ShapeDtypeStruct((pairs, blocks, 1, 2 * BLOCK), f32),
        ],
        grid_spec=pltpu.PrefetchScalarGridSpec(
            num_scalar_prefetch=1,
            grid=(pairs, blocks),
            in_specs=[q_spec, k_spec, k_spec, l_spec, l_spec],
            out_specs=[q_spec, lse_spec],
        ),
        compiler_params=pltpu.CompilerParams(vmem_limit_bytes=40 * MIB),
        cost_estimate=cost,
        name="attend",
    )(place, queries, keys, values, lows, highs)


def attend_back_kernel(
    window, place_ref, q_ref, k_ref, v_ref, low_ref, high_ref, o_ref, do_ref, lse_ref,
    dq_ref, dk_ref, dv_ref, dk_sum, dv_sum,
):
    scale = jnp.asarray(HD**-0.5, low_type)
    start = window_start(place_ref, window, k_ref.shape[0])
    here = pl.ds(start, window)
    rows = q_ref.shape[0]

    @pl.when(pl.program_id(1) == 0)
    def _():
        dk_sum[...] = jnp.zeros_like(dk_sum)
        dv_sum[...] = jnp.zeros_like(dv_sum)

    keys, values = k_ref[here], v_ref[here]
    queries = split_heads(q_ref[...] * scale)
    grads = split_heads(do_ref[...])
    scores = key_scores(queries, keys, low_ref[...], high_ref[...], start)
    probs = jnp.exp(scores - lse_ref[0, 0])
    grad_probs = outer_cols(values, grads)
    product = (do_ref[...].astype(f32) * o_ref[...].astype(f32)).T
    inner = jnp.concatenate(
        [
            jnp.sum(product[:HD], axis=0, keepdims=True),
            jnp.sum(product[HD:], axis=0, keepdims=True),
        ],
        axis=1,
    )
    grad_scores = (probs * (grad_probs - inner)).astype(low_type)
    dv_sum[here] += matmul(probs.astype(low_type), grads)
    dk_sum[here] += matmul(grad_scores, queries)
    grad_queries = inner_rows(keys, grad_scores) * HD**-0.5
    pair = jnp.concatenate([grad_queries[:HD, :rows], grad_queries[HD:, rows:]], axis=0)
    dq_ref[...] = pair.T.astype(low_type)

    @pl.when(pl.program_id(1) == pl.num_programs(1) - 1)
    def _():
        dk_ref[...] = dk_sum[...].astype(low_type)
        dv_ref[...] = dv_sum[...].astype(low_type)


def attend_back(place, queries, keys, values, lows, highs, context, grads, lse, window):
    rows, width = queries.shape
    count = keys.shape[0]
    pairs, blocks = width // PAIR, rows // BLOCK
    q_spec, k_spec, l_spec, lse_spec = attention_specs(rows, count)
    cost = pl.CostEstimate(
        flops=20 * rows * window * width,
        bytes_accessed=2 * width * (4 * rows + 4 * count),
        transcendentals=rows * window * width // HD,
    )
    return pl.pallas_call(
        functools.partial(attend_back_kernel, window),
        out_shape=[
            jax.ShapeDtypeStruct((rows, width), low_type),
            jax.ShapeDtypeStruct((count, width), low_type),
            jax.ShapeDtypeStruct((count, width), low_type),
        ],
        grid_spec=pltpu.PrefetchScalarGridSpec(
            num_scalar_prefetch=1,
            grid=(pairs, blocks),
            in_specs=[q_spec, k_spec, k_spec, l_spec, l_spec, q_spec, q_spec, lse_spec],
            out_specs=[q_spec, k_spec, k_spec],
            scratch_shapes=[pltpu.VMEM((count, PAIR), f32), pltpu.VMEM((count, PAIR), f32)],
        ),
        compiler_params=pltpu.CompilerParams(vmem_limit_bytes=48 * MIB),
        cost_estimate=cost,
        name="attend_back",
    )(place, queries, keys, values, lows, highs, context, grads, lse)


SWAP = ((0, 1), (1, 0))


def on_device(
    tokens,
    encoder,
    seg_ids,
    enc_lens,
    attn_qkv,
    attn_out,
    cross_q,
    cross_kv,
    cross_out,
    ffn_in,
    ffn_out,
    norm_gains,
    norm_biases,
    out_grad,
):
    outer = lax.axis_size("o")
    core, chip = lax.axis_index("c"), lax.axis_index("x")
    own = tokens.shape[0]
    half = 2 * own
    segment = seg_ids[0]
    seq_len = segment.shape[0]
    cols = cross_q.shape[1]
    width = tokens.shape[1]

    def units(block):
        k = block.shape[-1] // cols
        return block.reshape(block.shape[0], k, cols).transpose(1, 0, 2)

    shards = [
        attn_qkv.astype(low_type),
        attn_out.astype(low_type).T[None],
        cross_q.astype(low_type)[None],
        cross_kv.astype(low_type),
        cross_out.astype(low_type).T[None],
        units(ffn_in.astype(low_type)),
        units(ffn_out.astype(low_type).T),
    ]
    if outer > 1:
        shards = [lax.all_gather(s, "o", axis=1, tiled=True) for s in shards]
    rows = shards[0].shape[1]

    residual = tokens.astype(f32)
    normed, unit_one, inverse_one = norm_forward(residual, norm_gains[0], norm_biases[0])
    rows_one, grads_three, enc_full, *weights = gather_weights(
        normed.astype(low_type), out_grad, encoder[0], shards
    )

    def natural(weight):
        if outer == 1:
            return weight
        parts = weight.reshape(RING, 2, outer, rows // outer, -1)
        return parts.transpose(2, 0, 1, 3, 4).reshape(weight.shape)

    def gathered(weight):
        if outer == 1:
            return weight
        parts = weight.reshape(outer, RING, 2, rows // outer, -1)
        return parts.transpose(1, 2, 0, 3, 4).reshape(weight.shape)

    qkv_w, out_w, query_w, pair_w, back_w, up_w, down_w = map(natural, weights)
    heads_width = 2 * cols

    def half_of(values_in, which):
        return lax.dynamic_slice_in_dim(values_in, which * own, own, 0)

    def core_sum(partial):
        theirs = lax.ppermute(half_of(partial, 1 - core).astype(low_type), "c", SWAP)
        return half_of(partial, core) + theirs.astype(f32)

    def core_rows(mine):
        theirs = lax.ppermute(mine, "c", SWAP)
        return jnp.concatenate(
            [jnp.where(core == 0, mine, theirs), jnp.where(core == 0, theirs, mine)], axis=0
        )

    first = chip * half
    here = lax.dynamic_slice_in_dim(segment, first, half, 0)
    lows = jnp.sum((segment[None, :] < here[:, None]).astype(jnp.int32), axis=1)[None]
    highs = (first + jnp.arange(half, dtype=jnp.int32))[None]
    enc_lows = jnp.zeros_like(highs)
    enc_highs = jnp.broadcast_to(enc_lens[0] - 1, highs.shape)
    place = (chip * (half // BLOCK))[None].astype(jnp.int32)
    window = min(seq_len, seq_len // 2 + BLOCK)

    chip_rows = lax.dynamic_slice_in_dim(rows_one, first, half, 0)
    queries_one = matmul(chip_rows, qkv_w[:, :heads_width]).astype(low_type)
    pair_one = matmul(rows_one, qkv_w[:, heads_width:]).astype(low_type)
    keys_one, values_one = pair_one[:, :heads_width], pair_one[:, heads_width:]
    context_one, lse_one = attend(place, queries_one, keys_one, values_one, lows, highs, window)
    residual_one = residual + core_sum(outer_cols(context_one, out_w))

    normed, unit_two, inverse_two = norm_forward(residual_one, norm_gains[1], norm_biases[1])
    rows_two = core_rows(normed.astype(low_type))
    queries_two = matmul(rows_two, query_w).astype(low_type)
    pair_two = matmul(enc_full, pair_w).astype(low_type)
    keys_two, values_two = pair_two[:, :heads_width], pair_two[:, heads_width:]
    enc_count = enc_full.shape[0]
    context_two, lse_two = attend(
        place, queries_two, keys_two, values_two, enc_lows, enc_highs, enc_count
    )
    residual_two = residual_one + core_sum(outer_cols(context_two, back_w))

    normed, unit_three, inverse_three = norm_forward(residual_two, norm_gains[2], norm_biases[2])
    rows_three = core_rows(normed.astype(low_type))
    inner_pre = matmul(rows_three, up_w)
    sigmoid_pre = jax.nn.sigmoid(inner_pre)
    active = (inner_pre * sigmoid_pre).astype(low_type)
    out_tokens = (residual_two + core_sum(outer_cols(active, down_w))).astype(low_type)

    grad_active = matmul(grads_three, down_w)
    slope = sigmoid_pre * (1.0 + inner_pre * (1.0 - sigmoid_pre))
    grad_inner = (grad_active * slope).astype(low_type)
    down_grad = inner_rows(grads_three, active).astype(low_type)
    up_grad = inner_rows(rows_three, grad_inner).astype(low_type)
    grad_normed = core_sum(outer_cols(grad_inner, up_w))
    grad_residual, gain_three, bias_three = norm_backward(
        grad_normed, unit_three, inverse_three, norm_gains[2]
    )
    grad_total = out_grad.astype(f32) + grad_residual

    grads_two = core_rows(grad_total.astype(low_type))
    grad_context = matmul(grads_two, back_w).astype(low_type)
    back_grad = inner_rows(grads_two, context_two).astype(low_type)
    grad_queries, grad_keys, grad_values = attend_back(
        place, queries_two, keys_two, values_two, enc_lows, enc_highs,
        context_two, grad_context, lse_two, enc_count,
    )
    query_grad = inner_rows(rows_two, grad_queries).astype(low_type)
    grad_pair = jnp.concatenate([grad_keys, grad_values], axis=1)
    pair_grad = inner_rows(enc_full, grad_pair).astype(low_type)
    enc_grad = lax.psum_scatter(
        outer_cols(grad_pair, pair_w).astype(low_type), ("x", "c"), scatter_dimension=0, tiled=True
    ).astype(f32)[None]
    grad_normed = core_sum(outer_cols(grad_queries, query_w))
    grad_residual, gain_two, bias_two = norm_backward(
        grad_normed, unit_two, inverse_two, norm_gains[1]
    )
    grad_total = grad_total + grad_residual

    grads_one = core_rows(grad_total.astype(low_type))
    grad_context = matmul(grads_one, out_w).astype(low_type)
    out_w_grad = inner_rows(grads_one, context_one).astype(low_type)
    grad_queries, grad_keys, grad_values = attend_back(
        place, queries_one, keys_one, values_one, lows, highs,
        context_one, grad_context, lse_one, window,
    )
    grad_pair = jnp.concatenate([grad_keys, grad_values], axis=1)
    qkv_grad = jnp.concatenate(
        [
            inner_rows(chip_rows, grad_queries).astype(low_type),
            inner_rows(rows_one, grad_pair).astype(low_type),
        ],
        axis=1,
    )
    key_term = outer_cols(grad_pair, qkv_w[:, heads_width:])
    query_term = outer_cols(grad_queries, qkv_w[:, :heads_width])
    mine = lax.dynamic_slice_in_dim(key_term, first, half, 0) + query_term
    others = lax.dynamic_slice_in_dim(key_term, (1 - chip) * half, half, 0)
    to_chip = lax.ppermute(core_sum(others).astype(low_type), "x", SWAP)
    grad_normed = core_sum(mine) + to_chip.astype(f32)
    grad_residual, gain_one, bias_one = norm_backward(
        grad_normed, unit_one, inverse_one, norm_gains[0]
    )
    in_grad = grad_total + grad_residual

    small = jnp.stack([gain_one, gain_two, gain_three, bias_one, bias_two, bias_three])
    small = jnp.concatenate([small, jnp.zeros((2, width), f32)], axis=0)
    grads = [up_grad, down_grad, back_grad, query_grad, pair_grad, out_w_grad, qkv_grad]
    small, *sums = reduce_grads(small, [gathered(g) for g in grads], rows, cols)
    small = small[-1]
    if outer > 1:
        small = lax.psum(small, "o")
        sums = [lax.psum_scatter(s, "o", scatter_dimension=1, tiled=True) for s in sums]
    up_sum, down_sum, back_sum, query_sum, pair_sum, out_sum, qkv_sum = sums

    def joined(block):
        return block.transpose(1, 0, 2).reshape(block.shape[1], -1)

    return (
        out_tokens,
        in_grad,
        enc_grad,
        qkv_sum,
        out_sum[0].T,
        query_sum[0],
        pair_sum,
        back_sum[0].T,
        joined(up_sum),
        joined(down_sum).T,
        small[:3],
        small[3:6],
    )


def solution(mesh):
    count, tensor = mesh.devices.shape
    outer = count // (RING * 2)
    fine = Mesh(
        mesh.devices.reshape(outer, RING, 2, tensor // 2, 2), ("o", "z", "y", "x", "c")
    )
    dp, tp = ("o", "z", "y"), ("x", "c")
    in_specs = (
        P(dp + tp, None),
        P(dp, tp, None),
        P(dp, None),
        P(dp),
        P(None, dp, tp),
        P(tp, dp),
        P(dp, tp),
        P(None, dp, tp),
        P(tp, dp),
        P(dp, tp),
        P(tp, dp),
        P(),
        P(),
        P(dp + tp, None),
    )
    out_specs = (
        P(dp + tp, None),
        P(dp + tp, None),
        P(dp, tp, None),
        P(None, dp, tp),
        P(tp, dp),
        P(dp, tp),
        P(None, dp, tp),
        P(tp, dp),
        P(dp, tp),
        P(tp, dp),
        P(),
        P(),
    )
    return jax.shard_map(
        on_device, mesh=fine, in_specs=in_specs, out_specs=out_specs, check_vma=False
    )
```

```python
import functools

import jax
import jax.numpy as jnp
from jax import lax
from jax.experimental import pallas as pl
from jax.experimental.pallas import tpu as pltpu
from jax.sharding import Mesh
from jax.sharding import PartitionSpec as P

HD = 64
LANES = 128
PAIR = 2 * HD
RING = 4
epsilon = 1e-05
masked_score = -1e30
MESH = pl.DeviceIdType.MESH
low_type = jnp.bfloat16
f32 = jnp.float32
MIB = 1 << 20


def matmul(left, right):
    return jnp.dot(left, right, preferred_element_type=f32)


def inner_rows(left, right):
    return lax.dot_general(left, right, (((0,), (0,)), ((), ())), preferred_element_type=f32)


def outer_cols(left, right):
    return lax.dot_general(left, right, (((1,), (1,)), ((), ())), preferred_element_type=f32)


def norm_forward(values_in, gain_row, bias_row):
    average = jnp.mean(values_in, axis=-1, keepdims=True)
    centred = values_in - average
    inverse = lax.rsqrt(jnp.mean(centred * centred, axis=-1, keepdims=True) + epsilon)
    unit_rows = centred * inverse
    return (unit_rows * gain_row + bias_row, unit_rows, inverse)


def norm_backward(incoming, unit_rows, inverse, gain_row):
    scaled = incoming * gain_row
    first_mean = jnp.mean(scaled, axis=-1, keepdims=True)
    second_mean = jnp.mean(scaled * unit_rows, axis=-1, keepdims=True)
    result = inverse * (scaled - first_mean - unit_rows * second_mean)
    return (result, jnp.sum(incoming * unit_rows, axis=0), jnp.sum(incoming, axis=0))


class Place:
    def __init__(self):
        self.z = lax.axis_index("z")
        self.y = lax.axis_index("y")
        self.x = lax.axis_index("x")
        self.c = lax.axis_index("c")

    def to(self, which):
        if which == "x":
            return {"x": 1 - self.x}
        if which == "y":
            return {"y": 1 - self.y}
        if which == "c":
            return {"c": 1 - self.c}
        if which == "z1":
            return {"z": self.z + 1 - 2 * lax.rem(self.z, 2)}
        if which == "z2":
            return {"z": lax.rem(self.z + 2, RING)}
        if which == "down":
            return {"z": lax.rem(self.z + RING - 1, RING)}
        return {"z": lax.rem(self.z + 1, RING)}

    def ring(self, step):
        return lax.rem(self.z + step, RING)


def greet(place, names):
    barrier = pltpu.get_barrier_semaphore()
    for name in names:
        pl.semaphore_signal(barrier, inc=1, device_id=place.to(name), device_id_type=MESH)
    pl.semaphore_wait(barrier, len(names))


class Copies:
    def __init__(self, send_sems, recv_sems):
        self.send_sems, self.recv_sems = send_sems, recv_sems
        self.made = []

    def start(self, place, src, dst, which):
        at = len(self.made)
        copy = pltpu.make_async_remote_copy(
            src_ref=src,
            dst_ref=dst,
            send_sem=self.send_sems.at[at],
            recv_sem=self.recv_sems.at[at],
            device_id=place.to(which),
            device_id_type=MESH,
        )
        copy.start()
        self.made.append(copy)
        return copy

    def finish(self):
        for copy in self.made:
            copy.wait_send()


GATHER_ORDERS = ("xzy", "yzx", "zyx", "zxy")


def gather_unit(order, place, own, whole, base, rows, cols, copies):
    x, y = place.x, place.y

    def at(step, both_y, both_x):
        first = place.ring(step) * 2
        row = first * rows if both_y else (first + y) * rows
        col = base if both_x else base + x * cols
        return whole.at[
            pl.ds(pl.multiple_of(row, rows), rows * (2 if both_y else 1)),
            pl.ds(pl.multiple_of(col, LANES), cols * (2 if both_x else 1)),
        ]

    def send(where, which):
        return copies.start(place, where, where, which)

    arrived = {}
    mine = at(0, False, False)
    if order in ("xzy", "yzx"):
        axis, last = order[0], order[2]
        wide = dict(both_y=axis == "y", both_x=axis == "x")
        first = copies.start(place, own, mine, axis)
        yield
        first.wait_recv()
        hop = send(at(0, **wide), "down")
        ends = [send(at(0, **wide), last)]
        yield
        for step in range(1, RING):
            hop.wait_recv()
            if step < RING - 1:
                hop = send(at(step, **wide), "down")
            ends.append(send(at(step, **wide), last))
            yield
        for copy in ends:
            copy.wait_recv()
    else:
        mid, last = order[1], order[2]
        wide = dict(both_y=mid == "y", both_x=mid == "x")
        hop = copies.start(place, own, mine, "down")
        mids = [copies.start(place, own, mine, mid)]
        ends = []
        yield
        for step in range(1, RING + 1):
            if step < RING:
                hop.wait_recv()
                if step < RING - 1:
                    hop = send(at(step, False, False), "down")
                mids.append(send(at(step, False, False), mid))
            mids[step - 1].wait_recv()
            ends.append(send(at(step - 1, **wide), last))
            yield
        for copy in ends:
            copy.wait_recv()
    del arrived


class Levels:
    def __init__(self, groups, spacing=3):
        self.groups = [list(g) for g in groups]
        self.live = [list(g) for g in groups]
        self.spacing = spacing
        self.level = 0
        self.started = 0

    def step(self):
        if self.started < len(self.groups) and self.level % self.spacing == 0:
            self.started += 1
        for group in self.live[: self.started]:
            for unit in list(group):
                try:
                    next(unit)
                except StopIteration:
                    group.remove(unit)
        self.level += 1

    def until(self, group):
        while self.live[group]:
            self.step()

    def drain(self):
        for group in range(len(self.groups)):
            self.until(group)


class Locals:
    def __init__(self, sems):
        self.sems, self.made = sems, []

    def start(self, src, dst):
        copy = pltpu.make_async_copy(src, dst, self.sems.at[len(self.made)])
        copy.start()
        self.made.append(copy)
        return copy

    def finish(self):
        for copy in self.made:
            copy.wait()


def gather_groups(place, sizes, own, whole, copies, local, orders):
    rows, cols, units_of = sizes
    groups, group = [], []
    index = 0
    for which, count in enumerate(units_of):
        for unit in range(count):
            base = unit * 2 * cols
            src = own[which].at[unit]
            local.start(
                src,
                whole[which].at[
                    pl.ds(pl.multiple_of((place.z * 2 + place.y) * rows, rows), rows),
                    pl.ds(pl.multiple_of(base + place.x * cols, LANES), cols),
                ],
            )
            group.append(
                gather_unit(
                    orders[index], place, src, whole[which], base, rows, cols, copies
                )
            )
            index += 1
            if len(group) == 4:
                groups.append(group)
                group = []
    return groups


def first_kernel(sizes, orders, *refs):
    n_weights = len(sizes[2])
    h_own, *own = refs[: 1 + n_weights]
    h_all, *whole = refs[1 + n_weights : 2 + 2 * n_weights]
    send_sems, recv_sems, local_sems = refs[2 + 2 * n_weights :]
    place = Place()
    greet(place, ("x", "y", "c", "down", "up"))
    copies = Copies(send_sems, recv_sems)
    local = Locals(local_sems)
    x, c = place.x, place.c
    n = h_own.shape[0]

    def h_at(xx, cc):
        return h_all.at[pl.ds(pl.multiple_of((xx * 2 + cc) * n, 16), n)]

    hx = copies.start(place, h_own, h_at(x, c), "x")
    hc = copies.start(place, h_own, h_at(x, c), "c")
    local.start(h_own, h_at(x, c))
    groups = gather_groups(place, sizes, own, whole, copies, local, orders)
    local.finish()

    def rows_unit():
        yield
        yield
        hx.wait_recv()
        hxc = copies.start(place, h_at(1 - x, c), h_at(1 - x, c), "c")
        yield
        yield
        hc.wait_recv()
        hxc.wait_recv()

    groups[0].append(rows_unit())
    Levels(groups).drain()
    copies.finish()


ANY_SPEC = pl.BlockSpec(memory_space=pl.ANY)
VMEM_SPEC = pl.BlockSpec(memory_space=pltpu.VMEM)


def gather_shapes(shards):
    units_of = tuple(s.shape[0] for s in shards)
    rows, cols = shards[0].shape[1:]
    depth = rows * RING * 2
    shapes = [jax.ShapeDtypeStruct((depth, 2 * cols * k), low_type) for k in units_of]
    return (rows, cols, units_of), shapes


def gather_first(h_own, shards):
    sizes, shapes = gather_shapes(shards)
    n, width = h_own.shape
    n_units = sum(sizes[2])
    n_copies = 3 + n_units * 11
    out_shape = [jax.ShapeDtypeStruct((4 * n, width), low_type)] + shapes
    return pl.pallas_call(
        functools.partial(first_kernel, sizes, ("xzy", "zxy", "yzx", "xzy")),
        out_shape=out_shape,
        in_specs=[ANY_SPEC] * (1 + len(shards)),
        out_specs=[VMEM_SPEC] * len(out_shape),
        scratch_shapes=[
            pltpu.SemaphoreType.DMA((n_copies,)),
            pltpu.SemaphoreType.DMA((n_copies,)),
            pltpu.SemaphoreType.DMA((1 + n_units,)),
        ],
        compiler_params=pltpu.CompilerParams(
            collective_id=0, has_side_effects=True, vmem_limit_bytes=30 * MIB
        ),
        name="gather_first",
    )(h_own, *shards)


def norm_rows(values_in, gain_row, bias_row):
    return norm_forward(values_in, gain_row, bias_row)[0]


def loop_rows(count, tile, body):
    @pl.loop(0, count // tile)
    def _(i):
        body(pl.ds(pl.multiple_of(i * tile, tile), tile))


def forward_kernel(sizes, window, *refs):
    n_weights = len(sizes[2])
    (
        q_one, pair_one, out_w, lows, highs, enc_highs, gains, biases, residual, g_own, enc_own,
        *own,
    ) = refs[: 11 + n_weights]
    outs = refs[11 + n_weights : 24 + 2 * n_weights]
    whole = outs[:n_weights]
    (
        g_all, enc_all, context_one, lse_one, residual_one, rows_two, q_two, pair_two, context_two,
        lse_two, residual_two, rows_three, inner_pre,
    ) = outs[n_weights:]
    sent, landed, send_sems, recv_sems, local_sems = refs[24 + 2 * n_weights :]
    query_w, pair_w, back_w, up_w, _ = whole
    place = Place()
    greet(place, ("x", "y", "c", "down", "up"))
    copies = Copies(send_sems, recv_sems)
    local = Locals(local_sems)
    x, c = place.x, place.c
    n, e = residual.shape[0], enc_own.shape[0]
    heads_width = q_one.shape[1]
    mine = pl.ds(pl.multiple_of(c * n, 16), n)
    others = pl.ds(pl.multiple_of((1 - c) * n, 16), n)

    def e_at(xx, cc):
        return enc_all.at[pl.ds(pl.multiple_of((xx * 2 + cc) * e, 16), e)]

    ex = copies.start(place, enc_own, e_at(x, c), "x")
    ec = copies.start(place, enc_own, e_at(x, c), "c")
    gc = copies.start(place, g_own, g_all.at[mine], "c")
    local.start(g_own, g_all.at[mine])
    local.start(enc_own, e_at(x, c))
    orders = ("xzy", "yzx", "xzy", "zxy") + GATHER_ORDERS * 2
    groups = gather_groups(place, sizes, own, whole, copies, local, orders)
    local.finish()

    def enc_unit():
        yield
        yield
        ex.wait_recv()
        exc = copies.start(place, e_at(1 - x, c), e_at(1 - x, c), "c")
        yield
        yield
        ec.wait_recv()
        gc.wait_recv()
        exc.wait_recv()

    groups[0].append(enc_unit())
    comm = Levels(groups)

    def attention(q_ref, pair_ref, low_of, high_of, o_ref, lse_ref, span):
        keys_count = pair_ref.shape[0]
        for pair in range(heads_width // PAIR):
            comm.step()
            lanes = pl.ds(pair * PAIR, PAIR)
            value_lanes = pl.ds(heads_width + pair * PAIR, PAIR)

            @pl.loop(0, q_ref.shape[0] // BLOCK)
            def _(block):
                rows = pl.ds(pl.multiple_of(block * BLOCK, BLOCK), BLOCK)
                if span == keys_count:
                    start = 0
                else:
                    ends = (x * (q_ref.shape[0] // BLOCK) + block + 1) * BLOCK
                    start = pl.multiple_of(jnp.maximum(ends - span, 0), BLOCK)
                here = pl.ds(start, span)
                o_ref[rows, lanes], lse_ref[pair, block] = attend_step(
                    q_ref[rows, lanes],
                    pair_ref[here, lanes],
                    pair_ref[here, value_lanes],
                    low_of(rows),
                    high_of(rows),
                    start,
                )

    def branch(at, context, weight, before, after, gain_at, rows_ref):
        @pl.loop(0, n // LANES)
        def _(i):
            tile = pl.ds(pl.multiple_of(i * LANES, LANES), LANES)
            theirs = pl.ds(pl.multiple_of((1 - c) * n + i * LANES, LANES), LANES)
            sent[at, tile] = outer_cols(context[theirs], weight[...]).astype(low_type)

        over = copies.start(place, sent.at[at], landed.at[at], "c")

        @pl.loop(0, n // LANES)
        def _(i):
            tile = pl.ds(pl.multiple_of(i * LANES, LANES), LANES)
            own_rows = pl.ds(pl.multiple_of(c * n + i * LANES, LANES), LANES)
            after[tile] = before[tile] + outer_cols(context[own_rows], weight[...])

        over.wait_recv()

        @pl.loop(0, n // LANES)
        def _(i):
            tile = pl.ds(pl.multiple_of(i * LANES, LANES), LANES)
            own_rows = pl.ds(pl.multiple_of(c * n + i * LANES, LANES), LANES)
            total = after[tile] + landed[at, tile].astype(f32)
            after[tile] = total
            rows_ref[own_rows] = norm_rows(
                total, gains[gain_at : gain_at + 1], biases[gain_at : gain_at + 1]
            ).astype(low_type)

        return copies.start(place, rows_ref.at[mine], rows_ref.at[mine], "c")

    attention(q_one, pair_one, lambda r: lows[:, r], lambda r: highs[:, r], context_one, lse_one, window)
    comm.step()
    over = branch(0, context_one, out_w, residual, residual_one, 1, rows_two)
    comm.until(0)
    loop_rows(enc_all.shape[0], BLOCK, lambda r: store(pair_two, r, matmul(enc_all[r], pair_w[...])))
    over.wait_recv()
    comm.step()
    loop_rows(2 * n, BLOCK, lambda r: store(q_two, r, matmul(rows_two[r], query_w[...])))
    attention(
        q_two, pair_two, lambda r: jnp.zeros((1, BLOCK), jnp.int32), lambda r: enc_highs[:, r],
        context_two, lse_two, enc_all.shape[0],
    )
    comm.step()
    over = branch(1, context_two, back_w, residual_one, residual_two, 2, rows_three)
    comm.until(1)
    over.wait_recv()
    loop_rows(2 * n, LANES, lambda r: store(inner_pre, r, matmul(rows_three[r], up_w[...])))
    comm.drain()
    copies.finish()


def store(ref, rows, values_in):
    ref[rows] = values_in.astype(ref.dtype)


def forward(q_one, pair_one, out_w, lows, highs, enc_highs, gains, biases, residual, g_own, enc_own, shards, window):
    sizes, shapes = gather_shapes(shards)
    n, width = residual.shape
    e = enc_own.shape[0]
    hidden = shapes[-1].shape[1]
    heads_width = q_one.shape[1]
    n_units = sum(sizes[2])
    n_copies = 8 + n_units * 11
    lse = jax.ShapeDtypeStruct((heads_width // PAIR, 2 * n // BLOCK, 1, 2 * BLOCK), f32)

    def low(*shape):
        return jax.ShapeDtypeStruct(shape, low_type)

    keep = jax.ShapeDtypeStruct((n, width), f32)
    out_shape = shapes + [
        low(2 * n, width), low(4 * e, width), low(2 * n, heads_width), lse, keep, low(2 * n, width),
        low(2 * n, heads_width), low(4 * e, 2 * heads_width), low(2 * n, heads_width), lse, keep,
        low(2 * n, width), jax.ShapeDtypeStruct((2 * n, hidden), f32),
    ]
    return pl.pallas_call(
        functools.partial(forward_kernel, sizes, window),
        out_shape=out_shape,
        in_specs=[VMEM_SPEC] * 9 + [ANY_SPEC] * (2 + len(shards)),
        out_specs=[VMEM_SPEC] * len(out_shape),
        scratch_shapes=[
            pltpu.VMEM((2, n, width), low_type),
            pltpu.VMEM((2, n, width), low_type),
            pltpu.SemaphoreType.DMA((n_copies,)),
            pltpu.SemaphoreType.DMA((n_copies,)),
            pltpu.SemaphoreType.DMA((2 + n_units,)),
        ],
        compiler_params=pltpu.CompilerParams(
            collective_id=2, has_side_effects=True, vmem_limit_bytes=60 * MIB
        ),
        name="forward",
    )(q_one, pair_one, out_w, lows, highs, enc_highs, gains, biases, residual, g_own, enc_own, *shards)


REDUCE_ORDERS = ("xyz", "xzy", "yxz", "yzx")
CHUNK_ORDER = tuple(range(1, RING)) + (0,)


def reduce_unit(order, place, part, base, rows, cols, recv, out, copies):
    x, y = place.x, place.y

    def at(step, row_of, col_of):
        first = place.ring(step) * 2
        row = first * rows if row_of is None else (first + row_of) * rows
        col = base if col_of is None else base + col_of * cols
        return part.at[
            pl.ds(pl.multiple_of(row, rows), rows * (2 if row_of is None else 1)),
            pl.ds(pl.multiple_of(col, LANES), cols * (2 if col_of is None else 1)),
        ]

    used = [0]

    def landing(shape):
        height = shape[0] * (shape[1] // cols)
        where = [
            recv.at[pl.ds(used[0] + k * shape[0], shape[0])] for k in range(shape[1] // cols)
        ]
        used[0] += height
        return where

    def pieces(where, shape):
        return where

    def add(target, source):
        target[...] = (target[...].astype(f32) + source[...].astype(f32)).astype(low_type)

    def exchange(step, which, mid):
        sent = []
        if which == "x":
            if mid:
                spots = [(at(step, y, 1 - x), at(step, y, x))]
            else:
                spots = [(at(step, None, 1 - x), at(step, None, x))]
        else:
            if mid:
                spots = [(at(step, 1 - y, x), at(step, y, x))]
            else:
                spots = [(at(step, 1 - y, k), at(step, y, k)) for k in range(2)]
        for src, keep_at in spots:
            (land,) = landing((src.shape[0], cols))
            sent.append((copies.start(place, src, land, which), keep_at, land))
        return sent

    def take(sent):
        for copy, keep_at, land in sent:
            copy.wait_recv()
            add(keep_at, land)

    first, middle, last = order
    outer = {s: exchange(s, first, False) for s in CHUNK_ORDER}
    yield
    if last == "z":
        inner = {}
        hop = None
        for k, step in enumerate(CHUNK_ORDER):
            take(outer[step])
            inner[step] = exchange(step, middle, True)
            yield
        for step in CHUNK_ORDER:
            take(inner[step])
            if hop is not None:
                copy, land = hop
                copy.wait_recv()
                if step == 0:
                    total = at(0, y, x)[...].astype(f32) + land[...].astype(f32)
                    out[...] = total
                else:
                    add(at(step, y, x), land)
            if step != 0:
                (land,) = landing((rows, cols))
                hop = (copies.start(place, at(step, y, x), land, "down"), land)
                yield
    else:
        hop = None
        for step in CHUNK_ORDER:
            take(outer[step])
            if first == "x":
                spots = [at(step, None, x)]
            else:
                spots = [at(step, y, k) for k in range(2)]
            if hop is not None:
                for (copy, land), spot in zip(hop, spots):
                    copy.wait_recv()
                    add(spot, land)
            if step != 0:
                hop = []
                for spot in spots:
                    (land,) = landing((spot.shape[0], cols))
                    hop.append((copies.start(place, spot, land, "down"), land))
                yield
        src = at(0, 1 - y, x) if last == "y" else at(0, y, 1 - x)
        (land,) = landing((rows, cols))
        copy = copies.start(place, src, land, last)
        yield
        copy.wait_recv()
        out[...] = at(0, y, x)[...].astype(f32) + land[...].astype(f32)


def reduce_kernel(sizes, *refs):
    rows, cols, units_of = sizes
    n_weights = len(units_of)
    small = refs[0]
    parts = refs[1 : 1 + n_weights]
    outs = refs[1 + n_weights :]
    small_out = outs[0]
    sums = outs[1 : 1 + n_weights]
    recv, small_recv, send_sems, recv_sems = outs[1 + n_weights :]
    place = Place()
    greet(place, ("x", "y", "c", "down", "up", "z2"))
    copies = Copies(send_sems, recv_sems)
    groups, group = [], []
    index = 0
    for which, count in enumerate(units_of):
        for unit in range(count):
            order = REDUCE_ORDERS[len(group)]
            group.append(
                reduce_unit(
                    order,
                    place,
                    parts[which],
                    unit * 2 * cols,
                    rows,
                    cols,
                    recv.at[index],
                    sums[which].at[unit],
                    copies,
                )
            )
            index += 1
            if len(group) == len(REDUCE_ORDERS):
                groups.append(group)
                group = []

    def small_unit():
        small_out[0] = small[...]
        for at, which in enumerate(("c", "x", "y", "z1", "z2")):
            copy = copies.start(place, small_out.at[at], small_recv.at[at], which)
            yield
            copy.wait_recv()
            small_out[at + 1] = small_out[at] + small_recv[at]

    groups[0].append(small_unit())
    Levels(groups).drain()
    copies.finish()


def reduce_grads(small, parts, rows, cols):
    units_of = tuple(p.shape[1] // (2 * cols) for p in parts)
    n_units = sum(units_of)
    vmem = pl.BlockSpec(memory_space=pltpu.VMEM)
    out_shape = [jax.ShapeDtypeStruct((6,) + small.shape, f32)] + [
        jax.ShapeDtypeStruct((k, rows, cols), f32) for k in units_of
    ]
    n_copies = 5 + n_units * 15
    return pl.pallas_call(
        functools.partial(reduce_kernel, (rows, cols, units_of)),
        out_shape=out_shape,
        in_specs=[vmem] * (1 + len(parts)),
        out_specs=[vmem] * len(out_shape),
        scratch_shapes=[
            pltpu.VMEM((n_units, rows * 15, cols), low_type),
            pltpu.VMEM((5,) + small.shape, f32),
            pltpu.SemaphoreType.DMA((n_copies,)),
            pltpu.SemaphoreType.DMA((n_copies,)),
        ],
        input_output_aliases={},
        compiler_params=pltpu.CompilerParams(
            collective_id=1, has_side_effects=True, vmem_limit_bytes=52 * MIB
        ),
        name="reduce_grads",
    )(small, *parts)


BLOCK = 256


def split_heads(values_in):
    lane = lax.broadcasted_iota(jnp.int32, values_in.shape, 1)
    zero = jnp.zeros_like(values_in)
    return jnp.concatenate(
        [jnp.where(lane < HD, values_in, zero), jnp.where(lane >= HD, values_in, zero)], axis=0
    )


def window_start(place_ref, window, keys):
    if window == keys:
        return 0
    ends = (place_ref[0] + pl.program_id(1) + 1) * BLOCK
    return pl.multiple_of(jnp.maximum(ends - window, 0), BLOCK)


def key_scores(queries, keys, lows, highs, start):
    scores = outer_cols(keys, queries)
    ids = start + lax.broadcasted_iota(jnp.int32, scores.shape, 0)
    lows = jnp.concatenate([lows, lows], axis=1)
    highs = jnp.concatenate([highs, highs], axis=1)
    return jnp.where((ids >= lows) & (ids <= highs), scores, masked_score)


def attend_step(q_block, keys, values, lows, highs, start):
    rows = q_block.shape[0]
    queries = split_heads(q_block * jnp.asarray(HD**-0.5, low_type))
    scores = key_scores(queries, keys, lows, highs, start)
    peak = jnp.max(scores, axis=0, keepdims=True)
    probs = jnp.exp(scores - peak)
    total = jnp.sum(probs, axis=0, keepdims=True)
    context = inner_rows(values, probs.astype(low_type)) / total
    pair = jnp.concatenate([context[:HD, :rows], context[HD:, rows:]], axis=0)
    return pair.T.astype(low_type), peak + jnp.log(total)


def attention_specs(rows, keys):
    def block(i, j, p):
        return (j, i)

    def whole(i, j, p):
        return (0, i)

    def line(i, j, p):
        return (0, j)

    q_spec = pl.BlockSpec((BLOCK, PAIR), block)
    k_spec = pl.BlockSpec((keys, PAIR), whole)
    l_spec = pl.BlockSpec((1, BLOCK), line)
    lse_spec = pl.BlockSpec((1, 1, 1, 2 * BLOCK), lambda i, j, p: (i, j, 0, 0))
    return q_spec, k_spec, l_spec, lse_spec


def attend_back_kernel(
    window, place_ref, q_ref, k_ref, v_ref, low_ref, high_ref, o_ref, do_ref, lse_ref,
    dq_ref, dk_ref, dv_ref, dk_sum, dv_sum,
):
    scale = jnp.asarray(HD**-0.5, low_type)
    start = window_start(place_ref, window, k_ref.shape[0])
    here = pl.ds(start, window)
    rows = q_ref.shape[0]

    @pl.when(pl.program_id(1) == 0)
    def _():
        dk_sum[...] = jnp.zeros_like(dk_sum)
        dv_sum[...] = jnp.zeros_like(dv_sum)

    keys, values = k_ref[here], v_ref[here]
    queries = split_heads(q_ref[...] * scale)
    grads = split_heads(do_ref[...])
    scores = key_scores(queries, keys, low_ref[...], high_ref[...], start)
    probs = jnp.exp(scores - lse_ref[0, 0])
    grad_probs = outer_cols(values, grads)
    product = (do_ref[...].astype(f32) * o_ref[...].astype(f32)).T
    inner = jnp.concatenate(
        [
            jnp.sum(product[:HD], axis=0, keepdims=True),
            jnp.sum(product[HD:], axis=0, keepdims=True),
        ],
        axis=1,
    )
    grad_scores = (probs * (grad_probs - inner)).astype(low_type)
    dv_sum[here] += matmul(probs.astype(low_type), grads)
    dk_sum[here] += matmul(grad_scores, queries)
    grad_queries = inner_rows(keys, grad_scores) * HD**-0.5
    pair = jnp.concatenate([grad_queries[:HD, :rows], grad_queries[HD:, rows:]], axis=0)
    dq_ref[...] = pair.T.astype(low_type)

    @pl.when(pl.program_id(1) == pl.num_programs(1) - 1)
    def _():
        dk_ref[...] = dk_sum[...].astype(low_type)
        dv_ref[...] = dv_sum[...].astype(low_type)


def attend_back(place, queries, keys, values, lows, highs, context, grads, lse, window):
    rows, width = queries.shape
    count = keys.shape[0]
    pairs, blocks = width // PAIR, rows // BLOCK
    q_spec, k_spec, l_spec, lse_spec = attention_specs(rows, count)
    cost = pl.CostEstimate(
        flops=20 * rows * window * width,
        bytes_accessed=2 * width * (4 * rows + 4 * count),
        transcendentals=rows * window * width // HD,
    )
    return pl.pallas_call(
        functools.partial(attend_back_kernel, window),
        out_shape=[
            jax.ShapeDtypeStruct((rows, width), low_type),
            jax.ShapeDtypeStruct((count, width), low_type),
            jax.ShapeDtypeStruct((count, width), low_type),
        ],
        grid_spec=pltpu.PrefetchScalarGridSpec(
            num_scalar_prefetch=1,
            grid=(pairs, blocks),
            in_specs=[q_spec, k_spec, k_spec, l_spec, l_spec, q_spec, q_spec, lse_spec],
            out_specs=[q_spec, k_spec, k_spec],
            scratch_shapes=[pltpu.VMEM((count, PAIR), f32), pltpu.VMEM((count, PAIR), f32)],
        ),
        compiler_params=pltpu.CompilerParams(vmem_limit_bytes=48 * MIB),
        cost_estimate=cost,
        name="attend_back",
    )(place, queries, keys, values, lows, highs, context, grads, lse)


SWAP = ((0, 1), (1, 0))


def width_orders(outer, width):
    def spread(values_in):
        if outer == 1:
            return values_in
        parts = values_in.reshape(values_in.shape[:-1] + (outer, RING * 2, -1))
        return jnp.swapaxes(parts, -3, -2).reshape(values_in.shape)

    def back(values_in):
        if outer == 1:
            return values_in
        parts = values_in.reshape(values_in.shape[:-1] + (RING * 2, outer, -1))
        return jnp.swapaxes(parts, -3, -2).reshape(values_in.shape)

    return spread, back


def on_device(
    tokens,
    encoder,
    seg_ids,
    enc_lens,
    attn_qkv,
    attn_out,
    cross_q,
    cross_kv,
    cross_out,
    ffn_in,
    ffn_out,
    norm_gains,
    norm_biases,
    out_grad,
):
    outer = lax.axis_size("o")
    spread, gathered_back = width_orders(outer, tokens.shape[1])
    tokens, encoder, out_grad = spread(tokens), spread(encoder[0]), spread(out_grad)
    norm_gains, norm_biases = spread(norm_gains), spread(norm_biases)
    core, chip = lax.axis_index("c"), lax.axis_index("x")
    own = tokens.shape[0]
    half = 2 * own
    segment = seg_ids[0]
    seq_len = segment.shape[0]
    cols = cross_q.shape[1]
    width = tokens.shape[1]

    def units(block):
        k = block.shape[-1] // cols
        return block.reshape(block.shape[0], k, cols).transpose(1, 0, 2)

    shards = [
        attn_qkv.astype(low_type),
        attn_out.astype(low_type).T[None],
        cross_q.astype(low_type)[None],
        cross_kv.astype(low_type),
        cross_out.astype(low_type).T[None],
        units(ffn_in.astype(low_type)),
        units(ffn_out.astype(low_type).T),
    ]
    if outer > 1:
        shards = [lax.all_gather(s, "o", axis=1, tiled=True) for s in shards]
    rows = shards[0].shape[1]

    residual = tokens.astype(f32)
    normed, unit_one, inverse_one = norm_forward(residual, norm_gains[0], norm_biases[0])
    rows_one, qkv_w, out_w = gather_first(normed.astype(low_type), shards[:2])

    heads_width = 2 * cols

    def half_of(values_in, which):
        return lax.dynamic_slice_in_dim(values_in, which * own, own, 0)

    def core_sum(partial):
        theirs = lax.ppermute(half_of(partial, 1 - core).astype(low_type), "c", SWAP)
        return half_of(partial, core) + theirs.astype(f32)

    def core_rows(mine):
        theirs = lax.ppermute(mine, "c", SWAP)
        return jnp.concatenate(
            [jnp.where(core == 0, mine, theirs), jnp.where(core == 0, theirs, mine)], axis=0
        )

    first = chip * half
    here = lax.dynamic_slice_in_dim(segment, first, half, 0)
    lows = jnp.sum((segment[None, :] < here[:, None]).astype(jnp.int32), axis=1)[None]
    highs = (first + jnp.arange(half, dtype=jnp.int32))[None]
    enc_lows = jnp.zeros_like(highs)
    enc_highs = jnp.broadcast_to(enc_lens[0] - 1, highs.shape)
    place = (chip * (half // BLOCK))[None].astype(jnp.int32)
    window = min(seq_len, seq_len // 2 + BLOCK)

    chip_rows = lax.dynamic_slice_in_dim(rows_one, first, half, 0)
    queries_one = matmul(chip_rows, qkv_w[:, :heads_width]).astype(low_type)
    pair_one = matmul(rows_one, qkv_w[:, heads_width:]).astype(low_type)
    (
        query_w, pair_w, back_w, up_w, down_w, grads_three, enc_full, context_one, lse_one, residual_one,
        rows_two, queries_two, pair_two, context_two, lse_two, residual_two, rows_three, inner_pre,
    ) = forward(
        queries_one, pair_one, out_w, lows, highs, enc_highs, norm_gains, norm_biases, residual,
        out_grad, encoder, shards[2:], window,
    )
    enc_count = enc_full.shape[0]
    keys_one, values_one = pair_one[:, :heads_width], pair_one[:, heads_width:]
    keys_two, values_two = pair_two[:, :heads_width], pair_two[:, heads_width:]
    unit_two, inverse_two = norm_forward(residual_one, norm_gains[1], norm_biases[1])[1:]
    unit_three, inverse_three = norm_forward(residual_two, norm_gains[2], norm_biases[2])[1:]

    sigmoid_pre = jax.nn.sigmoid(inner_pre)
    active = (inner_pre * sigmoid_pre).astype(low_type)
    out_tokens = (residual_two + core_sum(outer_cols(active, down_w))).astype(low_type)

    grad_active = matmul(grads_three, down_w)
    slope = sigmoid_pre * (1.0 + inner_pre * (1.0 - sigmoid_pre))
    grad_inner = (grad_active * slope).astype(low_type)
    down_grad = inner_rows(grads_three, active).astype(low_type)
    up_grad = inner_rows(rows_three, grad_inner).astype(low_type)
    grad_normed = core_sum(outer_cols(grad_inner, up_w))
    grad_residual, gain_three, bias_three = norm_backward(
        grad_normed, unit_three, inverse_three, norm_gains[2]
    )
    grad_total = out_grad.astype(f32) + grad_residual

    grads_two = core_rows(grad_total.astype(low_type))
    grad_context = matmul(grads_two, back_w).astype(low_type)
    back_grad = inner_rows(grads_two, context_two).astype(low_type)
    grad_queries, grad_keys, grad_values = attend_back(
        place, queries_two, keys_two, values_two, enc_lows, enc_highs,
        context_two, grad_context, lse_two, enc_count,
    )
    query_grad = inner_rows(rows_two, grad_queries).astype(low_type)
    grad_pair = jnp.concatenate([grad_keys, grad_values], axis=1)
    pair_grad = inner_rows(enc_full, grad_pair).astype(low_type)
    enc_grad = lax.psum_scatter(
        outer_cols(grad_pair, pair_w).astype(low_type), ("x", "c"), scatter_dimension=0, tiled=True
    ).astype(f32)[None]
    grad_normed = core_sum(outer_cols(grad_queries, query_w))
    grad_residual, gain_two, bias_two = norm_backward(
        grad_normed, unit_two, inverse_two, norm_gains[1]
    )
    grad_total = grad_total + grad_residual

    grads_one = core_rows(grad_total.astype(low_type))
    grad_context = matmul(grads_one, out_w).astype(low_type)
    out_w_grad = inner_rows(grads_one, context_one).astype(low_type)
    grad_queries, grad_keys, grad_values = attend_back(
        place, queries_one, keys_one, values_one, lows, highs,
        context_one, grad_context, lse_one, window,
    )
    grad_pair = jnp.concatenate([grad_keys, grad_values], axis=1)
    qkv_grad = jnp.concatenate(
        [
            inner_rows(chip_rows, grad_queries).astype(low_type),
            inner_rows(rows_one, grad_pair).astype(low_type),
        ],
        axis=1,
    )
    key_term = outer_cols(grad_pair, qkv_w[:, heads_width:])
    query_term = outer_cols(grad_queries, qkv_w[:, :heads_width])
    mine = lax.dynamic_slice_in_dim(key_term, first, half, 0) + query_term
    others = lax.dynamic_slice_in_dim(key_term, (1 - chip) * half, half, 0)
    to_chip = lax.ppermute(core_sum(others).astype(low_type), "x", SWAP)
    grad_normed = core_sum(mine) + to_chip.astype(f32)
    grad_residual, gain_one, bias_one = norm_backward(
        grad_normed, unit_one, inverse_one, norm_gains[0]
    )
    in_grad = grad_total + grad_residual

    small = jnp.stack([gain_one, gain_two, gain_three, bias_one, bias_two, bias_three])
    small = jnp.concatenate([small, jnp.zeros((2, width), f32)], axis=0)
    grads = [up_grad, down_grad, back_grad, query_grad, pair_grad, out_w_grad, qkv_grad]
    small, *sums = reduce_grads(small, grads, rows, cols)
    small = small[-1]
    if outer > 1:
        small = lax.psum(small, "o")
        sums = [lax.psum_scatter(s, "o", scatter_dimension=1, tiled=True) for s in sums]
    up_sum, down_sum, back_sum, query_sum, pair_sum, out_sum, qkv_sum = sums

    def joined(block):
        return block.transpose(1, 0, 2).reshape(block.shape[1], -1)

    return (
        gathered_back(out_tokens),
        gathered_back(in_grad),
        gathered_back(enc_grad),
        qkv_sum,
        out_sum[0].T,
        query_sum[0],
        pair_sum,
        back_sum[0].T,
        joined(up_sum),
        joined(down_sum).T,
        gathered_back(small[:3]),
        gathered_back(small[3:6]),
    )


def solution(mesh):
    count, tensor = mesh.devices.shape
    outer = count // (RING * 2)
    fine = Mesh(
        mesh.devices.reshape(outer, RING, 2, tensor // 2, 2), ("o", "z", "y", "x", "c")
    )
    dp, tp = ("o", "z", "y"), ("x", "c")
    in_specs = (
        P(dp + tp, None),
        P(dp, tp, None),
        P(dp, None),
        P(dp),
        P(None, dp, tp),
        P(tp, dp),
        P(dp, tp),
        P(None, dp, tp),
        P(tp, dp),
        P(dp, tp),
        P(tp, dp),
        P(),
        P(),
        P(dp + tp, None),
    )
    out_specs = (
        P(dp + tp, None),
        P(dp + tp, None),
        P(dp, tp, None),
        P(None, dp, tp),
        P(tp, dp),
        P(dp, tp),
        P(None, dp, tp),
        P(tp, dp),
        P(dp, tp),
        P(tp, dp),
        P(),
        P(),
    )
    return jax.shard_map(
        on_device, mesh=fine, in_specs=in_specs, out_specs=out_specs, check_vma=False
    )
```

```python
import functools

import jax
import jax.numpy as jnp
from jax import lax
from jax.experimental import pallas as pl
from jax.experimental.pallas import tpu as pltpu
from jax.sharding import Mesh
from jax.sharding import PartitionSpec as P

HD = 64
LANES = 128
PAIR = 2 * HD
RING = 4
epsilon = 1e-05
masked_score = -1e30
MESH = pl.DeviceIdType.MESH
low_type = jnp.bfloat16
f32 = jnp.float32
MIB = 1 << 20


def matmul(left, right):
    return jnp.dot(left, right, preferred_element_type=f32)


def inner_rows(left, right):
    return lax.dot_general(left, right, (((0,), (0,)), ((), ())), preferred_element_type=f32)


def outer_cols(left, right):
    return lax.dot_general(left, right, (((1,), (1,)), ((), ())), preferred_element_type=f32)


def norm_forward(values_in, gain_row, bias_row):
    average = jnp.mean(values_in, axis=-1, keepdims=True)
    centred = values_in - average
    inverse = lax.rsqrt(jnp.mean(centred * centred, axis=-1, keepdims=True) + epsilon)
    unit_rows = centred * inverse
    return (unit_rows * gain_row + bias_row, unit_rows, inverse)


def norm_backward(incoming, unit_rows, inverse, gain_row):
    scaled = incoming * gain_row
    first_mean = jnp.mean(scaled, axis=-1, keepdims=True)
    second_mean = jnp.mean(scaled * unit_rows, axis=-1, keepdims=True)
    result = inverse * (scaled - first_mean - unit_rows * second_mean)
    return (result, jnp.sum(incoming * unit_rows, axis=0), jnp.sum(incoming, axis=0))


class Place:
    def __init__(self):
        self.z = lax.axis_index("z")
        self.y = lax.axis_index("y")
        self.x = lax.axis_index("x")
        self.c = lax.axis_index("c")

    def to(self, which):
        if which == "x":
            return {"x": 1 - self.x}
        if which == "y":
            return {"y": 1 - self.y}
        if which == "c":
            return {"c": 1 - self.c}
        if which == "z1":
            return {"z": self.z + 1 - 2 * lax.rem(self.z, 2)}
        if which == "z2":
            return {"z": lax.rem(self.z + 2, RING)}
        if which == "down":
            return {"z": lax.rem(self.z + RING - 1, RING)}
        return {"z": lax.rem(self.z + 1, RING)}

    def ring(self, step):
        return lax.rem(self.z + step, RING)


def greet(place, names):
    barrier = pltpu.get_barrier_semaphore()
    for name in names:
        pl.semaphore_signal(barrier, inc=1, device_id=place.to(name), device_id_type=MESH)
    pl.semaphore_wait(barrier, len(names))


class Copies:
    def __init__(self, send_sems, recv_sems):
        self.send_sems, self.recv_sems = send_sems, recv_sems
        self.made = []

    def start(self, place, src, dst, which):
        at = len(self.made)
        copy = pltpu.make_async_remote_copy(
            src_ref=src,
            dst_ref=dst,
            send_sem=self.send_sems.at[at],
            recv_sem=self.recv_sems.at[at],
            device_id=place.to(which),
            device_id_type=MESH,
        )
        copy.start()
        self.made.append(copy)
        return copy

    def finish(self):
        for copy in self.made:
            copy.wait_send()


GATHER_ORDERS = ("xzy", "yzx", "zyx", "zxy")


def gather_unit(order, place, own, whole, base, rows, cols, copies):
    x, y = place.x, place.y

    def at(step, both_y, both_x):
        first = place.ring(step) * 2
        row = first * rows if both_y else (first + y) * rows
        col = base if both_x else base + x * cols
        return whole.at[
            pl.ds(pl.multiple_of(row, rows), rows * (2 if both_y else 1)),
            pl.ds(pl.multiple_of(col, LANES), cols * (2 if both_x else 1)),
        ]

    def send(where, which):
        return copies.start(place, where, where, which)

    arrived = {}
    mine = at(0, False, False)
    if order in ("xzy", "yzx"):
        axis, last = order[0], order[2]
        wide = dict(both_y=axis == "y", both_x=axis == "x")
        first = copies.start(place, own, mine, axis)
        yield
        first.wait_recv()
        hop = send(at(0, **wide), "down")
        ends = [send(at(0, **wide), last)]
        yield
        for step in range(1, RING):
            hop.wait_recv()
            if step < RING - 1:
                hop = send(at(step, **wide), "down")
            ends.append(send(at(step, **wide), last))
            yield
        for copy in ends:
            copy.wait_recv()
    else:
        mid, last = order[1], order[2]
        wide = dict(both_y=mid == "y", both_x=mid == "x")
        hop = copies.start(place, own, mine, "down")
        mids = [copies.start(place, own, mine, mid)]
        ends = []
        yield
        for step in range(1, RING + 1):
            if step < RING:
                hop.wait_recv()
                if step < RING - 1:
                    hop = send(at(step, False, False), "down")
                mids.append(send(at(step, False, False), mid))
            mids[step - 1].wait_recv()
            ends.append(send(at(step - 1, **wide), last))
            yield
        for copy in ends:
            copy.wait_recv()
    del arrived


class Levels:
    def __init__(self, groups, spacing=None):
        self.live = [list(g) for g in groups]
        self.spacing = spacing
        self.level = 0
        self.started = 0

    def begin(self):
        self.started += 1
        self.step()

    def step(self):
        if self.spacing and self.started < len(self.live) and self.level % self.spacing == 0:
            self.started += 1
        for group in self.live[: self.started]:
            for unit in list(group):
                try:
                    next(unit)
                except StopIteration:
                    group.remove(unit)
        self.level += 1

    def until(self, group):
        while self.live[group]:
            self.step()

    def drain(self):
        for group in range(len(self.live)):
            self.until(group)


class Locals:
    def __init__(self, sems):
        self.sems, self.made = sems, []

    def start(self, src, dst):
        copy = pltpu.make_async_copy(src, dst, self.sems.at[len(self.made)])
        copy.start()
        self.made.append(copy)
        return len(self.made) - 1

    def wait(self, *which):
        for at in which:
            if self.made[at] is not None:
                self.made[at].wait()
                self.made[at] = None

    def finish(self):
        self.wait(*range(len(self.made)))


def gather_groups(place, sizes, own, whole, copies, local, orders):
    rows, cols, units_of = sizes
    groups, group = [], []
    index = 0
    for which, count in enumerate(units_of):
        for unit in range(count):
            base = unit * 2 * cols
            src = own[which].at[unit]
            local.start(
                src,
                whole[which].at[
                    pl.ds(pl.multiple_of((place.z * 2 + place.y) * rows, rows), rows),
                    pl.ds(pl.multiple_of(base + place.x * cols, LANES), cols),
                ],
            )
            group.append(
                gather_unit(
                    orders[index], place, src, whole[which], base, rows, cols, copies
                )
            )
            index += 1
            if len(group) == 4:
                groups.append(group)
                group = []
    return groups


def first_kernel(sizes, orders, *refs):
    n_weights = len(sizes[2])
    h_own, *own = refs[: 1 + n_weights]
    h_all, *whole = refs[1 + n_weights : 2 + 2 * n_weights]
    send_sems, recv_sems, local_sems = refs[2 + 2 * n_weights :]
    place = Place()
    greet(place, ("x", "y", "c", "down", "up"))
    copies = Copies(send_sems, recv_sems)
    local = Locals(local_sems)
    x, c = place.x, place.c
    n = h_own.shape[0]

    def h_at(xx, cc):
        return h_all.at[pl.ds(pl.multiple_of((xx * 2 + cc) * n, 16), n)]

    hx = copies.start(place, h_own, h_at(x, c), "x")
    hc = copies.start(place, h_own, h_at(x, c), "c")
    local.start(h_own, h_at(x, c))
    groups = gather_groups(place, sizes, own, whole, copies, local, orders)
    local.finish()

    def rows_unit():
        yield
        yield
        hx.wait_recv()
        hxc = copies.start(place, h_at(1 - x, c), h_at(1 - x, c), "c")
        yield
        yield
        hc.wait_recv()
        hxc.wait_recv()

    groups[0].append(rows_unit())
    Levels(groups, 3).drain()
    copies.finish()


ANY_SPEC = pl.BlockSpec(memory_space=pl.ANY)
VMEM_SPEC = pl.BlockSpec(memory_space=pltpu.VMEM)


def gather_shapes(shards):
    units_of = tuple(s.shape[0] for s in shards)
    rows, cols = shards[0].shape[1:]
    depth = rows * RING * 2
    shapes = [jax.ShapeDtypeStruct((depth, 2 * cols * k), low_type) for k in units_of]
    return (rows, cols, units_of), shapes


def gather_first(h_own, shards):
    sizes, shapes = gather_shapes(shards)
    n, width = h_own.shape
    n_units = sum(sizes[2])
    n_copies = 3 + n_units * 11
    out_shape = [jax.ShapeDtypeStruct((4 * n, width), low_type)] + shapes
    return pl.pallas_call(
        functools.partial(first_kernel, sizes, ("xzy", "zxy", "yzx", "xzy")),
        out_shape=out_shape,
        in_specs=[ANY_SPEC] * (1 + len(shards)),
        out_specs=[VMEM_SPEC] * len(out_shape),
        scratch_shapes=[
            pltpu.SemaphoreType.DMA((n_copies,)),
            pltpu.SemaphoreType.DMA((n_copies,)),
            pltpu.SemaphoreType.DMA((1 + n_units,)),
        ],
        compiler_params=pltpu.CompilerParams(
            collective_id=0, has_side_effects=True, vmem_limit_bytes=30 * MIB
        ),
        name="gather_first",
    )(h_own, *shards)


def norm_rows(values_in, gain_row, bias_row):
    return norm_forward(values_in, gain_row, bias_row)[0]


def loop_rows(count, tile, body):
    @pl.loop(0, count // tile)
    def _(i):
        body(pl.ds(pl.multiple_of(i * tile, tile), tile))


def exchange_rows(place, copies, n, sent, landed, make):
    @pl.loop(0, n // LANES)
    def _(i):
        tile = pl.ds(pl.multiple_of(i * LANES, LANES), LANES)
        theirs = pl.ds(pl.multiple_of((1 - place.c) * n + i * LANES, LANES), LANES)
        sent[tile] = make(theirs).astype(low_type)

    return copies.start(place, sent, landed, "c")


def own_tiles(place, n, body):
    @pl.loop(0, n // LANES)
    def _(i):
        tile = pl.ds(pl.multiple_of(i * LANES, LANES), LANES)
        body(tile, pl.ds(pl.multiple_of(place.c * n + i * LANES, LANES), LANES))


def blocks_of(place, rows_count, pair_count, span):
    def at(block):
        rows = pl.ds(pl.multiple_of(block * BLOCK, BLOCK), BLOCK)
        if span == pair_count:
            return rows, 0
        ends = (place.x * (rows_count // BLOCK) + block + 1) * BLOCK
        return rows, pl.multiple_of(jnp.maximum(ends - span, 0), BLOCK)

    return at


def forward_kernel(sizes, window, n_out, *refs):
    n_weights = len(sizes[2])
    (lows, highs, enc_highs, gains, biases, *hbm) = refs[: 9 + 2 + 2 + n_weights - 2]
    (q_in, pair_in, out_w_in, residual_in, g_own, enc_own, *own) = hbm
    at = 11 + n_weights
    outs, held = refs[at : at + n_out], refs[at + n_out : at + 2 * n_out]
    (q_one, pair_one, out_w, residual, sent, landed, send_sems, recv_sems, local_sems) = refs[
        at + 2 * n_out :
    ]
    whole = held[:n_weights]
    (
        g_all, enc_all, context_one, lse_one, residual_one, rows_two, q_two, pair_two, context_two,
        lse_two, residual_two, rows_three, active, slope,
    ) = held[n_weights:]
    query_w, pair_w, back_w, up_w, _ = whole
    place = Place()
    copies = Copies(send_sems, recv_sems)
    local = Locals(local_sems)
    loads = [
        local.start(src, dst)
        for src, dst in (
            (q_in, q_one), (pair_in, pair_one), (out_w_in, out_w), (residual_in, residual),
        )
    ]
    greet(place, ("x", "y", "c", "down", "up"))
    x, c = place.x, place.c
    n, e = residual.shape[0], enc_own.shape[0]
    heads_width = q_one.shape[1]
    mine = pl.ds(pl.multiple_of(c * n, 16), n)

    def flush(*names):
        for ref in names:
            local.start(ref, outs[[h is ref for h in held].index(True)])

    def e_at(xx, cc):
        return enc_all.at[pl.ds(pl.multiple_of((xx * 2 + cc) * e, 16), e)]

    ex = copies.start(place, enc_own, e_at(x, c), "x")
    ec = copies.start(place, enc_own, e_at(x, c), "c")
    gc = copies.start(place, g_own, g_all.at[mine], "c")
    first = len(local.made)
    local.start(g_own, g_all.at[mine])
    local.start(enc_own, e_at(x, c))
    orders = ("xzy", "yzx", "xzy", "zxy") + GATHER_ORDERS * 2
    groups = gather_groups(place, sizes, own, whole, copies, local, orders)
    local.wait(*range(first, len(local.made)))

    def enc_unit():
        yield
        yield
        ex.wait_recv()
        exc = copies.start(place, e_at(1 - x, c), e_at(1 - x, c), "c")
        yield
        yield
        ec.wait_recv()
        gc.wait_recv()
        exc.wait_recv()

    groups[0].append(enc_unit())
    comm = Levels(groups, 3)

    def attention(q_ref, pair_ref, low_of, high_of, o_ref, lse_ref, span):
        block_at = blocks_of(place, q_ref.shape[0], pair_ref.shape[0], span)
        for pair in range(heads_width // PAIR):
            comm.step()
            lanes = pl.ds(pair * PAIR, PAIR)
            value_lanes = pl.ds(heads_width + pair * PAIR, PAIR)

            @pl.loop(0, q_ref.shape[0] // BLOCK)
            def _(block):
                rows, start = block_at(block)
                here = pl.ds(start, span)
                o_ref[rows, lanes], lse_ref[pair, block] = attend_step(
                    q_ref[rows, lanes],
                    pair_ref[here, lanes],
                    pair_ref[here, value_lanes],
                    low_of(rows),
                    high_of(rows),
                    start,
                )

    def branch(at, context, weight, before, after, gain_at, rows_ref):
        over = exchange_rows(
            place, copies, n, sent.at[at], landed.at[at],
            lambda rows: outer_cols(context[rows], weight[...]),
        )

        def own_part(tile, rows):
            after[tile] = before[tile] + outer_cols(context[rows], weight[...])

        own_tiles(place, n, own_part)
        over.wait_recv()

        def rest(tile, rows):
            total = after[tile] + landed[at, tile].astype(f32)
            after[tile] = total
            rows_ref[rows] = norm_rows(
                total, gains[gain_at : gain_at + 1], biases[gain_at : gain_at + 1]
            ).astype(low_type)

        own_tiles(place, n, rest)
        return copies.start(place, rows_ref.at[mine], rows_ref.at[mine], "c")

    local.wait(*loads)
    attention(
        q_one, pair_one, lambda r: lows[:, r], lambda r: highs[:, r], context_one, lse_one, window
    )
    comm.step()
    over = branch(0, context_one, out_w, residual, residual_one, 1, rows_two)
    flush(context_one, lse_one, residual_one)
    comm.until(0)
    loop_rows(
        enc_all.shape[0], BLOCK, lambda r: store(pair_two, r, matmul(enc_all[r], pair_w[...]))
    )
    flush(query_w, pair_w, back_w, g_all, enc_all, pair_two)
    over.wait_recv()
    comm.step()
    loop_rows(2 * n, BLOCK, lambda r: store(q_two, r, matmul(rows_two[r], query_w[...])))
    flush(rows_two, q_two)
    attention(
        q_two, pair_two, lambda r: jnp.zeros((1, BLOCK), jnp.int32), lambda r: enc_highs[:, r],
        context_two, lse_two, enc_all.shape[0],
    )
    comm.step()
    over = branch(1, context_two, back_w, residual_one, residual_two, 2, rows_three)
    flush(context_two, lse_two, residual_two)
    comm.until(1)
    over.wait_recv()
    flush(rows_three, up_w)

    def up(rows):
        inner = matmul(rows_three[rows], up_w[...])
        gate = 1.0 / (1.0 + jnp.exp(-inner))
        active[rows] = (inner * gate).astype(low_type)
        slope[rows] = (gate * (1.0 + inner * (1.0 - gate))).astype(low_type)

    loop_rows(2 * n, LANES, up)
    flush(active, slope)
    comm.drain()
    flush(whole[-1])
    local.finish()
    copies.finish()


def store(ref, rows, values_in):
    ref[rows] = values_in.astype(ref.dtype)


def low(*shape):
    return jax.ShapeDtypeStruct(shape, low_type)


def wide(*shape):
    return jax.ShapeDtypeStruct(shape, f32)


def scratch_like(shapes):
    return [pltpu.VMEM(s.shape, s.dtype) for s in shapes]


def forward(q_one, pair_one, out_w, lows, highs, enc_highs, gains, biases, residual, g_own, enc_own, shards, window):
    sizes, shapes = gather_shapes(shards)
    n, width = residual.shape
    e = enc_own.shape[0]
    hidden = shapes[-1].shape[1]
    heads_width = q_one.shape[1]
    n_units = sum(sizes[2])
    n_copies = 8 + n_units * 11
    lse = wide(heads_width // PAIR, 2 * n // BLOCK, 1, 2 * BLOCK)
    out_shape = shapes + [
        low(2 * n, width), low(4 * e, width), low(2 * n, heads_width), lse, wide(n, width), low(2 * n, width),
        low(2 * n, heads_width), low(4 * e, 2 * heads_width), low(2 * n, heads_width), lse, wide(n, width),
        low(2 * n, width), low(2 * n, hidden), low(2 * n, hidden),
    ]
    return pl.pallas_call(
        functools.partial(forward_kernel, sizes, window, len(out_shape)),
        out_shape=out_shape,
        in_specs=[VMEM_SPEC] * 5 + [ANY_SPEC] * (6 + len(shards)),
        out_specs=[ANY_SPEC] * len(out_shape),
        scratch_shapes=scratch_like(out_shape)
        + scratch_like([q_one, pair_one, out_w, residual])
        + scratch_like([low(2, n, width)] * 2)
        + [
            pltpu.SemaphoreType.DMA((n_copies,)),
            pltpu.SemaphoreType.DMA((n_copies,)),
            pltpu.SemaphoreType.DMA((6 + n_units + len(out_shape),)),
        ],
        compiler_params=pltpu.CompilerParams(
            collective_id=2, has_side_effects=True, vmem_limit_bytes=60 * MIB
        ),
        name="forward",
    )(
        lows, highs, enc_highs, gains, biases, q_one, pair_one, out_w, residual, g_own, enc_own, *shards
    )


REDUCE_ORDERS = ("xyz", "xzy", "yxz", "yzx")
CHUNK_ORDER = tuple(range(1, RING)) + (0,)


def reduce_unit(order, place, part, base, rows, cols, recv, out, copies):
    x, y = place.x, place.y

    def at(step, row_of, col_of):
        first = place.ring(step) * 2
        row = first * rows if row_of is None else (first + row_of) * rows
        col = base if col_of is None else base + col_of * cols
        return part.at[
            pl.ds(pl.multiple_of(row, rows), rows * (2 if row_of is None else 1)),
            pl.ds(pl.multiple_of(col, LANES), cols * (2 if col_of is None else 1)),
        ]

    used = [0]

    def landing(shape):
        height = shape[0] * (shape[1] // cols)
        where = [
            recv.at[pl.ds(used[0] + k * shape[0], shape[0])] for k in range(shape[1] // cols)
        ]
        used[0] += height
        return where

    def pieces(where, shape):
        return where

    def add(target, source):
        target[...] = (target[...].astype(f32) + source[...].astype(f32)).astype(low_type)

    def exchange(step, which, mid):
        sent = []
        if which == "x":
            if mid:
                spots = [(at(step, y, 1 - x), at(step, y, x))]
            else:
                spots = [(at(step, None, 1 - x), at(step, None, x))]
        else:
            if mid:
                spots = [(at(step, 1 - y, x), at(step, y, x))]
            else:
                spots = [(at(step, 1 - y, k), at(step, y, k)) for k in range(2)]
        for src, keep_at in spots:
            (land,) = landing((src.shape[0], cols))
            sent.append((copies.start(place, src, land, which), keep_at, land))
        return sent

    def take(sent):
        for copy, keep_at, land in sent:
            copy.wait_recv()
            add(keep_at, land)

    first, middle, last = order
    outer = {s: exchange(s, first, False) for s in CHUNK_ORDER}
    yield
    if last == "z":
        inner = {}
        hop = None
        for k, step in enumerate(CHUNK_ORDER):
            take(outer[step])
            inner[step] = exchange(step, middle, True)
            yield
        for step in CHUNK_ORDER:
            take(inner[step])
            if hop is not None:
                copy, land = hop
                copy.wait_recv()
                if step == 0:
                    total = at(0, y, x)[...].astype(f32) + land[...].astype(f32)
                    out[...] = total
                else:
                    add(at(step, y, x), land)
            if step != 0:
                (land,) = landing((rows, cols))
                hop = (copies.start(place, at(step, y, x), land, "down"), land)
                yield
    else:
        hop = None
        for step in CHUNK_ORDER:
            take(outer[step])
            if first == "x":
                spots = [at(step, None, x)]
            else:
                spots = [at(step, y, k) for k in range(2)]
            if hop is not None:
                for (copy, land), spot in zip(hop, spots):
                    copy.wait_recv()
                    add(spot, land)
            if step != 0:
                hop = []
                for spot in spots:
                    (land,) = landing((spot.shape[0], cols))
                    hop.append((copies.start(place, spot, land, "down"), land))
                yield
        src = at(0, 1 - y, x) if last == "y" else at(0, y, 1 - x)
        (land,) = landing((rows, cols))
        copy = copies.start(place, src, land, last)
        yield
        copy.wait_recv()
        out[...] = at(0, y, x)[...].astype(f32) + land[...].astype(f32)


def reduce_groups(place, rows, cols, part, recv, outs, copies, first):
    return [
        reduce_unit(
            order, place, part, unit * 2 * cols, rows, cols, recv.at[first + unit], outs[unit], copies
        )
        for unit, order in enumerate(REDUCE_ORDERS)
    ]


def attention_back(place, comm, q_ref, pair_ref, low_of, high_of, o_ref, do_ref, lse_ref, span, dk_sum, dv_sum):
    heads_width = q_ref.shape[1]
    block_at = blocks_of(place, q_ref.shape[0], pair_ref.shape[0], span)
    for pair in range(heads_width // PAIR):
        comm.step()
        lanes = pl.ds(pair * PAIR, PAIR)
        value_lanes = pl.ds(heads_width + pair * PAIR, PAIR)
        dk_sum[...] = jnp.zeros_like(dk_sum)
        dv_sum[...] = jnp.zeros_like(dv_sum)

        @pl.loop(0, q_ref.shape[0] // BLOCK)
        def _(block):
            rows, start = block_at(block)
            here = pl.ds(start, span)
            dq, dk, dv = attend_back_step(
                q_ref[rows, lanes],
                pair_ref[here, lanes],
                pair_ref[here, value_lanes],
                low_of(rows),
                high_of(rows),
                start,
                o_ref[rows, lanes],
                do_ref[rows, lanes],
                lse_ref[pair, block],
            )
            q_ref[rows, lanes] = dq
            dk_sum[here] += dk
            dv_sum[here] += dv

        pair_ref[:, lanes] = dk_sum[...].astype(low_type)
        pair_ref[:, value_lanes] = dv_sum[...].astype(low_type)


def loop_cols(count, tile, body):
    loop_rows(count, tile, body)


def norm_back_tile(small, at, incoming, before, gain_row):
    _, unit_rows, inverse = norm_forward(before, jnp.ones_like(gain_row), jnp.zeros_like(gain_row))
    result, gain_sum, bias_sum = norm_backward(incoming, unit_rows, inverse, gain_row)
    small[at : at + 1] += gain_sum[None]
    small[at + 3 : at + 4] += bias_sum[None]
    return result


def back_one_kernel(sizes, *refs):
    rows, cols = sizes
    (
        enc_highs, gains, lse_two,
        down_in, up_in, active_in, slope_in, g_in, rows_in, residual_in, q_in, pair_in, context_in, back_in,
        down_sum, up_sum, small, out_tokens, grad_out, back_out, dq_out, dpair_out,
        down_w, up_w, active, slope, g_all, rows_three, residual, q_two, pair_two, context, back_w,
        part_down, part_up, recv, sent, landed, grad, g_two, back_part, grad_context, tokens_out, dk_sum, dv_sum,
        send_sems, recv_sems, local_sems,
    ) = refs
    place = Place()
    copies = Copies(send_sems, recv_sems)
    local = Locals(local_sems)
    c = place.c
    g_at, active_at, down_at, slope_at, rows_at, up_at, res_at, con_at, back_at, q_at, pair_at = [
        local.start(src, dst)
        for src, dst in (
            (g_in, g_all), (active_in, active), (down_in, down_w), (slope_in, slope), (rows_in, rows_three),
            (up_in, up_w), (residual_in, residual), (context_in, context), (back_in, back_w),
            (q_in, q_two), (pair_in, pair_two),
        )
    ]
    greet(place, ("x", "y", "c", "down", "up"))
    n, width = residual.shape
    mine = pl.ds(pl.multiple_of(c * n, 16), n)
    comm = Levels(
        [
            reduce_groups(place, rows, cols, part_down, recv, [down_sum.at[k] for k in range(4)], copies, 0),
            reduce_groups(place, rows, cols, part_up, recv, [up_sum.at[k] for k in range(4)], copies, 4),
        ]
    )
    small[...] = jnp.zeros_like(small)
    local.wait(g_at, active_at)
    loop_cols(width, BLOCK, lambda t: store(part_down, t, inner_rows(g_all[:, t], active[...])))
    comm.begin()
    local.wait(down_at, slope_at)

    def inner(tile):
        slope[tile] = (matmul(g_all[tile], down_w[...]) * slope[tile].astype(f32)).astype(low_type)

    loop_rows(2 * n, LANES, inner)
    local.wait(rows_at)
    loop_cols(width, BLOCK, lambda t: store(part_up, t, inner_rows(rows_three[:, t], slope[...])))
    comm.begin()
    local.wait(up_at)
    over = exchange_rows(
        place, copies, n, sent.at[0], landed.at[0], lambda r: outer_cols(slope[r], up_w[...])
    )

    def own_part(tile, rows_here):
        grad[tile] = outer_cols(slope[rows_here], up_w[...])

    own_tiles(place, n, own_part)
    comm.step()
    out_over = exchange_rows(
        place, copies, n, sent.at[1], landed.at[1], lambda r: outer_cols(active[r], down_w[...])
    )
    local.wait(res_at)
    over.wait_recv()

    def norm_part(tile, rows_here):
        incoming = grad[tile] + landed[0, tile].astype(f32)
        total = g_all[rows_here].astype(f32) + norm_back_tile(
            small, 2, incoming, residual[tile], gains[2:3]
        )
        grad[tile] = total
        g_two[rows_here] = total.astype(low_type)

    own_tiles(place, n, norm_part)
    g_over = copies.start(place, g_two.at[mine], g_two.at[mine], "c")
    local.start(grad, grad_out)
    comm.step()
    out_over.wait_recv()

    def out_part(tile, rows_here):
        total = residual[tile] + outer_cols(active[rows_here], down_w[...])
        tokens_out[tile] = (total + landed[1, tile].astype(f32)).astype(low_type)

    own_tiles(place, n, out_part)
    local.start(tokens_out, out_tokens)
    local.wait(con_at, back_at)
    g_over.wait_recv()
    loop_rows(2 * n, BLOCK, lambda r: store(grad_context, r, matmul(g_two[r], back_w[...])))
    loop_cols(width, BLOCK, lambda t: store(back_part, t, inner_rows(g_two[:, t], context[...])))
    local.start(back_part, back_out)
    local.wait(q_at, pair_at)
    attention_back(
        place, comm, q_two, pair_two, lambda r: jnp.zeros((1, BLOCK), jnp.int32),
        lambda r: enc_highs[:, r], context, grad_context, lse_two, pair_two.shape[0], dk_sum, dv_sum,
    )
    local.start(q_two, dq_out)
    local.start(pair_two, dpair_out)
    comm.drain()
    local.finish()
    copies.finish()


def back_one(enc_highs, gains, lse_two, down_w, up_w, active, slope, g_all, rows_three, residual, q_two, pair_two, context, back_w, rows, cols):
    n, width = residual.shape
    heads_width = q_two.shape[1]
    unit_sum = wide(4, rows, cols)
    hbm = [down_w, up_w, active, slope, g_all, rows_three, residual, q_two, pair_two, context, back_w]
    out_shape = [
        unit_sum, unit_sum, wide(8, width), low(n, width), wide(n, width), low(width, heads_width),
        low(2 * n, heads_width), low(*pair_two.shape),
    ]
    n_copies = 8 * 15 + 3
    return pl.pallas_call(
        functools.partial(back_one_kernel, (rows, cols)),
        out_shape=out_shape,
        in_specs=[VMEM_SPEC] * 3 + [ANY_SPEC] * len(hbm),
        out_specs=[VMEM_SPEC] * 3 + [ANY_SPEC] * 5,
        scratch_shapes=scratch_like(hbm)
        + scratch_like(
            [
                low(*down_w.shape), low(*up_w.shape), low(8, rows * 15, cols), low(2, n, width),
                low(2, n, width), wide(n, width), low(2 * n, width), low(width, heads_width),
                low(2 * n, heads_width), low(n, width), wide(pair_two.shape[0], PAIR), wide(pair_two.shape[0], PAIR),
            ]
        )
        + [
            pltpu.SemaphoreType.DMA((n_copies,)),
            pltpu.SemaphoreType.DMA((n_copies,)),
            pltpu.SemaphoreType.DMA((len(hbm) + 5,)),
        ],
        compiler_params=pltpu.CompilerParams(
            collective_id=1, has_side_effects=True, vmem_limit_bytes=60 * MIB
        ),
        name="back_one",
    )(enc_highs, gains, lse_two, *hbm)


def back_two_kernel(sizes, window, *refs):
    rows, cols = sizes
    (
        lows, highs, gains, lse_one, small_in,
        dq_in, dpair_in, rows_two_in, enc_in, query_in, pair_w_in, back_in, grad_in, residual_in, context_in,
        out_w_in, q_in, pair_in, rows_one_in, qkv_in, tokens_in,
        back_sum, query_sum, pair_sum, out_sum, qkv_sum, small_out, in_grad, enc_grad,
        dq_two, dpair_two, rows_two, enc_all, query_w, pair_w, grad, residual, context, out_w, q_one,
        pair_one, rows_one, qkv_w, tokens,
        part_cross, part_self, recv, sent, landed, total, g_one, grad_context, dk_sum, dv_sum,
        enc_sent, enc_landed, enc_total, small_recv, send_sems, recv_sems, local_sems,
    ) = refs
    place = Place()
    copies = Copies(send_sems, recv_sems)
    local = Locals(local_sems)
    x, c = place.x, place.c
    n, width = residual.shape
    heads_width = q_one.shape[1]
    e = enc_grad.shape[0]
    (
        dpair_at, enc_at, dq_at, rows_two_at, back_at, query_at, pair_w_at, grad_at, res_at, con_at, out_w_at,
        q_at, pair_at, rows_one_at, qkv_at, tokens_at,
    ) = [
        local.start(src, dst)
        for src, dst in (
            (dpair_in, dpair_two), (enc_in, enc_all), (dq_in, dq_two), (rows_two_in, rows_two),
            (back_in, part_cross.at[:, pl.ds(0, heads_width)]), (query_in, query_w), (pair_w_in, pair_w),
            (grad_in, grad), (residual_in, residual), (context_in, context), (out_w_in, out_w), (q_in, q_one),
            (pair_in, pair_one), (rows_one_in, rows_one), (qkv_in, qkv_w), (tokens_in, tokens),
        )
    ]
    greet(place, ("x", "y", "c", "down", "up", "z2"))
    mine = pl.ds(pl.multiple_of(c * n, 16), n)

    def small_unit():
        for at, which in enumerate(("c", "x", "y", "z1", "z2")):
            copy = copies.start(place, small_out.at[at], small_recv.at[at], which)
            yield
            copy.wait_recv()
            small_out[at + 1] = small_out[at] + small_recv[at]

    cross_sums = [back_sum.at[0], query_sum.at[0], pair_sum.at[0], pair_sum.at[1]]
    self_sums = [out_sum.at[0], qkv_sum.at[0], qkv_sum.at[1], qkv_sum.at[2]]
    comm = Levels(
        [
            reduce_groups(place, rows, cols, part_cross, recv, cross_sums, copies, 0),
            reduce_groups(place, rows, cols, part_self, recv, self_sums, copies, 4),
            [small_unit()],
        ]
    )
    small = small_out.at[0]
    small[...] = small_in[...]
    second = pl.ds(heads_width, heads_width)
    rest = pl.ds(2 * heads_width, 2 * heads_width)
    local.wait(dpair_at, enc_at)

    def pair_grads(t):
        part_cross[t, rest] = inner_rows(enc_all[:, t], dpair_two[...]).astype(low_type)

    loop_cols(width, BLOCK, pair_grads)
    local.wait(dq_at, rows_two_at, back_at)

    def query_grads(t):
        part_cross[t, second] = inner_rows(rows_two[:, t], dq_two[...]).astype(low_type)

    loop_cols(width, BLOCK, query_grads)
    comm.begin()
    local.wait(query_at)
    over = exchange_rows(
        place, copies, n, sent.at[0], landed.at[0], lambda r: outer_cols(dq_two[r], query_w[...])
    )

    def own_part(tile, rows_here):
        total[tile] = outer_cols(dq_two[rows_here], query_w[...])

    own_tiles(place, n, own_part)
    local.wait(pair_w_at)

    def enc_rows(xx, cc):
        return pl.ds(pl.multiple_of((xx * 2 + cc) * e, LANES), e)

    def enc_term(xx, cc):
        return outer_cols(dpair_two[enc_rows(xx, cc)], pair_w[...])

    enc_sent[0] = enc_term(x, 1 - c).astype(low_type)
    enc_sent[1] = enc_term(1 - x, 1 - c).astype(low_type)
    enc_over = copies.start(place, enc_sent.at[pl.ds(0, 2)], enc_landed.at[pl.ds(0, 2)], "c")
    local.wait(grad_at, res_at)
    over.wait_recv()

    def norm_part(tile, rows_here):
        incoming = total[tile] + landed[0, tile].astype(f32)
        after = grad[tile] + norm_back_tile(small, 1, incoming, residual[tile], gains[1:2])
        grad[tile] = after
        g_one[rows_here] = after.astype(low_type)

    own_tiles(place, n, norm_part)
    g_over = copies.start(place, g_one.at[mine], g_one.at[mine], "c")
    comm.step()
    enc_over.wait_recv()
    enc_sent[2] = (enc_term(1 - x, c) + enc_landed[1].astype(f32)).astype(low_type)
    enc_far = copies.start(place, enc_sent.at[2], enc_landed.at[2], "x")
    enc_total[...] = enc_term(x, c) + enc_landed[0].astype(f32)
    local.wait(con_at, out_w_at)
    g_over.wait_recv()
    loop_rows(2 * n, BLOCK, lambda r: store(grad_context, r, matmul(g_one[r], out_w[...])))

    def out_grads(t):
        part_self[t, pl.ds(0, heads_width)] = inner_rows(g_one[:, t], context[...]).astype(low_type)

    loop_cols(width, BLOCK, out_grads)
    local.wait(q_at, pair_at)
    attention_back(
        place, comm, q_one, pair_one, lambda r: lows[:, r], lambda r: highs[:, r],
        context, grad_context, lse_one, window, dk_sum, dv_sum,
    )
    local.wait(rows_one_at)
    chip_rows = pl.ds(pl.multiple_of(x * 2 * n, LANES), 2 * n)

    def self_grads(t):
        part_self[t, second] = inner_rows(rows_one[chip_rows, t], q_one[...]).astype(low_type)
        part_self[t, rest] = inner_rows(rows_one[:, t], pair_one[...]).astype(low_type)

    loop_cols(width, BLOCK, self_grads)
    comm.begin()
    enc_far.wait_recv()
    enc_total[...] += enc_landed[2].astype(f32)
    local.start(enc_total, enc_grad)
    local.wait(qkv_at)
    q_lanes, kv_lanes = pl.ds(0, heads_width), pl.ds(heads_width, 2 * heads_width)

    def key_term(xx, local_rows):
        at = pl.ds(pl.multiple_of(xx * 2 * n + local_rows.start, LANES), local_rows.size)
        return outer_cols(pair_one[at], qkv_w[:, kv_lanes])

    def query_term(local_rows):
        return outer_cols(q_one[local_rows], qkv_w[:, q_lanes])

    far_over = exchange_rows(
        place, copies, n, sent.at[1], landed.at[1], lambda r: key_term(1 - x, r)
    )
    near_over = exchange_rows(
        place, copies, n, sent.at[2], landed.at[2], lambda r: key_term(x, r) + query_term(r)
    )
    far_over.wait_recv()

    def far_part(tile, rows_here):
        sent[3, tile] = (key_term(1 - x, rows_here) + landed[1, tile].astype(f32)).astype(low_type)

    own_tiles(place, n, far_part)
    chip_over = copies.start(place, sent.at[3], landed.at[3], "x")

    def near_part(tile, rows_here):
        total[tile] = key_term(x, rows_here) + query_term(rows_here)

    own_tiles(place, n, near_part)
    comm.step()
    local.wait(tokens_at)
    near_over.wait_recv()
    chip_over.wait_recv()

    def last_part(tile, rows_here):
        incoming = total[tile] + landed[2, tile].astype(f32) + landed[3, tile].astype(f32)
        grad[tile] += norm_back_tile(small, 0, incoming, tokens[tile].astype(f32), gains[0:1])

    own_tiles(place, n, last_part)
    local.start(grad, in_grad)
    comm.begin()
    comm.drain()
    local.finish()
    copies.finish()


def back_two(lows, highs, gains, lse_one, small, hbm, rows, cols, window, enc_rows):
    grad, q_one, pair_one = hbm[7], hbm[11], hbm[12]
    n, width = grad.shape
    heads_width = q_one.shape[1]

    def sums(k):
        return wide(k, rows, cols)

    out_shape = [
        sums(1), sums(1), sums(2), sums(1), sums(3), wide(6, 8, width), wide(n, width), wide(enc_rows, width),
    ]
    n_copies = 8 * 15 + 8 + 5
    held = hbm[:6] + hbm[7:]
    return pl.pallas_call(
        functools.partial(back_two_kernel, (rows, cols), window),
        out_shape=out_shape,
        in_specs=[VMEM_SPEC] * 5 + [ANY_SPEC] * len(hbm),
        out_specs=[VMEM_SPEC] * 6 + [ANY_SPEC] * 2,
        scratch_shapes=scratch_like(held)
        + scratch_like(
            [
                low(width, 4 * heads_width), low(width, 4 * heads_width), low(8, rows * 15, cols),
                low(4, n, width), low(4, n, width), wide(n, width), low(2 * n, width),
                low(2 * n, heads_width), wide(pair_one.shape[0], PAIR), wide(pair_one.shape[0], PAIR),
                low(3, enc_rows, width), low(3, enc_rows, width), wide(enc_rows, width), wide(5, 8, width),
            ]
        )
        + [
            pltpu.SemaphoreType.DMA((n_copies,)),
            pltpu.SemaphoreType.DMA((n_copies,)),
            pltpu.SemaphoreType.DMA((len(hbm) + 2,)),
        ],
        compiler_params=pltpu.CompilerParams(
            collective_id=3, has_side_effects=True, vmem_limit_bytes=62 * MIB
        ),
        name="back_two",
    )(lows, highs, gains, lse_one, small, *hbm)


BLOCK = 256


def split_heads(values_in):
    lane = lax.broadcasted_iota(jnp.int32, values_in.shape, 1)
    zero = jnp.zeros_like(values_in)
    return jnp.concatenate(
        [jnp.where(lane < HD, values_in, zero), jnp.where(lane >= HD, values_in, zero)], axis=0
    )


def key_scores(queries, keys, lows, highs, start):
    scores = outer_cols(keys, queries)
    ids = start + lax.broadcasted_iota(jnp.int32, scores.shape, 0)
    lows = jnp.concatenate([lows, lows], axis=1)
    highs = jnp.concatenate([highs, highs], axis=1)
    return jnp.where((ids >= lows) & (ids <= highs), scores, masked_score)


def attend_step(q_block, keys, values, lows, highs, start):
    rows = q_block.shape[0]
    queries = split_heads(q_block * jnp.asarray(HD**-0.5, low_type))
    scores = key_scores(queries, keys, lows, highs, start)
    peak = jnp.max(scores, axis=0, keepdims=True)
    probs = jnp.exp(scores - peak)
    total = jnp.sum(probs, axis=0, keepdims=True)
    context = inner_rows(values, probs.astype(low_type)) / total
    pair = jnp.concatenate([context[:HD, :rows], context[HD:, rows:]], axis=0)
    return pair.T.astype(low_type), peak + jnp.log(total)


def attend_back_step(q_block, keys, values, lows, highs, start, context, grad_context, lse):
    rows = q_block.shape[0]
    queries = split_heads(q_block * jnp.asarray(HD**-0.5, low_type))
    grads = split_heads(grad_context)
    scores = key_scores(queries, keys, lows, highs, start)
    probs = jnp.exp(scores - lse)
    grad_probs = outer_cols(values, grads)
    product = (grad_context.astype(f32) * context.astype(f32)).T
    inner = jnp.concatenate(
        [
            jnp.sum(product[:HD], axis=0, keepdims=True),
            jnp.sum(product[HD:], axis=0, keepdims=True),
        ],
        axis=1,
    )
    grad_scores = (probs * (grad_probs - inner)).astype(low_type)
    dv = matmul(probs.astype(low_type), grads)
    dk = matmul(grad_scores, queries)
    grad_queries = inner_rows(keys, grad_scores) * HD**-0.5
    pair = jnp.concatenate([grad_queries[:HD, :rows], grad_queries[HD:, rows:]], axis=0)
    return pair.T.astype(low_type), dk, dv


def width_orders(outer, width):
    def spread(values_in):
        if outer == 1:
            return values_in
        parts = values_in.reshape(values_in.shape[:-1] + (outer, RING * 2, -1))
        return jnp.swapaxes(parts, -3, -2).reshape(values_in.shape)

    def back(values_in):
        if outer == 1:
            return values_in
        parts = values_in.reshape(values_in.shape[:-1] + (RING * 2, outer, -1))
        return jnp.swapaxes(parts, -3, -2).reshape(values_in.shape)

    return spread, back


def on_device(
    tokens,
    encoder,
    seg_ids,
    enc_lens,
    attn_qkv,
    attn_out,
    cross_q,
    cross_kv,
    cross_out,
    ffn_in,
    ffn_out,
    norm_gains,
    norm_biases,
    out_grad,
):
    outer = lax.axis_size("o")
    spread, gathered_back = width_orders(outer, tokens.shape[1])
    tokens, encoder, out_grad = spread(tokens), spread(encoder[0]), spread(out_grad)
    norm_gains, norm_biases = spread(norm_gains), spread(norm_biases)
    chip = lax.axis_index("x")
    own = tokens.shape[0]
    half = 2 * own
    segment = seg_ids[0]
    seq_len = segment.shape[0]
    cols = cross_q.shape[1]
    width = tokens.shape[1]

    def units(block):
        k = block.shape[-1] // cols
        return block.reshape(block.shape[0], k, cols).transpose(1, 0, 2)

    shards = [
        attn_qkv.astype(low_type),
        attn_out.astype(low_type).T[None],
        cross_q.astype(low_type)[None],
        cross_kv.astype(low_type),
        cross_out.astype(low_type).T[None],
        units(ffn_in.astype(low_type)),
        units(ffn_out.astype(low_type).T),
    ]
    if outer > 1:
        shards = [lax.all_gather(s, "o", axis=1, tiled=True) for s in shards]
    rows = shards[0].shape[1]

    residual = tokens.astype(f32)
    normed = norm_rows(residual, norm_gains[0], norm_biases[0])
    rows_one, qkv_w, out_w = gather_first(normed.astype(low_type), shards[:2])

    heads_width = 2 * cols

    first = chip * half
    here = lax.dynamic_slice_in_dim(segment, first, half, 0)
    lows = jnp.sum((segment[None, :] < here[:, None]).astype(jnp.int32), axis=1)[None]
    highs = (first + jnp.arange(half, dtype=jnp.int32))[None]
    enc_highs = jnp.broadcast_to(enc_lens[0] - 1, highs.shape)
    window = min(seq_len, seq_len // 2 + BLOCK)

    chip_rows = lax.dynamic_slice_in_dim(rows_one, first, half, 0)
    queries_one = matmul(chip_rows, qkv_w[:, :heads_width]).astype(low_type)
    pair_one = matmul(rows_one, qkv_w[:, heads_width:]).astype(low_type)
    (
        query_w, pair_w, back_w, up_w, down_w, grads_three, enc_full, context_one, lse_one, residual_one,
        rows_two, queries_two, pair_two, context_two, lse_two, residual_two, rows_three, active, slope,
    ) = forward(
        queries_one, pair_one, out_w, lows, highs, enc_highs, norm_gains, norm_biases, residual,
        out_grad, encoder, shards[2:], window,
    )
    down_sum, up_sum, small, out_tokens, grad_two, back_grad, grad_queries, grad_pair = back_one(
        enc_highs, norm_gains, lse_two, down_w, up_w, active, slope, grads_three, rows_three, residual_two,
        queries_two, pair_two, context_two, back_w, rows, cols,
    )
    back_sum, query_sum, pair_sum, out_sum, qkv_sum, small, in_grad, enc_grad = back_two(
        lows, highs, norm_gains, lse_one, small,
        [
            grad_queries, grad_pair, rows_two, enc_full, query_w, pair_w, back_grad, grad_two, residual_one,
            context_one, out_w, queries_one, pair_one, rows_one, qkv_w, tokens,
        ],
        rows, cols, window, encoder.shape[0],
    )
    enc_grad = enc_grad[None]
    sums = [up_sum, down_sum, back_sum, query_sum, pair_sum, out_sum, qkv_sum]
    small = small[-1]
    if outer > 1:
        small = lax.psum(small, "o")
        sums = [lax.psum_scatter(s, "o", scatter_dimension=1, tiled=True) for s in sums]
    up_sum, down_sum, back_sum, query_sum, pair_sum, out_sum, qkv_sum = sums

    def joined(block):
        return block.transpose(1, 0, 2).reshape(block.shape[1], -1)

    return (
        gathered_back(out_tokens),
        gathered_back(in_grad),
        gathered_back(enc_grad),
        qkv_sum,
        out_sum[0].T,
        query_sum[0],
        pair_sum,
        back_sum[0].T,
        joined(up_sum),
        joined(down_sum).T,
        gathered_back(small[:3]),
        gathered_back(small[3:6]),
    )


def solution(mesh):
    count, tensor = mesh.devices.shape
    outer = count // (RING * 2)
    fine = Mesh(
        mesh.devices.reshape(outer, RING, 2, tensor // 2, 2), ("o", "z", "y", "x", "c")
    )
    dp, tp = ("o", "z", "y"), ("x", "c")
    in_specs = (
        P(dp + tp, None),
        P(dp, tp, None),
        P(dp, None),
        P(dp),
        P(None, dp, tp),
        P(tp, dp),
        P(dp, tp),
        P(None, dp, tp),
        P(tp, dp),
        P(dp, tp),
        P(tp, dp),
        P(),
        P(),
        P(dp + tp, None),
    )
    out_specs = (
        P(dp + tp, None),
        P(dp + tp, None),
        P(dp, tp, None),
        P(None, dp, tp),
        P(tp, dp),
        P(dp, tp),
        P(None, dp, tp),
        P(tp, dp),
        P(dp, tp),
        P(tp, dp),
        P(),
        P(),
    )
    return jax.shard_map(
        on_device, mesh=fine, in_specs=in_specs, out_specs=out_specs, check_vma=False
    )
```

```python
import functools

import jax
import jax.numpy as jnp
from jax import lax
from jax.experimental import pallas as pl
from jax.experimental.pallas import tpu as pltpu
from jax.sharding import Mesh
from jax.sharding import PartitionSpec as P

HD = 64
DOCS = 4
LANES = 128
PAIR = 2 * HD
RING = 4
epsilon = 1e-05
masked_score = -1e30
MESH = pl.DeviceIdType.MESH
low_type = jnp.bfloat16
f32 = jnp.float32
MIB = 1 << 20


def matmul(left, right):
    return jnp.dot(left, right, preferred_element_type=f32)


def inner_rows(left, right):
    return lax.dot_general(left, right, (((0,), (0,)), ((), ())), preferred_element_type=f32)


def outer_cols(left, right):
    return lax.dot_general(left, right, (((1,), (1,)), ((), ())), preferred_element_type=f32)


def norm_forward(values_in, gain_row, bias_row):
    average = jnp.mean(values_in, axis=-1, keepdims=True)
    centred = values_in - average
    inverse = lax.rsqrt(jnp.mean(centred * centred, axis=-1, keepdims=True) + epsilon)
    unit_rows = centred * inverse
    return (unit_rows * gain_row + bias_row, unit_rows, inverse)


def norm_backward(incoming, unit_rows, inverse, gain_row):
    scaled = incoming * gain_row
    first_mean = jnp.mean(scaled, axis=-1, keepdims=True)
    second_mean = jnp.mean(scaled * unit_rows, axis=-1, keepdims=True)
    result = inverse * (scaled - first_mean - unit_rows * second_mean)
    return (result, jnp.sum(incoming * unit_rows, axis=0), jnp.sum(incoming, axis=0))


class Place:
    def __init__(self):
        self.z = lax.axis_index("z")
        self.y = lax.axis_index("y")
        self.x = lax.axis_index("x")
        self.c = lax.axis_index("c")

    def to(self, which):
        if which == "x":
            return {"x": 1 - self.x}
        if which == "y":
            return {"y": 1 - self.y}
        if which == "c":
            return {"c": 1 - self.c}
        if which == "z1":
            return {"z": self.z + 1 - 2 * lax.rem(self.z, 2)}
        if which == "z2":
            return {"z": lax.rem(self.z + 2, RING)}
        if which == "down":
            return {"z": lax.rem(self.z + RING - 1, RING)}
        return {"z": lax.rem(self.z + 1, RING)}

    def ring(self, step):
        return lax.rem(self.z + step, RING)


def greet(place, names):
    barrier = pltpu.get_barrier_semaphore()
    for name in names:
        pl.semaphore_signal(barrier, inc=1, device_id=place.to(name), device_id_type=MESH)
    pl.semaphore_wait(barrier, len(names))


class Copies:
    def __init__(self, send_sems, recv_sems):
        self.send_sems, self.recv_sems = send_sems, recv_sems
        self.made = []

    def start(self, place, src, dst, which):
        at = len(self.made)
        copy = pltpu.make_async_remote_copy(
            src_ref=src,
            dst_ref=dst,
            send_sem=self.send_sems.at[at],
            recv_sem=self.recv_sems.at[at],
            device_id=place.to(which),
            device_id_type=MESH,
        )
        copy.start()
        self.made.append(copy)
        return copy

    def finish(self):
        for copy in self.made:
            copy.wait_send()


GATHER_ORDERS = ("xzy", "yzx", "zyx", "zxy")


def gather_unit(order, place, whole, base, rows, cols, copies):
    x, y = place.x, place.y

    def at(step, both_y, both_x):
        first = place.ring(step) * 2
        row = first * rows if both_y else (first + y) * rows
        col = base if both_x else base + x * cols
        return whole.at[
            pl.ds(pl.multiple_of(row, rows), rows * (2 if both_y else 1)),
            pl.ds(pl.multiple_of(col, LANES), cols * (2 if both_x else 1)),
        ]

    def send(where, which):
        return copies.start(place, where, where, which)

    mine = at(0, False, False)
    if order in ("xzy", "yzx"):
        axis, last = order[0], order[2]
        wide = dict(both_y=axis == "y", both_x=axis == "x")
        first = send(mine, axis)
        yield
        first.wait_recv()
        hop = send(at(0, **wide), "down")
        ends = [send(at(0, **wide), last)]
        yield
        for step in range(1, RING):
            hop.wait_recv()
            if step < RING - 1:
                hop = send(at(step, **wide), "down")
            ends.append(send(at(step, **wide), last))
            yield
        for copy in ends:
            copy.wait_recv()
    else:
        mid, last = order[1], order[2]
        wide = dict(both_y=mid == "y", both_x=mid == "x")
        hop = send(mine, "down")
        mids = [send(mine, mid)]
        ends = []
        yield
        for step in range(1, RING + 1):
            if step < RING:
                hop.wait_recv()
                if step < RING - 1:
                    hop = send(at(step, False, False), "down")
                mids.append(send(at(step, False, False), mid))
            mids[step - 1].wait_recv()
            ends.append(send(at(step - 1, **wide), last))
            yield
        for copy in ends:
            copy.wait_recv()


class Levels:
    def __init__(self, groups, spacing=None):
        self.live = [list(g) for g in groups]
        self.spacing = spacing
        self.level = 0
        self.started = 0

    def begin(self):
        self.started += 1
        self.step()

    def step(self):
        if self.spacing and self.started < len(self.live) and self.level % self.spacing == 0:
            self.started += 1
        for group in self.live[: self.started]:
            for unit in list(group):
                try:
                    next(unit)
                except StopIteration:
                    group.remove(unit)
        self.level += 1

    def until(self, group):
        while self.live[group]:
            self.step()

    def drain(self):
        for group in range(len(self.live)):
            self.until(group)


class Paced:
    def __init__(self, groups, pace):
        self.groups, self.pace = [list(g) for g in groups], pace
        self.live, self.budget = [], 0.0

    def advance(self):
        unit = self.live.pop(0)
        try:
            next(unit)
            self.live.append(unit)
        except StopIteration:
            pass

    def begin(self):
        for unit in self.groups.pop(0):
            next(unit)
            self.live.append(unit)

    def spend(self, time):
        self.budget += time
        while self.budget >= self.pace:
            self.budget -= self.pace
            if self.live:
                self.advance()

    def drain(self):
        while self.live:
            self.advance()


PACE = 2.3


class Locals:
    def __init__(self, sems):
        self.sems, self.made = sems, []

    def start(self, src, dst):
        copy = pltpu.make_async_copy(src, dst, self.sems.at[len(self.made)])
        copy.start()
        self.made.append(copy)
        return len(self.made) - 1

    def wait(self, *which):
        for at in which:
            if self.made[at] is not None:
                self.made[at].wait()
                self.made[at] = None

    def finish(self):
        self.wait(*range(len(self.made)))


def own_block(place, whole, base, rows, cols):
    return whole.at[
        pl.ds(pl.multiple_of((place.z * 2 + place.y) * rows, rows), rows),
        pl.ds(pl.multiple_of(base + place.x * cols, LANES), cols),
    ]


def gather_groups(place, sizes, whole, copies, orders):
    rows, cols, units_of = sizes
    units = [
        gather_unit(order, place, whole[which], unit * 2 * cols, rows, cols, copies)
        for (which, unit), order in zip(
            ((w, u) for w, count in enumerate(units_of) for u in range(count)), orders, strict=True
        )
    ]
    return [units[k : k + 4] for k in range(0, len(units), 4)]


def place_own(place, sizes, which, master, whole):
    rows, cols, units_of = sizes
    for unit in range(units_of[which]):
        if len(master.shape) == 3:
            block = master[unit]
        elif master.shape[0] == rows:
            block = master[:, unit * cols : (unit + 1) * cols]
        else:
            block = master[unit * cols : (unit + 1) * cols].T
        own_block(place, whole, unit * 2 * cols, rows, cols)[...] = block.astype(low_type)


ANY_SPEC = pl.BlockSpec(memory_space=pl.ANY)
VMEM_SPEC = pl.BlockSpec(memory_space=pltpu.VMEM)


def norm_rows(values_in, gain_row, bias_row):
    return norm_forward(values_in, gain_row, bias_row)[0]


def loop_rows(count, tile, body):
    @pl.loop(0, count // tile)
    def _(i):
        body(pl.ds(pl.multiple_of(i * tile, tile), tile))


def exchange_rows(place, copies, n, sent, landed, make):
    theirs = pl.ds(pl.multiple_of((1 - place.c) * n, LANES), n)
    sent[...] = make(theirs).astype(low_type)
    return copies.start(place, sent, landed, "c")


def own_tiles(place, n, body):
    @pl.loop(0, n // LANES)
    def _(i):
        tile = pl.ds(pl.multiple_of(i * LANES, LANES), LANES)
        body(tile, pl.ds(pl.multiple_of(place.c * n + i * LANES, LANES), LANES))


def blocks_of(place, rows_count, pair_count, span):
    def at(block):
        rows = pl.ds(pl.multiple_of(block * BLOCK, BLOCK), BLOCK)
        if span == pair_count:
            return rows, 0
        ends = (place.x * (rows_count // BLOCK) + block + 1) * BLOCK
        return rows, pl.multiple_of(jnp.maximum(ends - span, 0), BLOCK)

    return at


def fill_biases(place, bias, segment, span):
    count = segment.shape[1]
    ids = segment[...].astype(f32)
    half = count // 2
    for block in range(bias.shape[0]):
        first = place.x * half + block * BLOCK
        mine = segment[:, pl.ds(pl.multiple_of(first, BLOCK), BLOCK)].astype(f32)
        lows = jnp.zeros(mine.shape, f32)
        for doc in range(DOCS - 1):
            size = jnp.sum(jnp.where(ids == doc, 1.0, 0.0), axis=1, keepdims=True)
            lows += jnp.where(mine > doc, size, 0.0)
        start = jnp.maximum(first + BLOCK - span, 0)
        keys = lax.broadcasted_iota(jnp.int32, bias.shape[1:], 0)
        rows = first - start + lax.broadcasted_iota(jnp.int32, bias.shape[1:], 1)
        seen = (keys.astype(f32) >= lows - start.astype(f32)) & (keys <= rows)
        bias[block] = jnp.where(seen, 0.0, masked_score)


def fill_enc_bias(bias, length):
    keys = lax.broadcasted_iota(jnp.int32, bias.shape, 0)
    bias[...] = jnp.where(keys < length, 0.0, masked_score)


def forward_kernel(sizes, window, n_out, *refs):
    n_weights = len(sizes[2])
    segment, gains, biases, enc_length, tokens_in, g_own, enc_own, *master_in = refs[: 7 + n_weights]
    at = 7 + n_weights
    g_all, *outs = refs[at : at + n_out]
    at += n_out
    held = refs[at : at + n_out - 1]
    at += n_out - 1
    masters = refs[at : at + n_weights]
    tokens, sent, landed, bias_one, bias_two, send_sems, recv_sems, local_sems = refs[at + n_weights :]
    whole = held[:n_weights]
    (
        rows_one, enc_all, q_one, pair_one, context_one, lse_one, residual_one, rows_two, q_two, pair_two,
        context_two, lse_two, residual_two, rows_three, active, slope,
    ) = held[n_weights:]
    qkv_w, out_w, query_w, pair_w, back_w, up_w, _ = whole
    place = Place()
    copies = Copies(send_sems, recv_sems)
    local = Locals(local_sems)
    x, c = place.x, place.c
    n, e = tokens.shape[0], enc_own.shape[0]
    heads_width = q_one.shape[1]
    mine = pl.ds(pl.multiple_of(c * n, 16), n)
    tokens_at = local.start(tokens_in, tokens)
    masters_at = [local.start(src, dst) for src, dst in zip(master_in, masters)]

    def flush(*names):
        for ref in names:
            local.start(ref, outs[[h is ref for h in held].index(True)])

    def part_of(ref, xx, cc, size):
        return ref.at[pl.ds(pl.multiple_of((xx * 2 + cc) * size, 16), size)]

    enc_at = local.start(enc_own, part_of(enc_all, x, c, e))
    local.start(g_own, g_all.at[mine])
    greet(place, ("x", "y", "c", "down", "up"))
    local.wait(tokens_at)
    h_own = part_of(rows_one, x, c, n)

    @pl.loop(0, n // LANES)
    def _(i):
        tile = pl.ds(pl.multiple_of(i * LANES, LANES), LANES)
        normed = norm_rows(tokens[tile].astype(f32), gains[0:1], biases[0:1])
        rows_one[pl.ds(pl.multiple_of((x * 2 + c) * n + i * LANES, LANES), LANES)] = normed.astype(low_type)

    hx = copies.start(place, h_own, h_own, "x")
    hc = copies.start(place, h_own, h_own, "c")
    orders = ("xzy", "zxy", "yzx", "xzy", "xzy", "yzx", "xzy", "zxy") + GATHER_ORDERS * 2
    groups = gather_groups(place, sizes, whole, copies, orders)

    def rows_unit(own_x, own_c, ref, size, also):
        yield
        yield
        own_x.wait_recv()
        far = part_of(ref, 1 - x, c, size)
        over = copies.start(place, far, far, "c")
        yield
        yield
        for copy in (own_c, over, *also):
            copy.wait_recv()

    groups[0].append(rows_unit(hx, hc, rows_one, n, ()))
    for which in range(n_weights):
        local.wait(masters_at[which])
        place_own(place, sizes, which, masters[which], whole[which])
        if which == 1:
            comm = Levels(groups, 4)
            comm.step()
    local.wait(enc_at)
    e_own = part_of(enc_all, x, c, e)
    ex = copies.start(place, e_own, e_own, "x")
    ec = copies.start(place, e_own, e_own, "c")
    gc = copies.start(place, g_own, g_all.at[mine], "c")
    groups_late = rows_unit(ex, ec, enc_all, e, (gc,))
    comm.live[1].append(groups_late)
    fill_biases(place, bias_one, segment, window)
    fill_enc_bias(bias_two, enc_length[0])

    def attention(q_ref, pair_ref, bias_of, o_ref, lse_ref, span):
        block_at = blocks_of(place, q_ref.shape[0], pair_ref.shape[0], span)
        for pair in range(heads_width // PAIR):
            comm.step()
            lanes = pl.ds(pair * PAIR, PAIR)
            value_lanes = pl.ds(heads_width + pair * PAIR, PAIR)

            @pl.loop(0, q_ref.shape[0] // BLOCK)
            def _(block):
                rows, start = block_at(block)
                here = pl.ds(start, span)
                o_ref[rows, lanes], lse_ref[pair, block] = attend_step(
                    q_ref[rows, lanes],
                    pair_ref[here, lanes],
                    pair_ref[here, value_lanes],
                    bias_of(block),
                )

    def branch(at, context, weight, before, after, gain_at, rows_ref):
        over = exchange_rows(
            place, copies, n, sent.at[at], landed.at[at],
            lambda rows: outer_cols(context[rows], weight[...]),
        )

        after[...] = before[...].astype(f32) + outer_cols(context[mine], weight[...])
        over.wait_recv()

        def rest(tile, rows):
            total = after[tile] + landed[at, tile].astype(f32)
            after[tile] = total
            rows_ref[rows] = norm_rows(
                total, gains[gain_at : gain_at + 1], biases[gain_at : gain_at + 1]
            ).astype(low_type)

        own_tiles(place, n, rest)
        return copies.start(place, rows_ref.at[mine], rows_ref.at[mine], "c")

    comm.until(0)
    flush(rows_one, qkv_w, out_w)

    def project(rows):
        first = pl.ds(pl.multiple_of(x * 2 * n + rows.start, BLOCK), rows.size)
        q_one[rows] = matmul(rows_one[first], qkv_w[:, :heads_width]).astype(low_type)

    loop_rows(2 * n, BLOCK, project)
    loop_rows(
        4 * n, BLOCK, lambda r: store(pair_one, r, matmul(rows_one[r], qkv_w[:, heads_width:]))
    )
    flush(q_one, pair_one)
    attention(q_one, pair_one, lambda block: bias_one[block], context_one, lse_one, window)
    comm.step()
    over = branch(0, context_one, out_w, tokens, residual_one, 1, rows_two)
    flush(context_one, lse_one, residual_one)
    comm.until(1)
    loop_rows(
        enc_all.shape[0], BLOCK, lambda r: store(pair_two, r, matmul(enc_all[r], pair_w[...]))
    )
    flush(query_w, pair_w, back_w, enc_all, pair_two)
    over.wait_recv()
    comm.step()
    loop_rows(2 * n, BLOCK, lambda r: store(q_two, r, matmul(rows_two[r], query_w[...])))
    flush(rows_two, q_two)
    attention(
        q_two, pair_two, lambda block: bias_two[...], context_two, lse_two, enc_all.shape[0]
    )
    comm.step()
    over = branch(1, context_two, back_w, residual_one, residual_two, 2, rows_three)
    flush(context_two, lse_two, residual_two)
    comm.until(2)
    over.wait_recv()
    flush(rows_three, up_w)

    def up(rows):
        inner = matmul(rows_three[rows], up_w[...])
        gate = 1.0 / (1.0 + jnp.exp(-inner))
        active[rows] = (inner * gate).astype(low_type)
        slope[rows] = (gate * (1.0 + inner * (1.0 - gate))).astype(low_type)

    loop_rows(2 * n, BLOCK, up)
    flush(active, slope)
    comm.drain()
    flush(whole[-1])
    local.finish()
    copies.finish()


def store(ref, rows, values_in):
    ref[rows] = values_in.astype(ref.dtype)


def low(*shape):
    return jax.ShapeDtypeStruct(shape, low_type)


def wide(*shape):
    return jax.ShapeDtypeStruct(shape, f32)


def scratch_like(shapes):
    return [pltpu.VMEM(s.shape, s.dtype) for s in shapes]


def forward(segment, gains, biases, enc_lens, tokens, g_own, enc_own, masters, sizes, window):
    rows, cols, units_of = sizes
    n, width = tokens.shape
    e = enc_own.shape[0]
    hidden = 2 * cols * units_of[-1]
    heads_width = 2 * cols
    n_units = sum(units_of)
    n_copies = 11 + n_units * 11
    lse = wide(heads_width // PAIR, 2 * n // BLOCK, 1, 2 * BLOCK)
    held = [low(width, 2 * cols * k) for k in units_of] + [
        low(4 * n, width), low(4 * e, width),
        low(2 * n, heads_width), low(4 * n, 2 * heads_width), low(2 * n, heads_width), lse, wide(n, width),
        low(2 * n, width), low(2 * n, heads_width), low(4 * e, 2 * heads_width), low(2 * n, heads_width), lse,
        wide(n, width), low(2 * n, width), low(2 * n, hidden), low(2 * n, hidden),
    ]
    out_shape = [low(2 * n, width)] + held
    return pl.pallas_call(
        functools.partial(forward_kernel, sizes, window, len(out_shape)),
        out_shape=out_shape,
        in_specs=[VMEM_SPEC] * 3
        + [pl.BlockSpec(memory_space=pltpu.SMEM)]
        + [ANY_SPEC] * (3 + len(masters)),
        out_specs=[ANY_SPEC] * len(out_shape),
        scratch_shapes=scratch_like(held + masters + [tokens])
        + scratch_like([low(2, n, width)] * 2)
        + scratch_like([wide(2 * n // BLOCK, window, BLOCK), wide(4 * e, BLOCK)])
        + [
            pltpu.SemaphoreType.DMA((n_copies,)),
            pltpu.SemaphoreType.DMA((n_copies,)),
            pltpu.SemaphoreType.DMA((3 + len(masters) + len(held),)),
        ],
        compiler_params=pltpu.CompilerParams(
            collective_id=2, has_side_effects=True, vmem_limit_bytes=62 * MIB
        ),
        name="forward",
    )(segment, gains, biases, enc_lens, tokens, g_own, enc_own, *masters)


REDUCE_ORDERS = ("xyz", "xzy", "yxz", "yzx")
CHUNK_ORDER = tuple(range(1, RING)) + (0,)


def reduce_unit(order, place, part, base, rows, cols, recv, out, copies):
    x, y = place.x, place.y

    def at(step, row_of, col_of):
        first = place.ring(step) * 2
        row = first * rows if row_of is None else (first + row_of) * rows
        col = base if col_of is None else base + col_of * cols
        return part.at[
            pl.ds(pl.multiple_of(row, rows), rows * (2 if row_of is None else 1)),
            pl.ds(pl.multiple_of(col, LANES), cols * (2 if col_of is None else 1)),
        ]

    used = [0]

    def landing(shape):
        height = shape[0] * (shape[1] // cols)
        where = [
            recv.at[pl.ds(used[0] + k * shape[0], shape[0])] for k in range(shape[1] // cols)
        ]
        used[0] += height
        return where

    def add(target, source):
        target[...] = target[...] + source[...]

    def exchange(step, which, mid):
        sent = []
        if which == "x":
            if mid:
                spots = [(at(step, y, 1 - x), at(step, y, x))]
            else:
                spots = [(at(step, None, 1 - x), at(step, None, x))]
        else:
            if mid:
                spots = [(at(step, 1 - y, x), at(step, y, x))]
            else:
                spots = [(at(step, 1 - y, k), at(step, y, k)) for k in range(2)]
        for src, keep_at in spots:
            (land,) = landing((src.shape[0], cols))
            sent.append((copies.start(place, src, land, which), keep_at, land))
        return sent

    def take(sent):
        for copy, keep_at, land in sent:
            copy.wait_recv()
            add(keep_at, land)

    def ring_hop(step, spots, ready, arrived):
        if step in ready:
            take(ready[step])
        for (copy, land), spot in zip(arrived or [], spots):
            copy.wait_recv()
            add(spot, land)
        sent = []
        if step != 0:
            for spot in spots:
                (land,) = landing((spot.shape[0], cols))
                sent.append((copies.start(place, spot, land, "down"), land))
        return sent

    first, middle, last = order
    outer, inner = {}, {}
    for step in CHUNK_ORDER[:2]:
        outer[step] = exchange(step, first, False)
    yield
    hop = None
    for k, step in enumerate(CHUNK_ORDER):
        take(outer[step])
        if k + 2 < RING:
            outer[CHUNK_ORDER[k + 2]] = exchange(CHUNK_ORDER[k + 2], first, False)
        if last == "z":
            inner[step] = exchange(step, middle, True)
            if k > 0:
                hop = ring_hop(CHUNK_ORDER[k - 1], [at(CHUNK_ORDER[k - 1], y, x)], inner, hop)
        else:
            if first == "x":
                spots = [at(step, None, x)]
            else:
                spots = [at(step, y, half) for half in range(2)]
            hop = ring_hop(step, spots, {}, hop)
        yield
    if last == "z":
        take(inner[0])
        ((copy, land),) = hop
    else:
        src = at(0, 1 - y, x) if last == "y" else at(0, y, 1 - x)
        (land,) = landing((rows, cols))
        copy = copies.start(place, src, land, last)
        yield
    copy.wait_recv()
    out[...] = at(0, y, x)[...].astype(f32) + land[...].astype(f32)


def reduce_group(place, rows, cols, part, recv, outs, copies, first, orders):
    return [
        reduce_unit(
            order, place, part, unit * 2 * cols, rows, cols, recv.at[first + unit], outs[unit], copies
        )
        for unit, order in enumerate(orders)
    ]


def attention_back(place, comm, q_ref, pair_ref, bias_of, o_ref, do_ref, lse_ref, span, dk_sum, dv_sum):
    heads_width = q_ref.shape[1]
    block_at = blocks_of(place, q_ref.shape[0], pair_ref.shape[0], span)
    for pair in range(heads_width // PAIR):
        lanes = pl.ds(pair * PAIR, PAIR)
        value_lanes = pl.ds(heads_width + pair * PAIR, PAIR)
        dk_sum[...] = jnp.zeros_like(dk_sum)
        dv_sum[...] = jnp.zeros_like(dv_sum)

        @pl.loop(0, q_ref.shape[0] // BLOCK)
        def _(block):
            rows, start = block_at(block)
            here = pl.ds(start, span)
            dq, dk, dv = attend_back_step(
                q_ref[rows, lanes],
                pair_ref[here, lanes],
                pair_ref[here, value_lanes],
                bias_of(block),
                o_ref[rows, lanes],
                do_ref[rows, lanes],
                lse_ref[pair, block],
            )
            q_ref[rows, lanes] = dq
            dk_sum[here] += dk
            dv_sum[here] += dv

        pair_ref[:, lanes] = dk_sum[...].astype(low_type)
        pair_ref[:, value_lanes] = dv_sum[...].astype(low_type)
        comm.spend(6.0)


def loop_cols(count, tile, body):
    loop_rows(count, tile, body)


def norm_back_tile(small, at, incoming, before, gain_row):
    _, unit_rows, inverse = norm_forward(before, jnp.ones_like(gain_row), jnp.zeros_like(gain_row))
    result, gain_sum, bias_sum = norm_backward(incoming, unit_rows, inverse, gain_row)
    small[at : at + 1] += gain_sum[None]
    small[at + 3 : at + 4] += bias_sum[None]
    return result


def back_one_kernel(sizes, *refs):
    rows, cols = sizes
    (
        enc_length, gains, lse_two,
        down_in, up_in, active_in, slope_in, g_in, rows_in, residual_in, q_in, pair_in, context_in, back_in,
        down_sum, up_sum, small, out_tokens, grad_out, back_out, dq_out, dpair_out, late_out,
        down_w, up_w, active, slope, g_all, rows_three, residual, q_two, pair_two, context, back_w,
        part_down, part_up, recv, sent, landed, grad, g_two, back_part, grad_context, tokens_out, dk_sum, dv_sum,
        bias, send_sems, recv_sems, local_sems,
    ) = refs
    place = Place()
    copies = Copies(send_sems, recv_sems)
    local = Locals(local_sems)
    c = place.c
    g_at, active_at, down_at, slope_at, rows_at, up_at, res_at, con_at, back_at, q_at, pair_at = [
        local.start(src, dst)
        for src, dst in (
            (g_in, g_all), (active_in, active), (down_in, down_w), (slope_in, slope), (rows_in, rows_three),
            (up_in, up_w), (residual_in, residual), (context_in, context), (back_in, back_w),
            (q_in, q_two), (pair_in, pair_two),
        )
    ]
    greet(place, ("x", "y", "c", "down", "up"))
    n, width = residual.shape
    mine = pl.ds(pl.multiple_of(c * n, 16), n)
    comm = Paced(
        [
            reduce_group(
                place, rows, cols, part_down, recv, [down_sum.at[k] for k in range(4)], copies, 0,
                REDUCE_ORDERS,
            ),
            reduce_group(
                place, rows, cols, part_up, recv, [up_sum.at[k] for k in range(2)], copies, 4, ("xzy", "yxz")
            ),
        ],
        PACE,
    )
    small[...] = jnp.zeros_like(small)
    fill_enc_bias(bias, enc_length[0])
    local.wait(g_at, active_at)
    loop_cols(width, BLOCK, lambda t: store(part_down, t, inner_rows(g_all[:, t], active[...])))
    comm.begin()
    local.wait(down_at, slope_at)

    def inner(tile):
        slope[tile] = (matmul(g_all[tile], down_w[...]) * slope[tile].astype(f32)).astype(low_type)

    loop_rows(2 * n, BLOCK, inner)
    comm.spend(4.5)
    local.wait(rows_at)
    loop_cols(width, BLOCK, lambda t: store(part_up, t, inner_rows(rows_three[:, t], slope[...])))
    comm.spend(4.8)
    comm.begin()
    local.start(part_up.at[:, pl.ds(4 * cols, 4 * cols)], late_out)
    local.wait(up_at)
    over = exchange_rows(
        place, copies, n, sent.at[0], landed.at[0], lambda r: outer_cols(slope[r], up_w[...])
    )
    comm.spend(2.4)
    grad[...] = outer_cols(slope[mine], up_w[...])
    comm.spend(2.4)
    out_over = exchange_rows(
        place, copies, n, sent.at[1], landed.at[1], lambda r: outer_cols(active[r], down_w[...])
    )
    local.wait(res_at)
    over.wait_recv()

    def norm_part(tile, rows_here):
        incoming = grad[tile] + landed[0, tile].astype(f32)
        total = g_all[rows_here].astype(f32) + norm_back_tile(
            small, 2, incoming, residual[tile], gains[2:3]
        )
        grad[tile] = total
        g_two[rows_here] = total.astype(low_type)

    own_tiles(place, n, norm_part)
    g_over = copies.start(place, g_two.at[mine], g_two.at[mine], "c")
    local.start(grad, grad_out)
    comm.spend(5.5)
    out_over.wait_recv()
    out_own = residual[...] + outer_cols(active[mine], down_w[...])
    tokens_out[...] = (out_own + landed[1].astype(f32)).astype(low_type)
    local.start(tokens_out, out_tokens)
    comm.spend(2.5)
    local.wait(con_at, back_at)
    g_over.wait_recv()
    loop_rows(2 * n, BLOCK, lambda r: store(grad_context, r, matmul(g_two[r], back_w[...])))
    loop_cols(width, BLOCK, lambda t: store(back_part, t, inner_rows(g_two[:, t], context[...])))
    local.start(back_part, back_out)
    comm.spend(3.0)
    local.wait(q_at, pair_at)
    attention_back(
        place, comm, q_two, pair_two, lambda block: bias[...], context, grad_context, lse_two, pair_two.shape[0], dk_sum, dv_sum,
    )
    local.start(q_two, dq_out)
    local.start(pair_two, dpair_out)
    comm.drain()
    local.finish()
    copies.finish()


def back_one(enc_lens, gains, lse_two, down_w, up_w, active, slope, g_all, rows_three, residual, q_two, pair_two, context, back_w, rows, cols):
    n, width = residual.shape
    heads_width = q_two.shape[1]
    hbm = [down_w, up_w, active, slope, g_all, rows_three, residual, q_two, pair_two, context, back_w]
    out_shape = [
        wide(4, rows, cols), wide(2, rows, cols), wide(8, width), low(n, width), wide(n, width),
        low(width, heads_width), low(2 * n, heads_width), low(*pair_two.shape), low(width, 4 * cols),
    ]
    n_copies = 6 * 15 + 3
    return pl.pallas_call(
        functools.partial(back_one_kernel, (rows, cols)),
        out_shape=out_shape,
        in_specs=[pl.BlockSpec(memory_space=pltpu.SMEM)] + [VMEM_SPEC] * 2 + [ANY_SPEC] * len(hbm),
        out_specs=[VMEM_SPEC] * 3 + [ANY_SPEC] * 6,
        scratch_shapes=scratch_like(hbm)
        + scratch_like(
            [
                low(*down_w.shape), low(*up_w.shape), low(6, rows * 15, cols), low(2, n, width),
                low(2, n, width), wide(n, width), low(2 * n, width), low(width, heads_width),
                low(2 * n, heads_width), low(n, width), wide(pair_two.shape[0], PAIR), wide(pair_two.shape[0], PAIR),
                wide(pair_two.shape[0], BLOCK),
            ]
        )
        + [
            pltpu.SemaphoreType.DMA((n_copies,)),
            pltpu.SemaphoreType.DMA((n_copies,)),
            pltpu.SemaphoreType.DMA((len(hbm) + 6,)),
        ],
        compiler_params=pltpu.CompilerParams(
            collective_id=1, has_side_effects=True, vmem_limit_bytes=60 * MIB
        ),
        name="back_one",
    )(enc_lens, gains, lse_two, *hbm)


def back_two_kernel(sizes, window, *refs):
    rows, cols = sizes
    (
        segment, gains, lse_one, small_in,
        dq_in, dpair_in, rows_two_in, enc_in, query_in, pair_w_in, back_in, grad_in, residual_in, context_in,
        out_w_in, q_in, pair_in, rows_one_in, qkv_in, tokens_in, late_in,
        late_sum, back_sum, query_sum, pair_sum, out_sum, qkv_sum, small_out, in_grad, enc_grad,
        dq_two, dpair_two, grad, residual, context, out_w, q_one, pair_one, tokens,
        rows_held, qkv_w, part_late, part_cross, part_self, recv, sent, landed, total, g_one, grad_context, dk_sum, dv_sum,
        enc_sent, enc_landed, enc_total, small_recv, bias, send_sems, recv_sems, local_sems,
    ) = refs
    place = Place()
    copies = Copies(send_sems, recv_sems)
    local = Locals(local_sems)
    x, c = place.x, place.c
    n, width = residual.shape
    heads_width = q_one.shape[1]
    e = enc_grad.shape[0]
    enc_all = rows_held.at[pl.ds(0, enc_in.shape[0])]
    rows_two = rows_held.at[pl.ds(enc_in.shape[0], 2 * n)]
    rows_one = rows_held.at[pl.ds(0, rows_one_in.shape[0])]
    query_w = qkv_w.at[:, pl.ds(0, heads_width)]
    pair_w = qkv_w.at[:, pl.ds(heads_width, 2 * heads_width)]
    (
        late_at, dpair_at, enc_at, dq_at, rows_two_at, back_at, query_at, pair_w_at, grad_at, res_at, con_at,
        out_w_at, q_at, pair_at, tokens_at,
    ) = [
        local.start(src, dst)
        for src, dst in (
            (late_in, part_late), (dpair_in, dpair_two), (enc_in, enc_all), (dq_in, dq_two),
            (rows_two_in, rows_two), (back_in, part_cross.at[:, pl.ds(0, heads_width)]), (query_in, query_w),
            (pair_w_in, pair_w), (grad_in, grad), (residual_in, residual), (context_in, context),
            (out_w_in, out_w), (q_in, q_one), (pair_in, pair_one), (tokens_in, tokens),
        )
    ]
    greet(place, ("x", "y", "c", "down", "up", "z2"))
    mine = pl.ds(pl.multiple_of(c * n, 16), n)

    def small_unit():
        for at, which in enumerate(("c", "x", "y", "z1", "z2")):
            copy = copies.start(place, small_out.at[at], small_recv.at[at], which)
            yield
            copy.wait_recv()
            small_out[at + 1] = small_out[at] + small_recv[at]

    cross_sums = [back_sum.at[0], query_sum.at[0], pair_sum.at[0], pair_sum.at[1]]
    self_sums = [qkv_sum.at[0], qkv_sum.at[1], qkv_sum.at[2]]
    late_sums = [late_sum.at[0], late_sum.at[1]]
    part_out = part_self.at[:, pl.ds(0, heads_width)]
    part_qkv = part_self.at[:, pl.ds(heads_width, 3 * heads_width)]
    comm = Paced(
        [
            reduce_group(place, rows, cols, part_late, recv, late_sums, copies, 0, ("yzx", "xzy")),
            reduce_group(
                place, rows, cols, part_cross, recv, cross_sums, copies, 2, ("yxz", "yzx", "xzy", "yzx")
            ),
            reduce_group(place, rows, cols, part_out, recv, [out_sum.at[0]], copies, 6, ("yzx",)),
            reduce_group(
                place, rows, cols, part_qkv, recv, self_sums, copies, 7, ("yxz", "yzx", "xzy")
            ),
            [small_unit()],
        ],
        PACE,
    )
    small = small_out.at[0]
    small[...] = small_in[...]
    second = pl.ds(heads_width, heads_width)
    rest = pl.ds(2 * heads_width, 2 * heads_width)
    local.wait(late_at)
    comm.begin()
    fill_biases(place, bias, segment, window)
    local.wait(dpair_at, enc_at)

    def pair_grads(t):
        part_cross[t, rest] = inner_rows(enc_all[:, t], dpair_two[...]).astype(low_type)

    loop_cols(width, BLOCK, pair_grads)
    comm.spend(4.0)
    local.wait(dq_at, rows_two_at, back_at)

    def query_grads(t):
        part_cross[t, second] = inner_rows(rows_two[:, t], dq_two[...]).astype(low_type)

    loop_cols(width, BLOCK, query_grads)
    comm.spend(1.5)
    comm.begin()
    rows_one_at = local.start(rows_one_in, rows_one)
    local.wait(query_at)
    over = exchange_rows(
        place, copies, n, sent.at[0], landed.at[0], lambda r: outer_cols(dq_two[r], query_w[...])
    )
    total[...] = outer_cols(dq_two[mine], query_w[...])
    comm.spend(2.2)
    local.wait(pair_w_at)

    def enc_rows(xx, cc):
        return pl.ds(pl.multiple_of((xx * 2 + cc) * e, LANES), e)

    def enc_term(xx, cc):
        return outer_cols(dpair_two[enc_rows(xx, cc)], pair_w[...])

    enc_sent[0] = enc_term(x, 1 - c).astype(low_type)
    enc_sent[1] = enc_term(1 - x, 1 - c).astype(low_type)
    enc_over = copies.start(place, enc_sent.at[pl.ds(0, 2)], enc_landed.at[pl.ds(0, 2)], "c")
    comm.spend(1.6)
    local.wait(grad_at, res_at)
    over.wait_recv()

    def norm_part(tile, rows_here):
        incoming = total[tile] + landed[0, tile].astype(f32)
        after = grad[tile] + norm_back_tile(small, 1, incoming, residual[tile], gains[1:2])
        grad[tile] = after
        g_one[rows_here] = after.astype(low_type)

    own_tiles(place, n, norm_part)
    g_over = copies.start(place, g_one.at[mine], g_one.at[mine], "c")
    comm.spend(4.0)
    enc_over.wait_recv()
    enc_sent[2] = (enc_term(1 - x, c) + enc_landed[1].astype(f32)).astype(low_type)
    enc_far = copies.start(place, enc_sent.at[2], enc_landed.at[2], "x")
    enc_total[...] = enc_term(x, c) + enc_landed[0].astype(f32)
    qkv_at = local.start(qkv_in, qkv_w)
    comm.spend(2.0)
    local.wait(con_at, out_w_at)
    g_over.wait_recv()
    loop_rows(2 * n, BLOCK, lambda r: store(grad_context, r, matmul(g_one[r], out_w[...])))

    def out_grads(t):
        part_self[t, pl.ds(0, heads_width)] = inner_rows(g_one[:, t], context[...]).astype(low_type)

    loop_cols(width, BLOCK, out_grads)
    comm.spend(2.6)
    comm.begin()
    local.wait(q_at, pair_at)
    attention_back(
        place, comm, q_one, pair_one, lambda block: bias[block], context, grad_context, lse_one, window, dk_sum, dv_sum,
    )
    enc_far.wait_recv()
    enc_total[...] += enc_landed[2].astype(f32)
    local.start(enc_total, enc_grad)
    local.wait(qkv_at)
    q_lanes, kv_lanes = pl.ds(0, heads_width), pl.ds(heads_width, 2 * heads_width)

    def key_term(xx, local_rows):
        at = pl.ds(pl.multiple_of(xx * 2 * n + local_rows.start, LANES), local_rows.size)
        return outer_cols(pair_one[at], qkv_w[:, kv_lanes])

    def query_term(local_rows):
        return outer_cols(q_one[local_rows], qkv_w[:, q_lanes])

    far_over = exchange_rows(
        place, copies, n, sent.at[1], landed.at[1], lambda r: key_term(1 - x, r)
    )
    near_over = exchange_rows(
        place, copies, n, sent.at[2], landed.at[2], lambda r: key_term(x, r) + query_term(r)
    )
    comm.spend(4.0)
    far_over.wait_recv()
    sent[3] = (key_term(1 - x, mine) + landed[1].astype(f32)).astype(low_type)
    chip_over = copies.start(place, sent.at[3], landed.at[3], "x")
    local.wait(rows_one_at)
    chip_rows = pl.ds(pl.multiple_of(x * 2 * n, LANES), 2 * n)

    def self_grads(t):
        part_self[t, second] = inner_rows(rows_one[chip_rows, t], q_one[...]).astype(low_type)
        part_self[t, rest] = inner_rows(rows_one[:, t], pair_one[...]).astype(low_type)

    comm.spend(1.5)
    loop_cols(width, BLOCK, self_grads)
    comm.spend(5.0)
    comm.begin()
    total[...] = key_term(x, mine) + query_term(mine)
    comm.spend(2.0)
    local.wait(tokens_at)
    near_over.wait_recv()
    chip_over.wait_recv()

    def last_part(tile, rows_here):
        incoming = total[tile] + landed[2, tile].astype(f32) + landed[3, tile].astype(f32)
        grad[tile] += norm_back_tile(small, 0, incoming, tokens[tile].astype(f32), gains[0:1])

    own_tiles(place, n, last_part)
    local.start(grad, in_grad)
    comm.begin()
    comm.drain()
    local.finish()
    copies.finish()


def back_two(segment, gains, lse_one, small, hbm, rows, cols, window, enc_rows):
    grad, q_one, pair_one = hbm[7], hbm[11], hbm[12]
    n, width = grad.shape
    heads_width = q_one.shape[1]

    def sums(k):
        return wide(k, rows, cols)

    out_shape = [
        sums(2), sums(1), sums(1), sums(2), sums(1), sums(3), wide(6, 8, width), wide(n, width), wide(enc_rows, width),
    ]
    n_copies = 10 * 15 + 8 + 5
    held = hbm[:2] + hbm[7:13] + hbm[15:16]
    held_rows = max(enc_rows * 4 + 2 * n, hbm[13].shape[0])
    return pl.pallas_call(
        functools.partial(back_two_kernel, (rows, cols), window),
        out_shape=out_shape,
        in_specs=[VMEM_SPEC] * 4 + [ANY_SPEC] * len(hbm),
        out_specs=[VMEM_SPEC] * 7 + [ANY_SPEC] * 2,
        scratch_shapes=scratch_like(held)
        + scratch_like(
            [
                low(held_rows, width), low(*hbm[14].shape), low(width, 4 * cols),
                low(width, 4 * heads_width), low(width, 4 * heads_width), low(10, rows * 15, cols),
                low(4, n, width), low(4, n, width), wide(n, width), low(2 * n, width),
                low(2 * n, heads_width), wide(pair_one.shape[0], PAIR), wide(pair_one.shape[0], PAIR),
                low(3, enc_rows, width), low(3, enc_rows, width), wide(enc_rows, width), wide(5, 8, width),
                wide(2 * n // BLOCK, window, BLOCK),
            ]
        )
        + [
            pltpu.SemaphoreType.DMA((n_copies,)),
            pltpu.SemaphoreType.DMA((n_copies,)),
            pltpu.SemaphoreType.DMA((len(hbm) + 2,)),
        ],
        compiler_params=pltpu.CompilerParams(
            collective_id=3, has_side_effects=True, vmem_limit_bytes=62 * MIB
        ),
        name="back_two",
    )(segment, gains, lse_one, small, *hbm)


BLOCK = 256


def split_heads(values_in):
    lane = lax.broadcasted_iota(jnp.int32, values_in.shape, 1)
    zero = jnp.zeros_like(values_in)
    return jnp.concatenate(
        [jnp.where(lane < HD, values_in, zero), jnp.where(lane >= HD, values_in, zero)], axis=0
    )


def key_scores(queries, keys, bias):
    return outer_cols(keys, queries) + jnp.concatenate([bias, bias], axis=1)


def attend_step(q_block, keys, values, bias):
    rows = q_block.shape[0]
    queries = split_heads(q_block * jnp.asarray(HD**-0.5, low_type))
    scores = key_scores(queries, keys, bias)
    peak = jnp.max(scores, axis=0, keepdims=True)
    probs = jnp.exp(scores - peak)
    total = jnp.sum(probs, axis=0, keepdims=True)
    context = inner_rows(values, probs.astype(low_type)) / total
    pair = jnp.concatenate([context[:HD, :rows], context[HD:, rows:]], axis=0)
    return pair.T.astype(low_type), peak + jnp.log(total)


def attend_back_step(q_block, keys, values, bias, context, grad_context, lse):
    rows = q_block.shape[0]
    queries = split_heads(q_block * jnp.asarray(HD**-0.5, low_type))
    grads = split_heads(grad_context)
    scores = key_scores(queries, keys, bias)
    probs = jnp.exp(scores - lse)
    grad_probs = outer_cols(values, grads)
    product = (grad_context.astype(f32) * context.astype(f32)).T
    inner = jnp.concatenate(
        [
            jnp.sum(product[:HD], axis=0, keepdims=True),
            jnp.sum(product[HD:], axis=0, keepdims=True),
        ],
        axis=1,
    )
    grad_scores = (probs * (grad_probs - inner)).astype(low_type)
    dv = matmul(probs.astype(low_type), grads)
    dk = matmul(grad_scores, queries)
    grad_queries = inner_rows(keys, grad_scores) * HD**-0.5
    pair = jnp.concatenate([grad_queries[:HD, :rows], grad_queries[HD:, rows:]], axis=0)
    return pair.T.astype(low_type), dk, dv


def width_orders(outer, width):
    def spread(values_in):
        if outer == 1:
            return values_in
        parts = values_in.reshape(values_in.shape[:-1] + (outer, RING * 2, -1))
        return jnp.swapaxes(parts, -3, -2).reshape(values_in.shape)

    def back(values_in):
        if outer == 1:
            return values_in
        parts = values_in.reshape(values_in.shape[:-1] + (RING * 2, outer, -1))
        return jnp.swapaxes(parts, -3, -2).reshape(values_in.shape)

    return spread, back


def on_device(
    tokens,
    encoder,
    seg_ids,
    enc_lens,
    attn_qkv,
    attn_out,
    cross_q,
    cross_kv,
    cross_out,
    ffn_in,
    ffn_out,
    norm_gains,
    norm_biases,
    out_grad,
):
    outer = lax.axis_size("o")
    spread, gathered_back = width_orders(outer, tokens.shape[1])
    tokens, encoder, out_grad = spread(tokens), spread(encoder[0]), spread(out_grad)
    norm_gains, norm_biases = spread(norm_gains), spread(norm_biases)
    seq_len = seg_ids.shape[1]
    cols = cross_q.shape[1]
    width = tokens.shape[1]

    def units(block):
        k = block.shape[-1] // cols
        return block.reshape(block.shape[0], k, cols).transpose(1, 0, 2)

    masters = [attn_qkv, attn_out, cross_q, cross_kv, cross_out, ffn_in, ffn_out]
    if outer > 1:
        masters = [
            attn_qkv, attn_out.T[None], cross_q[None], cross_kv, cross_out.T[None], units(ffn_in), units(ffn_out.T)
        ]
        masters = [lax.all_gather(m.astype(low_type), "o", axis=1, tiled=True) for m in masters]
    rows = cross_q.shape[0] * outer
    units_of = (3, 1, 1, 2, 1, ffn_in.shape[1] // cols, ffn_in.shape[1] // cols)
    window = min(seq_len, seq_len // 2 + BLOCK)
    (
        grads_three, qkv_w, out_w, query_w, pair_w, back_w, up_w, down_w, rows_one, enc_full, queries_one, pair_one,
        context_one, lse_one, residual_one, rows_two, queries_two, pair_two, context_two, lse_two, residual_two,
        rows_three, active, slope,
    ) = forward(
        seg_ids, norm_gains, norm_biases, enc_lens, tokens, out_grad, encoder, masters, (rows, cols, units_of), window
    )
    down_sum, up_sum, small, out_tokens, grad_two, back_grad, grad_queries, grad_pair, late_grad = back_one(
        enc_lens, norm_gains, lse_two, down_w, up_w, active, slope, grads_three, rows_three, residual_two,
        queries_two, pair_two, context_two, back_w, rows, cols,
    )
    late_sum, back_sum, query_sum, pair_sum, out_sum, qkv_sum, small, in_grad, enc_grad = back_two(
        seg_ids, norm_gains, lse_one, small,
        [
            grad_queries, grad_pair, rows_two, enc_full, query_w, pair_w, back_grad, grad_two, residual_one,
            context_one, out_w, queries_one, pair_one, rows_one, qkv_w, tokens, late_grad,
        ],
        rows, cols, window, encoder.shape[0],
    )
    enc_grad = enc_grad[None]
    up_sum = jnp.concatenate([up_sum, late_sum], axis=0)
    sums = [up_sum, down_sum, back_sum, query_sum, pair_sum, out_sum, qkv_sum]
    small = small[-1]
    if outer > 1:
        small = lax.psum(small, "o")
        sums = [lax.psum_scatter(s, "o", scatter_dimension=1, tiled=True) for s in sums]
    up_sum, down_sum, back_sum, query_sum, pair_sum, out_sum, qkv_sum = sums

    def joined(block):
        return block.transpose(1, 0, 2).reshape(block.shape[1], -1)

    return (
        gathered_back(out_tokens),
        gathered_back(in_grad),
        gathered_back(enc_grad),
        qkv_sum,
        out_sum[0].T,
        query_sum[0],
        pair_sum,
        back_sum[0].T,
        joined(up_sum),
        joined(down_sum).T,
        gathered_back(small[:3]),
        gathered_back(small[3:6]),
    )


def solution(mesh):
    count, tensor = mesh.devices.shape
    outer = count // (RING * 2)
    fine = Mesh(
        mesh.devices.reshape(outer, RING, 2, tensor // 2, 2), ("o", "z", "y", "x", "c")
    )
    dp, tp = ("o", "z", "y"), ("x", "c")
    in_specs = (
        P(dp + tp, None),
        P(dp, tp, None),
        P(dp, None),
        P(dp),
        P(None, dp, tp),
        P(tp, dp),
        P(dp, tp),
        P(None, dp, tp),
        P(tp, dp),
        P(dp, tp),
        P(tp, dp),
        P(),
        P(),
        P(dp + tp, None),
    )
    out_specs = (
        P(dp + tp, None),
        P(dp + tp, None),
        P(dp, tp, None),
        P(None, dp, tp),
        P(tp, dp),
        P(dp, tp),
        P(None, dp, tp),
        P(tp, dp),
        P(dp, tp),
        P(tp, dp),
        P(),
        P(),
    )
    return jax.shard_map(
        on_device, mesh=fine, in_specs=in_specs, out_specs=out_specs, check_vma=False
    )
```

```python
import functools

import jax
import jax.numpy as jnp
from jax import lax
from jax.experimental import pallas as pl
from jax.experimental.pallas import tpu as pltpu
from jax.sharding import Mesh
from jax.sharding import PartitionSpec as P

HD = 64
DOCS = 4
LANES = 128
PAIR = 2 * HD
RING = 4
epsilon = 1e-05
masked_score = -1e30
MESH = pl.DeviceIdType.MESH
low_type = jnp.bfloat16
f32 = jnp.float32
MIB = 1 << 20


def matmul(left, right):
    return jnp.dot(left, right, preferred_element_type=f32)


def inner_rows(left, right):
    return lax.dot_general(left, right, (((0,), (0,)), ((), ())), preferred_element_type=f32)


def outer_cols(left, right):
    return lax.dot_general(left, right, (((1,), (1,)), ((), ())), preferred_element_type=f32)


def norm_forward(values_in, gain_row, bias_row):
    average = jnp.mean(values_in, axis=-1, keepdims=True)
    centred = values_in - average
    inverse = lax.rsqrt(jnp.mean(centred * centred, axis=-1, keepdims=True) + epsilon)
    unit_rows = centred * inverse
    return (unit_rows * gain_row + bias_row, unit_rows, inverse)


def norm_backward(incoming, unit_rows, inverse, gain_row):
    scaled = incoming * gain_row
    first_mean = jnp.mean(scaled, axis=-1, keepdims=True)
    second_mean = jnp.mean(scaled * unit_rows, axis=-1, keepdims=True)
    result = inverse * (scaled - first_mean - unit_rows * second_mean)
    return (result, jnp.sum(incoming * unit_rows, axis=0), jnp.sum(incoming, axis=0))


class Place:
    def __init__(self):
        self.z = lax.axis_index("z")
        self.y = lax.axis_index("y")
        self.x = lax.axis_index("x")
        self.c = lax.axis_index("c")

    def to(self, which):
        if which == "x":
            return {"x": 1 - self.x}
        if which == "y":
            return {"y": 1 - self.y}
        if which == "c":
            return {"c": 1 - self.c}
        if which == "z1":
            return {"z": self.z + 1 - 2 * lax.rem(self.z, 2)}
        if which == "z2":
            return {"z": lax.rem(self.z + 2, RING)}
        if which == "down":
            return {"z": lax.rem(self.z + RING - 1, RING)}
        return {"z": lax.rem(self.z + 1, RING)}

    def ring(self, step):
        return lax.rem(self.z + step, RING)


def greet(place, names):
    barrier = pltpu.get_barrier_semaphore()
    for name in names:
        pl.semaphore_signal(barrier, inc=1, device_id=place.to(name), device_id_type=MESH)
    pl.semaphore_wait(barrier, len(names))


class Copies:
    def __init__(self, send_sems, recv_sems):
        self.send_sems, self.recv_sems = send_sems, recv_sems
        self.made = []

    def start(self, place, src, dst, which):
        at = len(self.made)
        copy = pltpu.make_async_remote_copy(
            src_ref=src,
            dst_ref=dst,
            send_sem=self.send_sems.at[at],
            recv_sem=self.recv_sems.at[at],
            device_id=place.to(which),
            device_id_type=MESH,
        )
        copy.start()
        self.made.append(copy)
        return copy

    def finish(self):
        for copy in self.made:
            copy.wait_send()


FORWARD_ORDERS = (
    "xzy", "zxy", "yzx", "xzy",
    "xzy", "yzx", "xzy", "zxy",
    "xzy", "yzx", "zxy", "yzx",
    "xzy", "yzx", "zyx", "zxy",
)


def gather_unit(order, place, whole, base, rows, cols, copies):
    x, y = place.x, place.y

    def at(step, both_y, both_x):
        first = place.ring(step) * 2
        row = first * rows if both_y else (first + y) * rows
        col = base if both_x else base + x * cols
        return whole.at[
            pl.ds(pl.multiple_of(row, rows), rows * (2 if both_y else 1)),
            pl.ds(pl.multiple_of(col, LANES), cols * (2 if both_x else 1)),
        ]

    def send(where, which):
        return copies.start(place, where, where, which)

    mine = at(0, False, False)
    if order in ("xzy", "yzx"):
        axis, last = order[0], order[2]
        wide = dict(both_y=axis == "y", both_x=axis == "x")
        first = send(mine, axis)
        yield
        first.wait_recv()
        hop = send(at(0, **wide), "down")
        ends = [send(at(0, **wide), last)]
        yield
        for step in range(1, RING):
            hop.wait_recv()
            if step < RING - 1:
                hop = send(at(step, **wide), "down")
            ends.append(send(at(step, **wide), last))
            yield
        for copy in ends:
            copy.wait_recv()
    else:
        mid, last = order[1], order[2]
        wide = dict(both_y=mid == "y", both_x=mid == "x")
        hop = send(mine, "down")
        mids = [send(mine, mid)]
        ends = []
        yield
        for step in range(1, RING + 1):
            if step < RING:
                hop.wait_recv()
                if step < RING - 1:
                    hop = send(at(step, False, False), "down")
                mids.append(send(at(step, False, False), mid))
            mids[step - 1].wait_recv()
            ends.append(send(at(step - 1, **wide), last))
            yield
        for copy in ends:
            copy.wait_recv()


class Paced:
    def __init__(self, groups, pace):
        self.groups, self.pace = [list(g) for g in groups], pace
        self.live, self.budget = [], 0.0

    def advance(self):
        unit = self.live.pop(0)
        try:
            next(unit)
            self.live.append(unit)
        except StopIteration:
            pass

    def begin(self):
        for unit in self.groups.pop(0):
            next(unit)
            self.live.append(unit)

    def spend(self, time):
        self.budget += time
        while self.budget >= self.pace:
            self.budget -= self.pace
            if self.live:
                self.advance()

    def drain(self):
        while self.live:
            self.advance()


PACE = 2.3
FLOW_PACE = 1.5
DEPTH = 7


class Flow:
    def __init__(self, units, pace, depth):
        self.waiting, self.pace, self.depth = list(units), pace, depth
        self.live, self.budget, self.done = [], 0.0, []

    def fill(self):
        while self.waiting and len(self.live) < self.depth:
            unit = self.waiting.pop(0)
            next(unit)
            self.live.append(unit)

    def advance(self):
        self.fill()
        unit = self.live.pop(0)
        try:
            next(unit)
            self.live.append(unit)
        except StopIteration:
            self.done.append(unit)
            self.fill()

    def spend(self, time):
        self.budget += time
        while self.budget >= self.pace:
            self.budget -= self.pace
            if self.live or self.waiting:
                self.advance()

    def until(self, units):
        while any(all(u is not d for d in self.done) for u in units):
            self.advance()

    def drain(self):
        while self.live or self.waiting:
            self.advance()


class Locals:
    def __init__(self, sems):
        self.sems, self.made = sems, []

    def start(self, src, dst):
        copy = pltpu.make_async_copy(src, dst, self.sems.at[len(self.made)])
        copy.start()
        self.made.append(copy)
        return len(self.made) - 1

    def wait(self, *which):
        for at in which:
            if self.made[at] is not None:
                self.made[at].wait()
                self.made[at] = None

    def finish(self):
        self.wait(*range(len(self.made)))


def own_block(place, whole, base, rows, cols):
    return whole.at[
        pl.ds(pl.multiple_of((place.z * 2 + place.y) * rows, rows), rows),
        pl.ds(pl.multiple_of(base + place.x * cols, LANES), cols),
    ]


def gather_groups(place, sizes, whole, copies, orders):
    rows, cols, units_of = sizes
    units = [
        gather_unit(order, place, whole[which], unit * 2 * cols, rows, cols, copies)
        for (which, unit), order in zip(
            ((w, u) for w, count in enumerate(units_of) for u in range(count)), orders, strict=True
        )
    ]
    return [units[k : k + 4] for k in range(0, len(units), 4)]


def place_own(place, sizes, which, master, whole):
    rows, cols, units_of = sizes
    for unit in range(units_of[which]):
        if len(master.shape) == 3:
            block = master[unit]
        elif master.shape[0] == rows:
            block = master[:, unit * cols : (unit + 1) * cols]
        else:
            block = master[unit * cols : (unit + 1) * cols].T
        own_block(place, whole, unit * 2 * cols, rows, cols)[...] = block.astype(low_type)


ANY_SPEC = pl.BlockSpec(memory_space=pl.ANY)
VMEM_SPEC = pl.BlockSpec(memory_space=pltpu.VMEM)


def norm_rows(values_in, gain_row, bias_row):
    return norm_forward(values_in, gain_row, bias_row)[0]


def loop_rows(count, tile, body):
    @pl.loop(0, count // tile)
    def _(i):
        body(pl.ds(pl.multiple_of(i * tile, tile), tile))


def exchange_rows(place, copies, n, sent, landed, make):
    theirs = pl.ds(pl.multiple_of((1 - place.c) * n, LANES), n)
    sent[...] = make(theirs).astype(low_type)
    return copies.start(place, sent, landed, "c")


def own_tiles(place, n, body):
    @pl.loop(0, n // LANES)
    def _(i):
        tile = pl.ds(pl.multiple_of(i * LANES, LANES), LANES)
        body(tile, pl.ds(pl.multiple_of(place.c * n + i * LANES, LANES), LANES))


def blocks_of(place, rows_count, pair_count, span):
    def at(block):
        rows = pl.ds(pl.multiple_of(block * BLOCK, BLOCK), BLOCK)
        if span == pair_count:
            return rows, 0
        ends = (place.x * (rows_count // BLOCK) + block + 1) * BLOCK
        return rows, pl.multiple_of(jnp.maximum(ends - span, 0), BLOCK)

    return at


def fill_biases(place, bias, segment, span):
    count = segment.shape[1]
    ids = segment[...].astype(f32)
    half = count // 2
    for block in range(bias.shape[0]):
        first = place.x * half + block * BLOCK
        mine = segment[:, pl.ds(pl.multiple_of(first, BLOCK), BLOCK)].astype(f32)
        lows = jnp.zeros(mine.shape, f32)
        for doc in range(DOCS - 1):
            size = jnp.sum(jnp.where(ids == doc, 1.0, 0.0), axis=1, keepdims=True)
            lows += jnp.where(mine > doc, size, 0.0)
        start = jnp.maximum(first + BLOCK - span, 0)
        keys = lax.broadcasted_iota(jnp.int32, bias.shape[1:], 0)
        rows = first - start + lax.broadcasted_iota(jnp.int32, bias.shape[1:], 1)
        seen = (keys.astype(f32) >= lows - start.astype(f32)) & (keys <= rows)
        bias[block] = jnp.where(seen, 0.0, masked_score)


def fill_enc_bias(bias, length):
    keys = lax.broadcasted_iota(jnp.int32, bias.shape, 0)
    bias[...] = jnp.where(keys < length, 0.0, masked_score)


def forward_kernel(sizes, window, n_out, *refs):
    n_weights = len(sizes[2])
    segment, gains, biases, enc_length, tokens_in, g_own, enc_own, *master_in = refs[: 7 + n_weights]
    at = 7 + n_weights
    g_all, *outs = refs[at : at + n_out]
    at += n_out
    held = refs[at : at + n_out - 1]
    at += n_out - 1
    masters = refs[at : at + n_weights]
    tokens, sent, landed, bias_one, bias_two, send_sems, recv_sems, local_sems = refs[at + n_weights :]
    whole = held[:n_weights]
    (
        rows_one, enc_all, q_one, pair_one, context_one, lse_one, residual_one, rows_two, q_two, pair_two,
        context_two, lse_two, residual_two, rows_three, active, slope,
    ) = held[n_weights:]
    qkv_w, out_w, query_w, pair_w, back_w, up_w, _ = whole
    place = Place()
    copies = Copies(send_sems, recv_sems)
    local = Locals(local_sems)
    x, c = place.x, place.c
    n, e = tokens.shape[0], enc_own.shape[0]
    heads_width = q_one.shape[1]
    mine = pl.ds(pl.multiple_of(c * n, 16), n)
    tokens_at = local.start(tokens_in, tokens)
    masters_at = [local.start(src, dst) for src, dst in zip(master_in, masters)]

    def flush(*names):
        for ref in names:
            local.start(ref, outs[[h is ref for h in held].index(True)])

    def part_of(ref, xx, cc, size):
        return ref.at[pl.ds(pl.multiple_of((xx * 2 + cc) * size, 16), size)]

    enc_at = local.start(enc_own, part_of(enc_all, x, c, e))
    local.start(g_own, g_all.at[mine])
    greet(place, ("x", "y", "c", "down", "up"))
    local.wait(tokens_at)
    h_own = part_of(rows_one, x, c, n)

    @pl.loop(0, n // LANES)
    def _(i):
        tile = pl.ds(pl.multiple_of(i * LANES, LANES), LANES)
        normed = norm_rows(tokens[tile].astype(f32), gains[0:1], biases[0:1])
        rows_one[pl.ds(pl.multiple_of((x * 2 + c) * n + i * LANES, LANES), LANES)] = normed.astype(low_type)

    hx = copies.start(place, h_own, h_own, "x")
    hc = copies.start(place, h_own, h_own, "c")
    orders = FORWARD_ORDERS
    groups = gather_groups(place, sizes, whole, copies, orders)

    def rows_unit(own_x, own_c, ref, size, also):
        yield
        yield
        own_x.wait_recv()
        far = part_of(ref, 1 - x, c, size)
        over = copies.start(place, far, far, "c")
        yield
        yield
        for copy in (own_c, over, *also):
            copy.wait_recv()

    groups[0].append(rows_unit(hx, hc, rows_one, n, ()))
    for which in range(n_weights):
        local.wait(masters_at[which])
        place_own(place, sizes, which, masters[which], whole[which])
        if which == 1:
            comm = Flow(groups[0], FLOW_PACE, len(groups[0]))
            comm.fill()
    local.wait(enc_at)
    e_own = part_of(enc_all, x, c, e)
    ex = copies.start(place, e_own, e_own, "x")
    ec = copies.start(place, e_own, e_own, "c")
    gc = copies.start(place, g_own, g_all.at[mine], "c")
    groups_late = rows_unit(ex, ec, enc_all, e, (gc,))
    groups[1].append(groups_late)
    comm.waiting.extend(groups[1] + groups[2] + groups[3])
    comm.depth = DEPTH
    fill_biases(place, bias_one, segment, window)
    fill_enc_bias(bias_two, enc_length[0])

    def attention(q_ref, pair_ref, bias_of, o_ref, lse_ref, span):
        block_at = blocks_of(place, q_ref.shape[0], pair_ref.shape[0], span)
        for pair in range(heads_width // PAIR):
            comm.spend(4.0)
            lanes = pl.ds(pair * PAIR, PAIR)
            value_lanes = pl.ds(heads_width + pair * PAIR, PAIR)

            @pl.loop(0, q_ref.shape[0] // BLOCK)
            def _(block):
                rows, start = block_at(block)
                here = pl.ds(start, span)
                o_ref[rows, lanes], lse_ref[pair, block] = attend_step(
                    q_ref[rows, lanes],
                    pair_ref[here, lanes],
                    pair_ref[here, value_lanes],
                    bias_of(block),
                )

    def branch(at, context, weight, before, after, gain_at, rows_ref):
        over = exchange_rows(
            place, copies, n, sent.at[at], landed.at[at],
            lambda rows: outer_cols(context[rows], weight[...]),
        )

        after[...] = before[...].astype(f32) + outer_cols(context[mine], weight[...])
        over.wait_recv()

        def rest(tile, rows):
            total = after[tile] + landed[at, tile].astype(f32)
            after[tile] = total
            rows_ref[rows] = norm_rows(
                total, gains[gain_at : gain_at + 1], biases[gain_at : gain_at + 1]
            ).astype(low_type)

        own_tiles(place, n, rest)
        return copies.start(place, rows_ref.at[mine], rows_ref.at[mine], "c")

    comm.until(groups[0])
    flush(rows_one, qkv_w, out_w)

    def project(rows):
        first = pl.ds(pl.multiple_of(x * 2 * n + rows.start, BLOCK), rows.size)
        q_one[rows] = matmul(rows_one[first], qkv_w[:, :heads_width]).astype(low_type)

    loop_rows(2 * n, BLOCK, project)
    comm.spend(2.0)
    loop_rows(
        4 * n, BLOCK, lambda r: store(pair_one, r, matmul(rows_one[r], qkv_w[:, heads_width:]))
    )
    flush(q_one, pair_one)
    comm.spend(4.0)
    attention(q_one, pair_one, lambda block: bias_one[block], context_one, lse_one, window)
    over = branch(0, context_one, out_w, tokens, residual_one, 1, rows_two)
    flush(context_one, lse_one, residual_one)
    comm.spend(5.0)
    comm.until(groups[1])
    loop_rows(
        enc_all.shape[0], BLOCK, lambda r: store(pair_two, r, matmul(enc_all[r], pair_w[...]))
    )
    flush(query_w, pair_w, back_w, enc_all, pair_two)
    over.wait_recv()
    comm.spend(3.0)
    loop_rows(2 * n, BLOCK, lambda r: store(q_two, r, matmul(rows_two[r], query_w[...])))
    flush(rows_two, q_two)
    attention(
        q_two, pair_two, lambda block: bias_two[...], context_two, lse_two, enc_all.shape[0]
    )
    over = branch(1, context_two, back_w, residual_one, residual_two, 2, rows_three)
    flush(context_two, lse_two, residual_two)
    comm.spend(5.0)
    comm.until(groups[2])
    over.wait_recv()
    flush(rows_three, up_w)

    def up(rows):
        inner = matmul(rows_three[rows], up_w[...])
        gate = 1.0 / (1.0 + jnp.exp(-inner))
        active[rows] = (inner * gate).astype(low_type)
        slope[rows] = (gate * (1.0 + inner * (1.0 - gate))).astype(low_type)

    loop_rows(2 * n, BLOCK, up)
    flush(active, slope)
    comm.drain()
    flush(whole[-1])
    local.finish()
    copies.finish()


def store(ref, rows, values_in):
    ref[rows] = values_in.astype(ref.dtype)


def low(*shape):
    return jax.ShapeDtypeStruct(shape, low_type)


def wide(*shape):
    return jax.ShapeDtypeStruct(shape, f32)


def scratch_like(shapes):
    return [pltpu.VMEM(s.shape, s.dtype) for s in shapes]


def forward(segment, gains, biases, enc_lens, tokens, g_own, enc_own, masters, sizes, window):
    rows, cols, units_of = sizes
    n, width = tokens.shape
    e = enc_own.shape[0]
    hidden = 2 * cols * units_of[-1]
    heads_width = 2 * cols
    n_units = sum(units_of)
    n_copies = 11 + n_units * 11
    lse = wide(heads_width // PAIR, 2 * n // BLOCK, 1, 2 * BLOCK)
    held = [low(width, 2 * cols * k) for k in units_of] + [
        low(4 * n, width), low(4 * e, width),
        low(2 * n, heads_width), low(4 * n, 2 * heads_width), low(2 * n, heads_width), lse, wide(n, width),
        low(2 * n, width), low(2 * n, heads_width), low(4 * e, 2 * heads_width), low(2 * n, heads_width), lse,
        wide(n, width), low(2 * n, width), low(2 * n, hidden), low(2 * n, hidden),
    ]
    out_shape = [low(2 * n, width)] + held
    return pl.pallas_call(
        functools.partial(forward_kernel, sizes, window, len(out_shape)),
        out_shape=out_shape,
        in_specs=[VMEM_SPEC] * 3
        + [pl.BlockSpec(memory_space=pltpu.SMEM)]
        + [ANY_SPEC] * (3 + len(masters)),
        out_specs=[ANY_SPEC] * len(out_shape),
        scratch_shapes=scratch_like(held + masters + [tokens])
        + scratch_like([low(2, n, width)] * 2)
        + scratch_like([wide(2 * n // BLOCK, window, BLOCK), wide(4 * e, BLOCK)])
        + [
            pltpu.SemaphoreType.DMA((n_copies,)),
            pltpu.SemaphoreType.DMA((n_copies,)),
            pltpu.SemaphoreType.DMA((3 + len(masters) + len(held),)),
        ],
        compiler_params=pltpu.CompilerParams(
            collective_id=2, has_side_effects=True, vmem_limit_bytes=62 * MIB
        ),
        name="forward",
    )(segment, gains, biases, enc_lens, tokens, g_own, enc_own, *masters)


REDUCE_ORDERS = ("xyz", "xzy", "yxz", "yzx")
CHUNK_ORDER = tuple(range(1, RING)) + (0,)


def reduce_unit(order, place, part, base, rows, cols, recv, out, copies):
    x, y = place.x, place.y

    def at(step, row_of, col_of):
        first = place.ring(step) * 2
        row = first * rows if row_of is None else (first + row_of) * rows
        col = base if col_of is None else base + col_of * cols
        return part.at[
            pl.ds(pl.multiple_of(row, rows), rows * (2 if row_of is None else 1)),
            pl.ds(pl.multiple_of(col, LANES), cols * (2 if col_of is None else 1)),
        ]

    used = [0]

    def landing(shape):
        height = shape[0] * (shape[1] // cols)
        where = [
            recv.at[pl.ds(used[0] + k * shape[0], shape[0])] for k in range(shape[1] // cols)
        ]
        used[0] += height
        return where

    def add(target, source):
        target[...] = target[...] + source[...]

    def exchange(step, which, mid):
        sent = []
        if which == "x":
            if mid:
                spots = [(at(step, y, 1 - x), at(step, y, x))]
            else:
                spots = [(at(step, None, 1 - x), at(step, None, x))]
        else:
            if mid:
                spots = [(at(step, 1 - y, x), at(step, y, x))]
            else:
                spots = [(at(step, 1 - y, k), at(step, y, k)) for k in range(2)]
        for src, keep_at in spots:
            (land,) = landing((src.shape[0], cols))
            sent.append((copies.start(place, src, land, which), keep_at, land))
        return sent

    def take(sent):
        for copy, keep_at, land in sent:
            copy.wait_recv()
            add(keep_at, land)

    def ring_hop(step, spots, ready, arrived):
        if step in ready:
            take(ready[step])
        for (copy, land), spot in zip(arrived or [], spots):
            copy.wait_recv()
            add(spot, land)
        sent = []
        if step != 0:
            for spot in spots:
                (land,) = landing((spot.shape[0], cols))
                sent.append((copies.start(place, spot, land, "down"), land))
        return sent

    first, middle, last = order
    outer, inner = {}, {}
    for step in CHUNK_ORDER[:2]:
        outer[step] = exchange(step, first, False)
    yield
    hop = None
    for k, step in enumerate(CHUNK_ORDER):
        take(outer[step])
        if k + 2 < RING:
            outer[CHUNK_ORDER[k + 2]] = exchange(CHUNK_ORDER[k + 2], first, False)
        if last == "z":
            inner[step] = exchange(step, middle, True)
            if k > 0:
                hop = ring_hop(CHUNK_ORDER[k - 1], [at(CHUNK_ORDER[k - 1], y, x)], inner, hop)
        else:
            if first == "x":
                spots = [at(step, None, x)]
            else:
                spots = [at(step, y, half) for half in range(2)]
            hop = ring_hop(step, spots, {}, hop)
        yield
    if last == "z":
        take(inner[0])
        ((copy, land),) = hop
    else:
        src = at(0, 1 - y, x) if last == "y" else at(0, y, 1 - x)
        (land,) = landing((rows, cols))
        copy = copies.start(place, src, land, last)
        yield
    copy.wait_recv()
    out[...] = at(0, y, x)[...].astype(f32) + land[...].astype(f32)


def reduce_group(place, rows, cols, part, recv, outs, copies, first, orders):
    return [
        reduce_unit(
            order, place, part, unit * 2 * cols, rows, cols, recv.at[first + unit], outs[unit], copies
        )
        for unit, order in enumerate(orders)
    ]


def attention_back(place, comm, q_ref, pair_ref, bias_of, o_ref, do_ref, lse_ref, span, dk_sum, dv_sum):
    heads_width = q_ref.shape[1]
    block_at = blocks_of(place, q_ref.shape[0], pair_ref.shape[0], span)
    for pair in range(heads_width // PAIR):
        lanes = pl.ds(pair * PAIR, PAIR)
        value_lanes = pl.ds(heads_width + pair * PAIR, PAIR)
        dk_sum[...] = jnp.zeros_like(dk_sum)
        dv_sum[...] = jnp.zeros_like(dv_sum)

        @pl.loop(0, q_ref.shape[0] // BLOCK)
        def _(block):
            rows, start = block_at(block)
            here = pl.ds(start, span)
            dq, dk, dv = attend_back_step(
                q_ref[rows, lanes],
                pair_ref[here, lanes],
                pair_ref[here, value_lanes],
                bias_of(block),
                o_ref[rows, lanes],
                do_ref[rows, lanes],
                lse_ref[pair, block],
            )
            q_ref[rows, lanes] = dq
            dk_sum[here] += dk
            dv_sum[here] += dv

        pair_ref[:, lanes] = dk_sum[...].astype(low_type)
        pair_ref[:, value_lanes] = dv_sum[...].astype(low_type)
        comm.spend(6.0)


def loop_cols(count, tile, body):
    loop_rows(count, tile, body)


def norm_back_tile(small, at, incoming, before, gain_row):
    _, unit_rows, inverse = norm_forward(before, jnp.ones_like(gain_row), jnp.zeros_like(gain_row))
    result, gain_sum, bias_sum = norm_backward(incoming, unit_rows, inverse, gain_row)
    small[at : at + 1] += gain_sum[None]
    small[at + 3 : at + 4] += bias_sum[None]
    return result


def back_one_kernel(sizes, *refs):
    rows, cols = sizes
    (
        enc_length, gains, lse_two,
        down_in, up_in, active_in, slope_in, g_in, rows_in, residual_in, q_in, pair_in, context_in, back_in,
        down_sum, up_sum, small, out_tokens, grad_out, back_out, dq_out, dpair_out, late_out,
        down_w, up_w, active, slope, g_all, rows_three, residual, q_two, pair_two, context, back_w,
        part_down, part_up, recv, sent, landed, grad, g_two, back_part, grad_context, tokens_out, dk_sum, dv_sum,
        bias, send_sems, recv_sems, local_sems,
    ) = refs
    place = Place()
    copies = Copies(send_sems, recv_sems)
    local = Locals(local_sems)
    c = place.c
    g_at, active_at, down_at, slope_at, rows_at, up_at, res_at, con_at, back_at, q_at, pair_at = [
        local.start(src, dst)
        for src, dst in (
            (g_in, g_all), (active_in, active), (down_in, down_w), (slope_in, slope), (rows_in, rows_three),
            (up_in, up_w), (residual_in, residual), (context_in, context), (back_in, back_w),
            (q_in, q_two), (pair_in, pair_two),
        )
    ]
    greet(place, ("x", "y", "c", "down", "up"))
    n, width = residual.shape
    mine = pl.ds(pl.multiple_of(c * n, 16), n)
    comm = Paced(
        [
            reduce_group(
                place, rows, cols, part_down, recv, [down_sum.at[k] for k in range(4)], copies, 0,
                REDUCE_ORDERS,
            ),
            reduce_group(
                place, rows, cols, part_up, recv, [up_sum.at[k] for k in range(2)], copies, 4, ("xzy", "yxz")
            ),
        ],
        PACE,
    )
    small[...] = jnp.zeros_like(small)
    fill_enc_bias(bias, enc_length[0])
    local.wait(g_at, active_at)
    loop_cols(width, BLOCK, lambda t: store(part_down, t, inner_rows(g_all[:, t], active[...])))
    comm.begin()
    local.wait(down_at, slope_at)

    def inner(tile):
        slope[tile] = (matmul(g_all[tile], down_w[...]) * slope[tile].astype(f32)).astype(low_type)

    loop_rows(2 * n, BLOCK, inner)
    comm.spend(4.5)
    local.wait(rows_at)
    loop_cols(width, BLOCK, lambda t: store(part_up, t, inner_rows(rows_three[:, t], slope[...])))
    comm.spend(4.8)
    comm.begin()
    local.start(part_up.at[:, pl.ds(4 * cols, 4 * cols)], late_out)
    local.wait(up_at)
    over = exchange_rows(
        place, copies, n, sent.at[0], landed.at[0], lambda r: outer_cols(slope[r], up_w[...])
    )
    comm.spend(2.4)
    grad[...] = outer_cols(slope[mine], up_w[...])
    comm.spend(2.4)
    out_over = exchange_rows(
        place, copies, n, sent.at[1], landed.at[1], lambda r: outer_cols(active[r], down_w[...])
    )
    local.wait(res_at)
    over.wait_recv()

    def norm_part(tile, rows_here):
        incoming = grad[tile] + landed[0, tile].astype(f32)
        total = g_all[rows_here].astype(f32) + norm_back_tile(
            small, 2, incoming, residual[tile], gains[2:3]
        )
        grad[tile] = total
        g_two[rows_here] = total.astype(low_type)

    own_tiles(place, n, norm_part)
    g_over = copies.start(place, g_two.at[mine], g_two.at[mine], "c")
    local.start(grad, grad_out)
    comm.spend(5.5)
    out_over.wait_recv()
    out_own = residual[...] + outer_cols(active[mine], down_w[...])
    tokens_out[...] = (out_own + landed[1].astype(f32)).astype(low_type)
    local.start(tokens_out, out_tokens)
    comm.spend(2.5)
    local.wait(con_at, back_at)
    g_over.wait_recv()
    loop_rows(2 * n, BLOCK, lambda r: store(grad_context, r, matmul(g_two[r], back_w[...])))
    loop_cols(width, BLOCK, lambda t: store(back_part, t, inner_rows(g_two[:, t], context[...])))
    local.start(back_part, back_out)
    comm.spend(3.0)
    local.wait(q_at, pair_at)
    attention_back(
        place, comm, q_two, pair_two, lambda block: bias[...], context, grad_context, lse_two, pair_two.shape[0], dk_sum, dv_sum,
    )
    local.start(q_two, dq_out)
    local.start(pair_two, dpair_out)
    comm.drain()
    local.finish()
    copies.finish()


def back_one(enc_lens, gains, lse_two, down_w, up_w, active, slope, g_all, rows_three, residual, q_two, pair_two, context, back_w, rows, cols):
    n, width = residual.shape
    heads_width = q_two.shape[1]
    hbm = [down_w, up_w, active, slope, g_all, rows_three, residual, q_two, pair_two, context, back_w]
    out_shape = [
        wide(4, rows, cols), wide(2, rows, cols), wide(8, width), low(n, width), wide(n, width),
        low(width, heads_width), low(2 * n, heads_width), low(*pair_two.shape), low(width, 4 * cols),
    ]
    n_copies = 6 * 15 + 3
    return pl.pallas_call(
        functools.partial(back_one_kernel, (rows, cols)),
        out_shape=out_shape,
        in_specs=[pl.BlockSpec(memory_space=pltpu.SMEM)] + [VMEM_SPEC] * 2 + [ANY_SPEC] * len(hbm),
        out_specs=[VMEM_SPEC] * 3 + [ANY_SPEC] * 6,
        scratch_shapes=scratch_like(hbm)
        + scratch_like(
            [
                low(*down_w.shape), low(*up_w.shape), low(6, rows * 15, cols), low(2, n, width),
                low(2, n, width), wide(n, width), low(2 * n, width), low(width, heads_width),
                low(2 * n, heads_width), low(n, width), wide(pair_two.shape[0], PAIR), wide(pair_two.shape[0], PAIR),
                wide(pair_two.shape[0], BLOCK),
            ]
        )
        + [
            pltpu.SemaphoreType.DMA((n_copies,)),
            pltpu.SemaphoreType.DMA((n_copies,)),
            pltpu.SemaphoreType.DMA((len(hbm) + 6,)),
        ],
        compiler_params=pltpu.CompilerParams(
            collective_id=1, has_side_effects=True, vmem_limit_bytes=60 * MIB
        ),
        name="back_one",
    )(enc_lens, gains, lse_two, *hbm)


def back_two_kernel(sizes, window, *refs):
    rows, cols = sizes
    (
        segment, gains, lse_one, small_in,
        dq_in, dpair_in, rows_two_in, enc_in, query_in, pair_w_in, back_in, grad_in, residual_in, context_in,
        out_w_in, q_in, pair_in, rows_one_in, qkv_in, tokens_in, late_in,
        late_sum, back_sum, query_sum, pair_sum, out_sum, qkv_sum, small_out, in_grad, enc_grad,
        dq_two, dpair_two, grad, residual, context, out_w, q_one, pair_one, tokens,
        rows_held, qkv_w, part_late, part_cross, part_self, recv, sent, landed, total, g_one, grad_context, dk_sum, dv_sum,
        enc_sent, enc_landed, enc_total, small_recv, bias, send_sems, recv_sems, local_sems,
    ) = refs
    place = Place()
    copies = Copies(send_sems, recv_sems)
    local = Locals(local_sems)
    x, c = place.x, place.c
    n, width = residual.shape
    heads_width = q_one.shape[1]
    e = enc_grad.shape[0]
    enc_all = rows_held.at[pl.ds(0, enc_in.shape[0])]
    rows_two = rows_held.at[pl.ds(enc_in.shape[0], 2 * n)]
    rows_one = rows_held.at[pl.ds(0, rows_one_in.shape[0])]
    query_w = qkv_w.at[:, pl.ds(0, heads_width)]
    pair_w = qkv_w.at[:, pl.ds(heads_width, 2 * heads_width)]
    (
        late_at, dpair_at, enc_at, dq_at, rows_two_at, back_at, query_at, pair_w_at, grad_at, res_at, con_at,
        out_w_at, q_at, pair_at, tokens_at,
    ) = [
        local.start(src, dst)
        for src, dst in (
            (late_in, part_late), (dpair_in, dpair_two), (enc_in, enc_all), (dq_in, dq_two),
            (rows_two_in, rows_two), (back_in, part_cross.at[:, pl.ds(0, heads_width)]), (query_in, query_w),
            (pair_w_in, pair_w), (grad_in, grad), (residual_in, residual), (context_in, context),
            (out_w_in, out_w), (q_in, q_one), (pair_in, pair_one), (tokens_in, tokens),
        )
    ]
    greet(place, ("x", "y", "c", "down", "up", "z2"))
    mine = pl.ds(pl.multiple_of(c * n, 16), n)

    def small_unit():
        for at, which in enumerate(("c", "x", "y", "z1", "z2")):
            copy = copies.start(place, small_out.at[at], small_recv.at[at], which)
            yield
            copy.wait_recv()
            small_out[at + 1] = small_out[at] + small_recv[at]

    cross_sums = [back_sum.at[0], query_sum.at[0], pair_sum.at[0], pair_sum.at[1]]
    self_sums = [qkv_sum.at[0], qkv_sum.at[1], qkv_sum.at[2]]
    late_sums = [late_sum.at[0], late_sum.at[1]]
    part_out = part_self.at[:, pl.ds(0, heads_width)]
    part_qkv = part_self.at[:, pl.ds(heads_width, 3 * heads_width)]
    comm = Paced(
        [
            reduce_group(place, rows, cols, part_late, recv, late_sums, copies, 0, ("yzx", "xzy")),
            reduce_group(
                place, rows, cols, part_cross, recv, cross_sums, copies, 2, ("yxz", "yzx", "xzy", "yzx")
            ),
            reduce_group(place, rows, cols, part_out, recv, [out_sum.at[0]], copies, 6, ("yzx",)),
            reduce_group(
                place, rows, cols, part_qkv, recv, self_sums, copies, 7, ("yxz", "yzx", "xzy")
            ),
            [small_unit()],
        ],
        PACE,
    )
    small = small_out.at[0]
    small[...] = small_in[...]
    second = pl.ds(heads_width, heads_width)
    rest = pl.ds(2 * heads_width, 2 * heads_width)
    local.wait(late_at)
    comm.begin()
    fill_biases(place, bias, segment, window)
    local.wait(dpair_at, enc_at)

    def pair_grads(t):
        part_cross[t, rest] = inner_rows(enc_all[:, t], dpair_two[...]).astype(low_type)

    loop_cols(width, BLOCK, pair_grads)
    comm.spend(4.0)
    local.wait(dq_at, rows_two_at, back_at)

    def query_grads(t):
        part_cross[t, second] = inner_rows(rows_two[:, t], dq_two[...]).astype(low_type)

    loop_cols(width, BLOCK, query_grads)
    comm.spend(1.5)
    comm.begin()
    rows_one_at = local.start(rows_one_in, rows_one)
    local.wait(query_at)
    over = exchange_rows(
        place, copies, n, sent.at[0], landed.at[0], lambda r: outer_cols(dq_two[r], query_w[...])
    )
    total[...] = outer_cols(dq_two[mine], query_w[...])
    comm.spend(2.2)
    local.wait(pair_w_at)

    def enc_rows(xx, cc):
        return pl.ds(pl.multiple_of((xx * 2 + cc) * e, LANES), e)

    def enc_term(xx, cc):
        return outer_cols(dpair_two[enc_rows(xx, cc)], pair_w[...])

    enc_sent[0] = enc_term(x, 1 - c).astype(low_type)
    enc_sent[1] = enc_term(1 - x, 1 - c).astype(low_type)
    enc_over = copies.start(place, enc_sent.at[pl.ds(0, 2)], enc_landed.at[pl.ds(0, 2)], "c")
    comm.spend(1.6)
    local.wait(grad_at, res_at)
    over.wait_recv()

    def norm_part(tile, rows_here):
        incoming = total[tile] + landed[0, tile].astype(f32)
        after = grad[tile] + norm_back_tile(small, 1, incoming, residual[tile], gains[1:2])
        grad[tile] = after
        g_one[rows_here] = after.astype(low_type)

    own_tiles(place, n, norm_part)
    g_over = copies.start(place, g_one.at[mine], g_one.at[mine], "c")
    comm.spend(4.0)
    enc_over.wait_recv()
    enc_sent[2] = (enc_term(1 - x, c) + enc_landed[1].astype(f32)).astype(low_type)
    enc_far = copies.start(place, enc_sent.at[2], enc_landed.at[2], "x")
    enc_total[...] = enc_term(x, c) + enc_landed[0].astype(f32)
    qkv_at = local.start(qkv_in, qkv_w)
    comm.spend(2.0)
    local.wait(con_at, out_w_at)
    g_over.wait_recv()
    loop_rows(2 * n, BLOCK, lambda r: store(grad_context, r, matmul(g_one[r], out_w[...])))

    def out_grads(t):
        part_self[t, pl.ds(0, heads_width)] = inner_rows(g_one[:, t], context[...]).astype(low_type)

    loop_cols(width, BLOCK, out_grads)
    comm.spend(2.6)
    comm.begin()
    local.wait(q_at, pair_at)
    attention_back(
        place, comm, q_one, pair_one, lambda block: bias[block], context, grad_context, lse_one, window, dk_sum, dv_sum,
    )
    enc_far.wait_recv()
    enc_total[...] += enc_landed[2].astype(f32)
    local.start(enc_total, enc_grad)
    local.wait(qkv_at)
    q_lanes, kv_lanes = pl.ds(0, heads_width), pl.ds(heads_width, 2 * heads_width)

    def key_term(xx, local_rows):
        at = pl.ds(pl.multiple_of(xx * 2 * n + local_rows.start, LANES), local_rows.size)
        return outer_cols(pair_one[at], qkv_w[:, kv_lanes])

    def query_term(local_rows):
        return outer_cols(q_one[local_rows], qkv_w[:, q_lanes])

    far_over = exchange_rows(
        place, copies, n, sent.at[1], landed.at[1], lambda r: key_term(1 - x, r)
    )
    near_over = exchange_rows(
        place, copies, n, sent.at[2], landed.at[2], lambda r: key_term(x, r) + query_term(r)
    )
    comm.spend(4.0)
    far_over.wait_recv()
    sent[3] = (key_term(1 - x, mine) + landed[1].astype(f32)).astype(low_type)
    chip_over = copies.start(place, sent.at[3], landed.at[3], "x")
    local.wait(rows_one_at)
    chip_rows = pl.ds(pl.multiple_of(x * 2 * n, LANES), 2 * n)

    def self_grads(t):
        part_self[t, second] = inner_rows(rows_one[chip_rows, t], q_one[...]).astype(low_type)
        part_self[t, rest] = inner_rows(rows_one[:, t], pair_one[...]).astype(low_type)

    comm.spend(1.5)
    loop_cols(width, BLOCK, self_grads)
    comm.spend(5.0)
    comm.begin()
    total[...] = key_term(x, mine) + query_term(mine)
    comm.spend(2.0)
    local.wait(tokens_at)
    near_over.wait_recv()
    chip_over.wait_recv()

    def last_part(tile, rows_here):
        incoming = total[tile] + landed[2, tile].astype(f32) + landed[3, tile].astype(f32)
        grad[tile] += norm_back_tile(small, 0, incoming, tokens[tile].astype(f32), gains[0:1])

    own_tiles(place, n, last_part)
    local.start(grad, in_grad)
    comm.begin()
    comm.drain()
    local.finish()
    copies.finish()


def back_two(segment, gains, lse_one, small, hbm, rows, cols, window, enc_rows):
    grad, q_one, pair_one = hbm[7], hbm[11], hbm[12]
    n, width = grad.shape
    heads_width = q_one.shape[1]

    def sums(k):
        return wide(k, rows, cols)

    out_shape = [
        sums(2), sums(1), sums(1), sums(2), sums(1), sums(3), wide(6, 8, width), wide(n, width), wide(enc_rows, width),
    ]
    n_copies = 10 * 15 + 8 + 5
    held = hbm[:2] + hbm[7:13] + hbm[15:16]
    held_rows = max(enc_rows * 4 + 2 * n, hbm[13].shape[0])
    return pl.pallas_call(
        functools.partial(back_two_kernel, (rows, cols), window),
        out_shape=out_shape,
        in_specs=[VMEM_SPEC] * 4 + [ANY_SPEC] * len(hbm),
        out_specs=[VMEM_SPEC] * 7 + [ANY_SPEC] * 2,
        scratch_shapes=scratch_like(held)
        + scratch_like(
            [
                low(held_rows, width), low(*hbm[14].shape), low(width, 4 * cols),
                low(width, 4 * heads_width), low(width, 4 * heads_width), low(10, rows * 15, cols),
                low(4, n, width), low(4, n, width), wide(n, width), low(2 * n, width),
                low(2 * n, heads_width), wide(pair_one.shape[0], PAIR), wide(pair_one.shape[0], PAIR),
                low(3, enc_rows, width), low(3, enc_rows, width), wide(enc_rows, width), wide(5, 8, width),
                wide(2 * n // BLOCK, window, BLOCK),
            ]
        )
        + [
            pltpu.SemaphoreType.DMA((n_copies,)),
            pltpu.SemaphoreType.DMA((n_copies,)),
            pltpu.SemaphoreType.DMA((len(hbm) + 2,)),
        ],
        compiler_params=pltpu.CompilerParams(
            collective_id=3, has_side_effects=True, vmem_limit_bytes=62 * MIB
        ),
        name="back_two",
    )(segment, gains, lse_one, small, *hbm)


BLOCK = 256


def split_heads(values_in):
    lane = lax.broadcasted_iota(jnp.int32, values_in.shape, 1)
    zero = jnp.zeros_like(values_in)
    return jnp.concatenate(
        [jnp.where(lane < HD, values_in, zero), jnp.where(lane >= HD, values_in, zero)], axis=0
    )


def key_scores(queries, keys, bias):
    return outer_cols(keys, queries) + jnp.concatenate([bias, bias], axis=1)


def attend_step(q_block, keys, values, bias):
    rows = q_block.shape[0]
    queries = split_heads(q_block * jnp.asarray(HD**-0.5, low_type))
    scores = key_scores(queries, keys, bias)
    peak = jnp.max(scores, axis=0, keepdims=True)
    probs = jnp.exp(scores - peak)
    total = jnp.sum(probs, axis=0, keepdims=True)
    context = inner_rows(values, probs.astype(low_type)) / total
    pair = jnp.concatenate([context[:HD, :rows], context[HD:, rows:]], axis=0)
    return pair.T.astype(low_type), peak + jnp.log(total)


def attend_back_step(q_block, keys, values, bias, context, grad_context, lse):
    rows = q_block.shape[0]
    queries = split_heads(q_block * jnp.asarray(HD**-0.5, low_type))
    grads = split_heads(grad_context)
    scores = key_scores(queries, keys, bias)
    probs = jnp.exp(scores - lse)
    grad_probs = outer_cols(values, grads)
    product = (grad_context.astype(f32) * context.astype(f32)).T
    inner = jnp.concatenate(
        [
            jnp.sum(product[:HD], axis=0, keepdims=True),
            jnp.sum(product[HD:], axis=0, keepdims=True),
        ],
        axis=1,
    )
    grad_scores = (probs * (grad_probs - inner)).astype(low_type)
    dv = matmul(probs.astype(low_type), grads)
    dk = matmul(grad_scores, queries)
    grad_queries = inner_rows(keys, grad_scores) * HD**-0.5
    pair = jnp.concatenate([grad_queries[:HD, :rows], grad_queries[HD:, rows:]], axis=0)
    return pair.T.astype(low_type), dk, dv


def finish_kernel(n_parts, *refs):
    parts, outs, held, sems = refs[:n_parts], refs[n_parts:-1 - n_parts], refs[-1 - n_parts : -1], refs[-1]
    local = Locals(sems)
    for src, dst in zip(parts, held):
        local.start(src, dst)
    local.finish()
    tokens_in, in_grad_in, enc_in, small, up, late, down, back, query, pair, out, qkv = held
    tokens_out, in_grad, enc_grad, qkv_out, out_out, query_out, pair_out, back_out, up_out, down_out, gain, bias = outs
    cols = up.shape[2]
    tokens_out[...] = tokens_in[...]
    in_grad[...] = in_grad_in[...]
    enc_grad[0] = enc_in[...]
    qkv_out[...] = qkv[...]
    out_out[...] = out[0].T
    query_out[...] = query[0]
    pair_out[...] = pair[...]
    back_out[...] = back[0].T
    for unit in range(up.shape[0] + late.shape[0]):
        block = up[unit] if unit < up.shape[0] else late[unit - up.shape[0]]
        up_out[:, unit * cols : (unit + 1) * cols] = block
    for unit in range(down.shape[0]):
        down_out[unit * cols : (unit + 1) * cols] = down[unit].T
    gain[...] = small[small.shape[0] - 1, 0:3]
    bias[...] = small[small.shape[0] - 1, 3:6]


def finish(*parts):
    tokens, in_grad, enc_grad, small, up, late, down, back, query, pair, out, qkv = parts
    rows, cols = up.shape[1:]
    width = small.shape[2]
    hidden = cols * down.shape[0]
    out_shape = [
        low(*tokens.shape), wide(*in_grad.shape), wide(1, *enc_grad.shape), wide(*qkv.shape), wide(cols, rows),
        wide(rows, cols), wide(*pair.shape), wide(cols, rows), wide(rows, hidden), wide(hidden, rows),
        wide(3, width), wide(3, width),
    ]
    return pl.pallas_call(
        functools.partial(finish_kernel, len(parts)),
        out_shape=out_shape,
        in_specs=[ANY_SPEC] * len(parts),
        out_specs=[VMEM_SPEC] * len(out_shape),
        scratch_shapes=scratch_like(parts) + [pltpu.SemaphoreType.DMA((len(parts),))],
        compiler_params=pltpu.CompilerParams(vmem_limit_bytes=62 * MIB),
        name="finish",
    )(*parts)


def width_orders(outer, width):
    def spread(values_in):
        if outer == 1:
            return values_in
        parts = values_in.reshape(values_in.shape[:-1] + (outer, RING * 2, -1))
        return jnp.swapaxes(parts, -3, -2).reshape(values_in.shape)

    def back(values_in):
        if outer == 1:
            return values_in
        parts = values_in.reshape(values_in.shape[:-1] + (RING * 2, outer, -1))
        return jnp.swapaxes(parts, -3, -2).reshape(values_in.shape)

    return spread, back


def on_device(
    tokens,
    encoder,
    seg_ids,
    enc_lens,
    attn_qkv,
    attn_out,
    cross_q,
    cross_kv,
    cross_out,
    ffn_in,
    ffn_out,
    norm_gains,
    norm_biases,
    out_grad,
):
    outer = lax.axis_size("o")
    spread, gathered_back = width_orders(outer, tokens.shape[1])
    tokens, encoder, out_grad = spread(tokens), spread(encoder[0]), spread(out_grad)
    norm_gains, norm_biases = spread(norm_gains), spread(norm_biases)
    seq_len = seg_ids.shape[1]
    cols = cross_q.shape[1]
    width = tokens.shape[1]

    def units(block):
        k = block.shape[-1] // cols
        return block.reshape(block.shape[0], k, cols).transpose(1, 0, 2)

    masters = [attn_qkv, attn_out, cross_q, cross_kv, cross_out, ffn_in, ffn_out]
    if outer > 1:
        masters = [
            attn_qkv, attn_out.T[None], cross_q[None], cross_kv, cross_out.T[None], units(ffn_in), units(ffn_out.T)
        ]
        masters = [lax.all_gather(m.astype(low_type), "o", axis=1, tiled=True) for m in masters]
    rows = cross_q.shape[0] * outer
    units_of = (3, 1, 1, 2, 1, ffn_in.shape[1] // cols, ffn_in.shape[1] // cols)
    window = min(seq_len, seq_len // 2 + BLOCK)
    (
        grads_three, qkv_w, out_w, query_w, pair_w, back_w, up_w, down_w, rows_one, enc_full, queries_one, pair_one,
        context_one, lse_one, residual_one, rows_two, queries_two, pair_two, context_two, lse_two, residual_two,
        rows_three, active, slope,
    ) = forward(
        seg_ids, norm_gains, norm_biases, enc_lens, tokens, out_grad, encoder, masters, (rows, cols, units_of), window
    )
    down_sum, up_sum, small, out_tokens, grad_two, back_grad, grad_queries, grad_pair, late_grad = back_one(
        enc_lens, norm_gains, lse_two, down_w, up_w, active, slope, grads_three, rows_three, residual_two,
        queries_two, pair_two, context_two, back_w, rows, cols,
    )
    late_sum, back_sum, query_sum, pair_sum, out_sum, qkv_sum, small, in_grad, enc_grad = back_two(
        seg_ids, norm_gains, lse_one, small,
        [
            grad_queries, grad_pair, rows_two, enc_full, query_w, pair_w, back_grad, grad_two, residual_one,
            context_one, out_w, queries_one, pair_one, rows_one, qkv_w, tokens, late_grad,
        ],
        rows, cols, window, encoder.shape[0],
    )
    if outer == 1:
        return tuple(
            finish(
                out_tokens, in_grad, enc_grad, small, up_sum, late_sum, down_sum, back_sum, query_sum, pair_sum,
                out_sum, qkv_sum,
            )
        )
    enc_grad = enc_grad[None]
    up_sum = jnp.concatenate([up_sum, late_sum], axis=0)
    sums = [up_sum, down_sum, back_sum, query_sum, pair_sum, out_sum, qkv_sum]
    small = small[-1]
    small = lax.psum(small, "o")
    sums = [lax.psum_scatter(s, "o", scatter_dimension=1, tiled=True) for s in sums]
    up_sum, down_sum, back_sum, query_sum, pair_sum, out_sum, qkv_sum = sums

    def joined(block):
        return block.transpose(1, 0, 2).reshape(block.shape[1], -1)

    return (
        gathered_back(out_tokens),
        gathered_back(in_grad),
        gathered_back(enc_grad),
        qkv_sum,
        out_sum[0].T,
        query_sum[0],
        pair_sum,
        back_sum[0].T,
        joined(up_sum),
        joined(down_sum).T,
        gathered_back(small[:3]),
        gathered_back(small[3:6]),
    )


def solution(mesh):
    count, tensor = mesh.devices.shape
    outer = count // (RING * 2)
    fine = Mesh(
        mesh.devices.reshape(outer, RING, 2, tensor // 2, 2), ("o", "z", "y", "x", "c")
    )
    dp, tp = ("o", "z", "y"), ("x", "c")
    in_specs = (
        P(dp + tp, None),
        P(dp, tp, None),
        P(dp, None),
        P(dp),
        P(None, dp, tp),
        P(tp, dp),
        P(dp, tp),
        P(None, dp, tp),
        P(tp, dp),
        P(dp, tp),
        P(tp, dp),
        P(),
        P(),
        P(dp + tp, None),
    )
    out_specs = (
        P(dp + tp, None),
        P(dp + tp, None),
        P(dp, tp, None),
        P(None, dp, tp),
        P(tp, dp),
        P(dp, tp),
        P(None, dp, tp),
        P(tp, dp),
        P(dp, tp),
        P(tp, dp),
        P(),
        P(),
    )
    return jax.shard_map(
        on_device, mesh=fine, in_specs=in_specs, out_specs=out_specs, check_vma=False
    )
```

```python
import functools

import jax
import jax.numpy as jnp
from jax import lax
from jax.experimental import pallas as pl
from jax.experimental.pallas import tpu as pltpu
from jax.sharding import Mesh
from jax.sharding import PartitionSpec as P

HD = 64
DOCS = 4
LANES = 128
PAIR = 2 * HD
RING = 4
epsilon = 1e-05
masked_score = -1e30
MESH = pl.DeviceIdType.MESH
low_type = jnp.bfloat16
f32 = jnp.float32
MIB = 1 << 20


def matmul(left, right):
    return jnp.dot(left, right, preferred_element_type=f32)


def inner_rows(left, right):
    return lax.dot_general(left, right, (((0,), (0,)), ((), ())), preferred_element_type=f32)


def outer_cols(left, right):
    return lax.dot_general(left, right, (((1,), (1,)), ((), ())), preferred_element_type=f32)


def norm_forward(values_in, gain_row, bias_row):
    average = jnp.mean(values_in, axis=-1, keepdims=True)
    centred = values_in - average
    inverse = lax.rsqrt(jnp.mean(centred * centred, axis=-1, keepdims=True) + epsilon)
    unit_rows = centred * inverse
    return (unit_rows * gain_row + bias_row, unit_rows, inverse)


def norm_backward(incoming, unit_rows, inverse, gain_row):
    scaled = incoming * gain_row
    first_mean = jnp.mean(scaled, axis=-1, keepdims=True)
    second_mean = jnp.mean(scaled * unit_rows, axis=-1, keepdims=True)
    result = inverse * (scaled - first_mean - unit_rows * second_mean)
    return (result, jnp.sum(incoming * unit_rows, axis=0), jnp.sum(incoming, axis=0))


class Place:
    def __init__(self):
        self.z = lax.axis_index("z")
        self.y = lax.axis_index("y")
        self.x = lax.axis_index("x")
        self.c = lax.axis_index("c")

    def to(self, which):
        if which == "x":
            return {"x": 1 - self.x}
        if which == "y":
            return {"y": 1 - self.y}
        if which == "c":
            return {"c": 1 - self.c}
        if which == "z1":
            return {"z": self.z + 1 - 2 * lax.rem(self.z, 2)}
        if which == "z2":
            return {"z": lax.rem(self.z + 2, RING)}
        if which == "down":
            return {"z": lax.rem(self.z + RING - 1, RING)}
        return {"z": lax.rem(self.z + 1, RING)}

    def ring(self, step):
        return lax.rem(self.z + step, RING)


def greet(place, names):
    barrier = pltpu.get_barrier_semaphore()
    for name in names:
        pl.semaphore_signal(barrier, inc=1, device_id=place.to(name), device_id_type=MESH)
    pl.semaphore_wait(barrier, len(names))


class Copies:
    def __init__(self, send_sems, recv_sems):
        self.send_sems, self.recv_sems = send_sems, recv_sems
        self.made = []

    def start(self, place, src, dst, which):
        at = len(self.made)
        copy = pltpu.make_async_remote_copy(
            src_ref=src,
            dst_ref=dst,
            send_sem=self.send_sems.at[at],
            recv_sem=self.recv_sems.at[at],
            device_id=place.to(which),
            device_id_type=MESH,
        )
        copy.start()
        self.made.append(copy)
        return copy

    def finish(self):
        for copy in self.made:
            copy.wait_send()


FORWARD_ORDERS = (
    "yzx", "zxy", "yzx", "xzy",
    "xzy", "yzx", "yzx", "zxy",
    "zy", "zy", "zy", "yz",
    "zy", "zy", "zy", "zy",
)


def gather_unit(order, place, whole, base, rows, cols, copies):
    x, y = place.x, place.y

    def at(step, both_y, both_x):
        first = place.ring(step) * 2
        row = first * rows if both_y else (first + y) * rows
        col = base if both_x else base + x * cols
        return whole.at[
            pl.ds(pl.multiple_of(row, rows), rows * (2 if both_y else 1)),
            pl.ds(pl.multiple_of(col, LANES), cols * (2 if both_x else 1)),
        ]

    def send(where, which):
        return copies.start(place, where, where, which)

    if len(order) == 2:
        yield from gather_flat(order, place, whole, base, rows, cols, send)
        return
    mine = at(0, False, False)
    if order in ("xzy", "yzx"):
        axis, last = order[0], order[2]
        wide = dict(both_y=axis == "y", both_x=axis == "x")
        first = send(mine, axis)
        yield
        first.wait_recv()
        hop = send(at(0, **wide), "down")
        ends = [send(at(0, **wide), last)]
        yield
        for step in range(1, RING):
            hop.wait_recv()
            if step < RING - 1:
                hop = send(at(step, **wide), "down")
            ends.append(send(at(step, **wide), last))
            yield
        for copy in ends:
            copy.wait_recv()
    else:
        mid, last = order[1], order[2]
        wide = dict(both_y=mid == "y", both_x=mid == "x")
        hop = send(mine, "down")
        mids = [send(mine, mid)]
        ends = []
        yield
        for step in range(1, RING + 1):
            if step < RING:
                hop.wait_recv()
                if step < RING - 1:
                    hop = send(at(step, False, False), "down")
                mids.append(send(at(step, False, False), mid))
            mids[step - 1].wait_recv()
            ends.append(send(at(step - 1, **wide), last))
            yield
        for copy in ends:
            copy.wait_recv()


class Paced:
    def __init__(self, groups, pace):
        self.groups, self.pace = [list(g) for g in groups], pace
        self.live, self.budget = [], 0.0

    def advance(self):
        unit = self.live.pop(0)
        try:
            next(unit)
            self.live.append(unit)
        except StopIteration:
            pass

    def begin(self):
        for unit in self.groups.pop(0):
            next(unit)
            self.live.append(unit)

    def spend(self, time):
        self.budget += time
        while self.budget >= self.pace:
            self.budget -= self.pace
            if self.live:
                self.advance()

    def drain(self):
        while self.live:
            self.advance()


PACE = 3.2
FLAT_PACE = 1.4
FLOW_PACE = 1.5
DEPTH = 7


class Flow:
    def __init__(self, units, pace, depth):
        self.waiting, self.pace, self.depth = list(units), pace, depth
        self.live, self.budget, self.done = [], 0.0, []

    def fill(self):
        while self.waiting and len(self.live) < self.depth:
            unit = self.waiting.pop(0)
            next(unit)
            self.live.append(unit)

    def advance(self):
        self.fill()
        unit = self.live.pop(0)
        try:
            next(unit)
            self.live.append(unit)
        except StopIteration:
            self.done.append(unit)
            self.fill()

    def spend(self, time):
        self.budget += time
        while self.budget >= self.pace:
            self.budget -= self.pace
            if self.live or self.waiting:
                self.advance()

    def until(self, units):
        while any(all(u is not d for d in self.done) for u in units):
            self.advance()

    def drain(self):
        while self.live or self.waiting:
            self.advance()


class Locals:
    def __init__(self, sems):
        self.sems, self.made = sems, []

    def start(self, src, dst):
        copy = pltpu.make_async_copy(src, dst, self.sems.at[len(self.made)])
        copy.start()
        self.made.append(copy)
        return len(self.made) - 1

    def wait(self, *which):
        for at in which:
            if self.made[at] is not None:
                self.made[at].wait()
                self.made[at] = None

    def finish(self):
        self.wait(*range(len(self.made)))


def gather_flat(order, place, whole, base, rows, cols, send):
    def at(step, both_y):
        first = place.ring(step) * 2
        row = first * rows if both_y else (first + place.y) * rows
        return whole.at[
            pl.ds(pl.multiple_of(row, rows), rows * (2 if both_y else 1)), pl.ds(base, cols)
        ]

    both, ends = order == "yz", []
    if both:
        first = send(at(0, False), "y")
        yield
        first.wait_recv()
    for step in range(RING):
        if step:
            hop.wait_recv()
        if step < RING - 1:
            hop = send(at(step, both), "down")
        if not both:
            ends.append(send(at(step, False), "y"))
        yield
    for copy in ends:
        copy.wait_recv()


def is_flat(which):
    return which >= 5


def own_block(place, which, whole, unit, rows, cols):
    col = unit * cols if is_flat(which) else unit * 2 * cols + place.x * cols
    return whole.at[
        pl.ds(pl.multiple_of((place.z * 2 + place.y) * rows, rows), rows),
        pl.ds(pl.multiple_of(col, LANES), cols),
    ]


def gather_groups(place, sizes, whole, copies, orders):
    rows, cols, units_of = sizes
    units = [
        gather_unit(
            order, place, whole[which], unit * cols * (1 if is_flat(which) else 2), rows, cols, copies
        )
        for (which, unit), order in zip(
            ((w, u) for w, count in enumerate(units_of) for u in range(count)), orders, strict=True
        )
    ]
    return [units[k : k + 4] for k in range(0, len(units), 4)]


def place_own(place, sizes, which, master, whole):
    rows, cols, units_of = sizes
    for unit in range(units_of[which]):
        if len(master.shape) == 3:
            block = master[unit]
        elif master.shape[0] == rows:
            block = master[:, unit * cols : (unit + 1) * cols]
        else:
            block = master[unit * cols : (unit + 1) * cols].T
        own_block(place, which, whole, unit, rows, cols)[...] = block.astype(low_type)


ANY_SPEC = pl.BlockSpec(memory_space=pl.ANY)
VMEM_SPEC = pl.BlockSpec(memory_space=pltpu.VMEM)


def norm_rows(values_in, gain_row, bias_row):
    return norm_forward(values_in, gain_row, bias_row)[0]


def loop_rows(count, tile, body):
    @pl.loop(0, count // tile)
    def _(i):
        body(pl.ds(pl.multiple_of(i * tile, tile), tile))


def exchange_rows(place, copies, n, sent, landed, make):
    theirs = pl.ds(pl.multiple_of((1 - place.c) * n, LANES), n)
    sent[...] = make(theirs).astype(low_type)
    return copies.start(place, sent, landed, "c")


def own_tiles(place, n, body):
    @pl.loop(0, n // LANES)
    def _(i):
        tile = pl.ds(pl.multiple_of(i * LANES, LANES), LANES)
        body(tile, pl.ds(pl.multiple_of(place.c * n + i * LANES, LANES), LANES))


def blocks_of(place, rows_count, pair_count, span):
    def at(block):
        rows = pl.ds(pl.multiple_of(block * BLOCK, BLOCK), BLOCK)
        if span == pair_count:
            return rows, 0
        ends = (place.x * (rows_count // BLOCK) + block + 1) * BLOCK
        return rows, pl.multiple_of(jnp.maximum(ends - span, 0), BLOCK)

    return at


def fill_biases(place, bias, segment, span):
    count = segment.shape[1]
    ids = segment[...].astype(f32)
    half = count // 2
    for block in range(bias.shape[0]):
        first = place.x * half + block * BLOCK
        mine = segment[:, pl.ds(pl.multiple_of(first, BLOCK), BLOCK)].astype(f32)
        lows = jnp.zeros(mine.shape, f32)
        for doc in range(DOCS - 1):
            size = jnp.sum(jnp.where(ids == doc, 1.0, 0.0), axis=1, keepdims=True)
            lows += jnp.where(mine > doc, size, 0.0)
        start = jnp.maximum(first + BLOCK - span, 0)
        keys = lax.broadcasted_iota(jnp.int32, bias.shape[1:], 0)
        rows = first - start + lax.broadcasted_iota(jnp.int32, bias.shape[1:], 1)
        seen = (keys.astype(f32) >= lows - start.astype(f32)) & (keys <= rows)
        bias[block] = jnp.where(seen, 0.0, masked_score)


def fill_enc_bias(bias, length):
    keys = lax.broadcasted_iota(jnp.int32, bias.shape, 0)
    bias[...] = jnp.where(keys < length, 0.0, masked_score)


def forward_kernel(sizes, window, n_out, *refs):
    n_weights = len(sizes[2])
    segment, gains, biases, enc_length, tokens_in, g_own, enc_own, *master_in = refs[: 7 + n_weights]
    at = 7 + n_weights
    g_all, *outs = refs[at : at + n_out]
    at += n_out
    held = refs[at : at + n_out - 1]
    at += n_out - 1
    masters = refs[at : at + n_weights]
    tokens, sent, landed, bias_one, bias_two, send_sems, recv_sems, local_sems = refs[at + n_weights :]
    whole = held[:n_weights]
    (
        rows_one, enc_all, q_one, pair_one, context_one, lse_one, residual_one, rows_two, q_two, pair_two,
        context_two, lse_two, residual_two, rows_three, active, slope,
    ) = held[n_weights:]
    qkv_w, out_w, query_w, pair_w, back_w, up_w, _ = whole
    place = Place()
    copies = Copies(send_sems, recv_sems)
    local = Locals(local_sems)
    x, c = place.x, place.c
    n, e = tokens.shape[0], enc_own.shape[0]
    heads_width = q_one.shape[1]
    mine = pl.ds(pl.multiple_of(c * n, 16), n)
    tokens_at = local.start(tokens_in, tokens)
    masters_at = [local.start(src, dst) for src, dst in zip(master_in, masters)]

    def flush(*names):
        for ref in names:
            local.start(ref, outs[[h is ref for h in held].index(True)])

    def part_of(ref, xx, cc, size):
        return ref.at[pl.ds(pl.multiple_of((xx * 2 + cc) * size, 16), size)]

    enc_at = local.start(enc_own, part_of(enc_all, x, c, e))
    local.start(g_own, part_of(g_all, x, c, n))
    greet(place, ("x", "y", "c", "down", "up"))
    local.wait(tokens_at)
    h_own = part_of(rows_one, x, c, n)

    @pl.loop(0, n // LANES)
    def _(i):
        tile = pl.ds(pl.multiple_of(i * LANES, LANES), LANES)
        normed = norm_rows(tokens[tile].astype(f32), gains[0:1], biases[0:1])
        rows_one[pl.ds(pl.multiple_of((x * 2 + c) * n + i * LANES, LANES), LANES)] = normed.astype(low_type)

    hx = copies.start(place, h_own, h_own, "x")
    hc = copies.start(place, h_own, h_own, "c")
    orders = FORWARD_ORDERS
    groups = gather_groups(place, sizes, whole, copies, orders)

    def rows_unit(own_x, own_c, ref, size, also):
        yield
        yield
        own_x.wait_recv()
        far = part_of(ref, 1 - x, c, size)
        over = copies.start(place, far, far, "c")
        yield
        yield
        for copy in (own_c, over, *also):
            copy.wait_recv()

    groups[0].append(rows_unit(hx, hc, rows_one, n, ()))
    for which in range(n_weights):
        local.wait(masters_at[which])
        place_own(place, sizes, which, masters[which], whole[which])
        if which == 1:
            comm = Flow(groups[0], FLOW_PACE, len(groups[0]))
            comm.fill()
    local.wait(enc_at)
    e_own = part_of(enc_all, x, c, e)
    ex = copies.start(place, e_own, e_own, "x")
    ec = copies.start(place, e_own, e_own, "c")

    def grads_unit():
        gx = copies.start(place, g_own, part_of(g_all, x, c, n), "x")
        gc = copies.start(place, g_own, part_of(g_all, x, c, n), "c")
        yield from rows_unit(gx, gc, g_all, n, ())

    groups[1].append(rows_unit(ex, ec, enc_all, e, ()))
    groups[3].append(grads_unit())
    comm.waiting.extend(groups[1] + groups[2] + groups[3])
    comm.depth = DEPTH
    fill_biases(place, bias_one, segment, window)
    fill_enc_bias(bias_two, enc_length[0])

    def attention(q_ref, pair_ref, bias_of, o_ref, lse_ref, span):
        block_at = blocks_of(place, q_ref.shape[0], pair_ref.shape[0], span)
        for pair in range(heads_width // PAIR):
            comm.spend(4.0)
            lanes = pl.ds(pair * PAIR, PAIR)
            value_lanes = pl.ds(heads_width + pair * PAIR, PAIR)

            @pl.loop(0, q_ref.shape[0] // BLOCK)
            def _(block):
                rows, start = block_at(block)
                here = pl.ds(start, span)
                o_ref[rows, lanes], lse_ref[pair, block] = attend_step(
                    q_ref[rows, lanes],
                    pair_ref[here, lanes],
                    pair_ref[here, value_lanes],
                    bias_of(block),
                )

    def branch(at, context, weight, before, after, gain_at, rows_ref):
        over = exchange_rows(
            place, copies, n, sent.at[at], landed.at[at],
            lambda rows: outer_cols(context[rows], weight[...]),
        )

        after[...] = before[...].astype(f32) + outer_cols(context[mine], weight[...])
        over.wait_recv()

        def rest(tile, rows):
            total = after[tile] + landed[at, tile].astype(f32)
            after[tile] = total
            rows_ref[rows] = norm_rows(
                total, gains[gain_at : gain_at + 1], biases[gain_at : gain_at + 1]
            ).astype(low_type)

        own_tiles(place, n, rest)
        return copies.start(place, rows_ref.at[mine], rows_ref.at[mine], "c")

    comm.until(groups[0])
    flush(rows_one, qkv_w, out_w)

    def project(rows):
        first = pl.ds(pl.multiple_of(x * 2 * n + rows.start, BLOCK), rows.size)
        q_one[rows] = matmul(rows_one[first], qkv_w[:, :heads_width]).astype(low_type)

    loop_rows(2 * n, BLOCK, project)
    comm.spend(2.0)
    loop_rows(
        4 * n, BLOCK, lambda r: store(pair_one, r, matmul(rows_one[r], qkv_w[:, heads_width:]))
    )
    flush(q_one, pair_one)
    comm.spend(4.0)
    attention(q_one, pair_one, lambda block: bias_one[block], context_one, lse_one, window)
    over = branch(0, context_one, out_w, tokens, residual_one, 1, rows_two)
    flush(context_one, lse_one, residual_one)
    comm.spend(5.0)
    comm.until(groups[1])
    loop_rows(
        enc_all.shape[0], BLOCK, lambda r: store(pair_two, r, matmul(enc_all[r], pair_w[...]))
    )
    flush(query_w, pair_w, back_w, enc_all, pair_two)
    over.wait_recv()
    comm.spend(3.0)
    loop_rows(2 * n, BLOCK, lambda r: store(q_two, r, matmul(rows_two[r], query_w[...])))
    flush(rows_two, q_two)
    attention(
        q_two, pair_two, lambda block: bias_two[...], context_two, lse_two, enc_all.shape[0]
    )
    chip = rows_three.at[pl.ds(pl.multiple_of(x * 2 * n, BLOCK), 2 * n)]
    over = branch(1, context_two, back_w, residual_one, residual_two, 2, chip)
    h_three = part_of(rows_three, x, c, n)
    far_over = copies.start(place, h_three, h_three, "x")
    flush(context_two, lse_two, residual_two)
    comm.spend(5.0)
    over.wait_recv()
    comm.until(groups[2])

    def up(chip_at, rows):
        here = pl.ds(pl.multiple_of(chip_at * 2 * n + rows.start, BLOCK), rows.size)
        inner = matmul(rows_three[here], up_w[...])
        gate = 1.0 / (1.0 + jnp.exp(-inner))
        active[here] = (inner * gate).astype(low_type)
        slope[here] = (gate * (1.0 + inner * (1.0 - gate))).astype(low_type)

    loop_rows(2 * n, BLOCK, lambda rows: up(x, rows))
    far_over.wait_recv()
    far = part_of(rows_three, 1 - x, c, n)
    over = copies.start(place, far, far, "c")
    comm.spend(3.0)
    over.wait_recv()
    flush(rows_three, up_w)
    loop_rows(2 * n, BLOCK, lambda rows: up(1 - x, rows))
    flush(active, slope)
    comm.drain()
    flush(whole[-1])
    local.finish()
    copies.finish()


def store(ref, rows, values_in):
    ref[rows] = values_in.astype(ref.dtype)


def low(*shape):
    return jax.ShapeDtypeStruct(shape, low_type)


def wide(*shape):
    return jax.ShapeDtypeStruct(shape, f32)


def scratch_like(shapes):
    return [pltpu.VMEM(s.shape, s.dtype) for s in shapes]


def forward(segment, gains, biases, enc_lens, tokens, g_own, enc_own, masters, sizes, window):
    rows, cols, units_of = sizes
    n, width = tokens.shape
    e = enc_own.shape[0]
    hidden = cols * units_of[-1]
    heads_width = 2 * cols
    n_units = sum(units_of)
    n_copies = 16 + n_units * 11
    lse = wide(heads_width // PAIR, 2 * n // BLOCK, 1, 2 * BLOCK)
    held = [low(width, cols * k * (1 if is_flat(w) else 2)) for w, k in enumerate(units_of)] + [
        low(4 * n, width), low(4 * e, width),
        low(2 * n, heads_width), low(4 * n, 2 * heads_width), low(2 * n, heads_width), lse, wide(n, width),
        low(2 * n, width), low(2 * n, heads_width), low(4 * e, 2 * heads_width), low(2 * n, heads_width), lse,
        wide(n, width), low(4 * n, width), low(4 * n, hidden), low(4 * n, hidden),
    ]
    out_shape = [low(4 * n, width)] + held
    return pl.pallas_call(
        functools.partial(forward_kernel, sizes, window, len(out_shape)),
        out_shape=out_shape,
        in_specs=[VMEM_SPEC] * 3
        + [pl.BlockSpec(memory_space=pltpu.SMEM)]
        + [ANY_SPEC] * (3 + len(masters)),
        out_specs=[ANY_SPEC] * len(out_shape),
        scratch_shapes=scratch_like(held + masters + [tokens])
        + scratch_like([low(2, n, width)] * 2)
        + scratch_like([wide(2 * n // BLOCK, window, BLOCK), wide(4 * e, BLOCK)])
        + [
            pltpu.SemaphoreType.DMA((n_copies,)),
            pltpu.SemaphoreType.DMA((n_copies,)),
            pltpu.SemaphoreType.DMA((3 + len(masters) + len(held),)),
        ],
        compiler_params=pltpu.CompilerParams(
            collective_id=2, has_side_effects=True, vmem_limit_bytes=62 * MIB
        ),
        name="forward",
    )(segment, gains, biases, enc_lens, tokens, g_own, enc_own, *masters)


REDUCE_ORDERS = ("xyz", "xzy", "yxz", "yzx")
CHUNK_ORDER = tuple(range(1, RING)) + (0,)


def reduce_unit(order, place, part, base, rows, cols, recv, out, copies):
    x, y = place.x, place.y

    def at(step, row_of, col_of):
        first = place.ring(step) * 2
        row = first * rows if row_of is None else (first + row_of) * rows
        col = base if col_of is None else base + col_of * cols
        return part.at[
            pl.ds(pl.multiple_of(row, rows), rows * (2 if row_of is None else 1)),
            pl.ds(pl.multiple_of(col, LANES), cols * (2 if col_of is None else 1)),
        ]

    used = [0]

    def landing(shape):
        height = shape[0] * (shape[1] // cols)
        where = [
            recv.at[pl.ds(used[0] + k * shape[0], shape[0])] for k in range(shape[1] // cols)
        ]
        used[0] += height
        return where

    def add(target, source):
        target[...] = target[...] + source[...]

    def exchange(step, which, mid):
        sent = []
        if which == "x":
            if mid:
                spots = [(at(step, y, 1 - x), at(step, y, x))]
            else:
                spots = [(at(step, None, 1 - x), at(step, None, x))]
        else:
            if mid:
                spots = [(at(step, 1 - y, x), at(step, y, x))]
            else:
                spots = [(at(step, 1 - y, k), at(step, y, k)) for k in range(2)]
        for src, keep_at in spots:
            (land,) = landing((src.shape[0], cols))
            sent.append((copies.start(place, src, land, which), keep_at, land))
        return sent

    def take(sent):
        for copy, keep_at, land in sent:
            copy.wait_recv()
            add(keep_at, land)

    def ring_hop(step, spots, ready, arrived):
        if step in ready:
            take(ready[step])
        for (copy, land), spot in zip(arrived or [], spots):
            copy.wait_recv()
            add(spot, land)
        sent = []
        if step != 0:
            for spot in spots:
                (land,) = landing((spot.shape[0], cols))
                sent.append((copies.start(place, spot, land, "down"), land))
        return sent

    first, middle, last = order
    outer, inner = {}, {}
    for step in CHUNK_ORDER[:2]:
        outer[step] = exchange(step, first, False)
    yield
    hop = None
    for k, step in enumerate(CHUNK_ORDER):
        take(outer[step])
        if k + 2 < RING:
            outer[CHUNK_ORDER[k + 2]] = exchange(CHUNK_ORDER[k + 2], first, False)
        if last == "z":
            inner[step] = exchange(step, middle, True)
            if k > 0:
                hop = ring_hop(CHUNK_ORDER[k - 1], [at(CHUNK_ORDER[k - 1], y, x)], inner, hop)
        else:
            if first == "x":
                spots = [at(step, None, x)]
            else:
                spots = [at(step, y, half) for half in range(2)]
            hop = ring_hop(step, spots, {}, hop)
        yield
    if last == "z":
        take(inner[0])
        ((copy, land),) = hop
    else:
        src = at(0, 1 - y, x) if last == "y" else at(0, y, 1 - x)
        (land,) = landing((rows, cols))
        copy = copies.start(place, src, land, last)
        yield
    copy.wait_recv()
    out[...] = at(0, y, x)[...].astype(f32) + land[...].astype(f32)


def reduce_flat(order, place, part, base, rows, cols, recv, out, copies):
    y = place.y

    def at(step, both_y, row_of=y):
        first = place.ring(step) * 2
        row = first * rows if both_y else (first + row_of) * rows
        return part.at[
            pl.ds(pl.multiple_of(row, rows), rows * (2 if both_y else 1)), pl.ds(base, cols)
        ]

    used = [0]

    def send(src, which):
        land = recv.at[pl.ds(used[0], src.shape[0])]
        used[0] += src.shape[0]
        return copies.start(place, src, land, which), land

    def add(target, sent):
        copy, land = sent
        copy.wait_recv()
        target[...] = target[...] + land[...]

    both = order == "zy"
    outer, hop = {}, None
    if not both:
        for step in CHUNK_ORDER[:2]:
            outer[step] = send(at(step, False, 1 - y), "y")
        yield
    for k, step in enumerate(CHUNK_ORDER):
        spot = at(step, both)
        if not both:
            add(spot, outer[step])
            if k + 2 < RING:
                ahead = CHUNK_ORDER[k + 2]
                outer[ahead] = send(at(ahead, False, 1 - y), "y")
        if step != 0:
            if hop is not None:
                add(spot, hop)
            hop = send(spot, "down")
            yield
    if both:
        add(at(0, True), hop)
        hop = send(at(0, False, 1 - y), "y")
        yield
    copy, land = hop
    copy.wait_recv()
    out[...] = at(0, False)[...].astype(f32) + land[...].astype(f32)


def flat_group(place, rows, cols, part, recv, outs, copies, first, orders):
    return [
        reduce_flat(order, place, part, unit * cols, rows, cols, recv.at[first + unit], outs[unit], copies)
        for unit, order in enumerate(orders)
    ]


def reduce_group(place, rows, cols, part, recv, outs, copies, first, orders):
    return [
        reduce_unit(
            order, place, part, unit * 2 * cols, rows, cols, recv.at[first + unit], outs[unit], copies
        )
        for unit, order in enumerate(orders)
    ]


def attention_back(place, comm, q_ref, pair_ref, bias_of, o_ref, do_ref, lse_ref, span, dk_sum, dv_sum, pairs):
    heads_width = q_ref.shape[1]
    block_at = blocks_of(place, q_ref.shape[0], pair_ref.shape[0], span)
    for pair in pairs:
        lanes = pl.ds(pair * PAIR, PAIR)
        value_lanes = pl.ds(heads_width + pair * PAIR, PAIR)
        dk_sum[...] = jnp.zeros_like(dk_sum)
        dv_sum[...] = jnp.zeros_like(dv_sum)

        @pl.loop(0, q_ref.shape[0] // BLOCK)
        def _(block):
            rows, start = block_at(block)
            here = pl.ds(start, span)
            dq, dk, dv = attend_back_step(
                q_ref[rows, lanes],
                pair_ref[here, lanes],
                pair_ref[here, value_lanes],
                bias_of(block),
                o_ref[rows, lanes],
                do_ref[rows, lanes],
                lse_ref[pair, block],
            )
            q_ref[rows, lanes] = dq
            dk_sum[here] += dk
            dv_sum[here] += dv

        pair_ref[:, lanes] = dk_sum[...].astype(low_type)
        pair_ref[:, value_lanes] = dv_sum[...].astype(low_type)
        comm.spend(6.0)


def loop_cols(count, tile, body):
    loop_rows(count, tile, body)


def norm_back_tile(small, at, incoming, before, gain_row):
    _, unit_rows, inverse = norm_forward(before, jnp.ones_like(gain_row), jnp.zeros_like(gain_row))
    result, gain_sum, bias_sum = norm_backward(incoming, unit_rows, inverse, gain_row)
    small[at : at + 1] += gain_sum[None]
    small[at + 3 : at + 4] += bias_sum[None]
    return result


def back_one_kernel(sizes, *refs):
    rows, cols = sizes
    (
        enc_length, gains, lse_two,
        down_in, up_in, active_in, slope_in, g_in, rows_in, residual_in, q_in, pair_in, context_in, back_in,
        down_sum, up_sum, small, out_tokens, grad_out, back_out, dq_out, dpair_out,
        down_w, up_w, active, slope, g_all, rows_three, residual, q_two, pair_two, context, back_w,
        part_down, part_up, recv, sent, landed, grad, g_two, back_part, grad_context, tokens_out, dk_sum, dv_sum,
        bias, out_total, send_sems, recv_sems, local_sems,
    ) = refs
    place = Place()
    copies = Copies(send_sems, recv_sems)
    local = Locals(local_sems)
    x, c = place.x, place.c
    g_at, active_at, down_at, slope_at, rows_at, up_at, res_at, con_at, back_at, q_at, pair_at = [
        local.start(src, dst)
        for src, dst in (
            (g_in, g_all), (active_in, active), (down_in, down_w), (slope_in, slope), (rows_in, rows_three),
            (up_in, up_w), (residual_in, residual), (context_in, context), (back_in, back_w),
            (q_in, q_two), (pair_in, pair_two),
        )
    ]
    greet(place, ("x", "y", "c", "down", "up"))
    n, width = residual.shape
    mine = pl.ds(pl.multiple_of(c * n, 16), n)
    comm = Paced(
        [
            flat_group(
                place, rows, cols, part_down, recv, [down_sum.at[k] for k in range(4)], copies, 0,
                ("yz", "zy", "yz", "yz"),
            ),
            flat_group(
                place, rows, cols, part_up, recv, [up_sum.at[k] for k in range(4)], copies, 4,
                ("yz", "yz", "zy", "yz"),
            ),
        ],
        FLAT_PACE,
    )
    small[...] = jnp.zeros_like(small)
    fill_enc_bias(bias, enc_length[0])

    def on_chip(chip, local_rows):
        return pl.ds(pl.multiple_of(chip * 2 * n + local_rows.start, LANES), local_rows.size)

    local.wait(g_at, down_at, slope_at)

    def inner(tile):
        slope[tile] = (matmul(g_all[tile], down_w[...]) * slope[tile].astype(f32)).astype(low_type)

    loop_rows(4 * n, BLOCK, inner)
    local.wait(up_at)

    def up_term(chip, local_rows):
        return outer_cols(slope[on_chip(chip, local_rows)], up_w[...])

    def down_term(chip, local_rows):
        return outer_cols(active[on_chip(chip, local_rows)], down_w[...])

    far_over = exchange_rows(
        place, copies, n, sent.at[0], landed.at[0], lambda r: up_term(1 - x, r)
    )
    near_over = exchange_rows(place, copies, n, sent.at[1], landed.at[1], lambda r: up_term(x, r))
    grad[...] = up_term(x, mine)
    far_over.wait_recv()
    sent[2] = (up_term(1 - x, mine) + landed[0].astype(f32)).astype(low_type)
    chip_over = copies.start(place, sent.at[2], landed.at[2], "x")
    local.wait(active_at)
    loop_cols(width, BLOCK, lambda t: store(part_down, t, inner_rows(g_all[:, t], active[...])))
    comm.begin()
    local.wait(rows_at)
    loop_cols(width, BLOCK, lambda t: store(part_up, t, inner_rows(rows_three[:, t], slope[...])))
    comm.spend(4.8)
    comm.begin()
    out_far = exchange_rows(
        place, copies, n, sent.at[3], landed.at[3], lambda r: down_term(1 - x, r)
    )
    out_near = exchange_rows(place, copies, n, sent.at[4], landed.at[4], lambda r: down_term(x, r))
    local.wait(res_at)
    out_total[...] = residual[...] + down_term(x, mine)
    comm.spend(3.0)
    out_far.wait_recv()
    sent[5] = (down_term(1 - x, mine) + landed[3].astype(f32)).astype(low_type)
    out_chip = copies.start(place, sent.at[5], landed.at[5], "x")
    comm.spend(1.5)
    near_over.wait_recv()
    chip_over.wait_recv()

    def norm_part(tile, rows_here):
        incoming = grad[tile] + landed[1, tile].astype(f32) + landed[2, tile].astype(f32)
        total = g_all[on_chip(x, rows_here)].astype(f32) + norm_back_tile(
            small, 2, incoming, residual[tile], gains[2:3]
        )
        grad[tile] = total
        g_two[rows_here] = total.astype(low_type)

    own_tiles(place, n, norm_part)
    g_over = copies.start(place, g_two.at[mine], g_two.at[mine], "c")
    local.start(grad, grad_out)
    comm.spend(5.5)
    local.wait(con_at, back_at)
    g_over.wait_recv()
    loop_rows(2 * n, BLOCK, lambda r: store(grad_context, r, matmul(g_two[r], back_w[...])))
    loop_cols(width, BLOCK, lambda t: store(back_part, t, inner_rows(g_two[:, t], context[...])))
    local.start(back_part, back_out)
    comm.spend(3.0)
    local.wait(q_at, pair_at)
    attention_back(
        place, comm, q_two, pair_two, lambda block: bias[...], context, grad_context, lse_two, pair_two.shape[0], dk_sum, dv_sum, range(q_two.shape[1] // PAIR),
    )
    local.start(q_two, dq_out)
    local.start(pair_two, dpair_out)
    out_near.wait_recv()
    out_chip.wait_recv()
    tokens_out[...] = (out_total[...] + landed[4].astype(f32) + landed[5].astype(f32)).astype(low_type)
    local.start(tokens_out, out_tokens)
    comm.drain()
    local.finish()
    copies.finish()


def back_one(enc_lens, gains, lse_two, down_w, up_w, active, slope, g_all, rows_three, residual, q_two, pair_two, context, back_w, rows, cols):
    n, width = residual.shape
    heads_width = q_two.shape[1]
    hbm = [down_w, up_w, active, slope, g_all, rows_three, residual, q_two, pair_two, context, back_w]
    out_shape = [
        wide(4, rows, cols), wide(4, rows, cols), wide(8, width), low(n, width), wide(n, width),
        low(width, heads_width), low(2 * n, heads_width), low(*pair_two.shape),
    ]
    n_copies = 8 * 7 + 8
    return pl.pallas_call(
        functools.partial(back_one_kernel, (rows, cols)),
        out_shape=out_shape,
        in_specs=[pl.BlockSpec(memory_space=pltpu.SMEM)] + [VMEM_SPEC] * 2 + [ANY_SPEC] * len(hbm),
        out_specs=[VMEM_SPEC] * 3 + [ANY_SPEC] * 5,
        scratch_shapes=scratch_like(hbm)
        + scratch_like(
            [
                low(*down_w.shape), low(*up_w.shape), low(8, rows * 7, cols), low(6, n, width),
                low(6, n, width), wide(n, width), low(2 * n, width), low(width, heads_width),
                low(2 * n, heads_width), low(n, width), wide(pair_two.shape[0], PAIR), wide(pair_two.shape[0], PAIR),
                wide(pair_two.shape[0], BLOCK), wide(n, width),
            ]
        )
        + [
            pltpu.SemaphoreType.DMA((n_copies,)),
            pltpu.SemaphoreType.DMA((n_copies,)),
            pltpu.SemaphoreType.DMA((len(hbm) + 5,)),
        ],
        compiler_params=pltpu.CompilerParams(
            collective_id=1, has_side_effects=True, vmem_limit_bytes=60 * MIB
        ),
        name="back_one",
    )(enc_lens, gains, lse_two, *hbm)


def back_two_kernel(sizes, window, *refs):
    rows, cols = sizes
    (
        segment, gains, lse_one, small_in,
        dq_in, dpair_in, rows_two_in, enc_in, query_in, pair_w_in, back_in, grad_in, residual_in, context_in,
        out_w_in, q_in, pair_in, rows_one_in, qkv_in, tokens_in,
        back_sum, query_sum, pair_sum, out_sum, qkv_sum, small_out, in_grad, enc_grad,
        dq_two, dpair_two, grad, residual, context, out_w, q_one, pair_one, tokens,
        rows_held, qkv_w, part_cross, part_out, part_half, recv, sent, landed, total, g_one, grad_context, dk_sum, dv_sum,
        enc_sent, enc_landed, enc_total, small_recv, bias, send_sems, recv_sems, local_sems,
    ) = refs
    place = Place()
    copies = Copies(send_sems, recv_sems)
    local = Locals(local_sems)
    x, c = place.x, place.c
    n, width = residual.shape
    heads_width = q_one.shape[1]
    e = enc_grad.shape[0]
    enc_all = rows_held.at[pl.ds(0, enc_in.shape[0])]
    rows_two = rows_held.at[pl.ds(enc_in.shape[0], 2 * n)]
    rows_one = rows_held.at[pl.ds(0, rows_one_in.shape[0])]
    query_w = qkv_w.at[:, pl.ds(0, heads_width)]
    pair_w = qkv_w.at[:, pl.ds(heads_width, 2 * heads_width)]
    (
        dpair_at, enc_at, dq_at, rows_two_at, back_at, query_at, pair_w_at, grad_at, res_at, con_at,
        out_w_at, q_at, pair_at, tokens_at,
    ) = [
        local.start(src, dst)
        for src, dst in (
            (dpair_in, dpair_two), (enc_in, enc_all), (dq_in, dq_two),
            (rows_two_in, rows_two), (back_in, part_cross.at[:, pl.ds(0, heads_width)]), (query_in, query_w),
            (pair_w_in, pair_w), (grad_in, grad), (residual_in, residual), (context_in, context),
            (out_w_in, out_w), (q_in, q_one), (pair_in, pair_one), (tokens_in, tokens),
        )
    ]
    greet(place, ("x", "y", "c", "down", "up", "z2"))
    mine = pl.ds(pl.multiple_of(c * n, 16), n)

    def small_unit():
        for at, which in enumerate(("c", "x", "y", "z1", "z2")):
            copy = copies.start(place, small_out.at[at], small_recv.at[at], which)
            yield
            copy.wait_recv()
            small_out[at + 1] = small_out[at] + small_recv[at]

    cross_sums = [back_sum.at[0], query_sum.at[0], pair_sum.at[0], pair_sum.at[1]]
    half = cols // 2

    def half_group(which, orders):
        lanes = pl.ds(which * half, half)
        return [
            reduce_unit(
                order, place, part_half.at[which], unit * cols, rows, half, recv.at[5 + unit, :, lanes],
                qkv_sum.at[unit, :, lanes], copies,
            )
            for unit, order in enumerate(orders)
        ]

    comm = Paced(
        [
            reduce_group(
                place, rows, cols, part_cross, recv, cross_sums, copies, 0, ("yxz", "yzx", "xzy", "yzx")
            ),
            reduce_group(place, rows, cols, part_out, recv, [out_sum.at[0]], copies, 4, ("yzx",)),
            half_group(0, ("yzx", "yzx", "xzy")),
            half_group(1, ("yxz", "yzx", "xzy")),
            [small_unit()],
        ],
        PACE,
    )
    small = small_out.at[0]
    small[...] = small_in[...]
    second = pl.ds(heads_width, heads_width)
    rest = pl.ds(2 * heads_width, 2 * heads_width)
    fill_biases(place, bias, segment, window)
    local.wait(dpair_at, enc_at)

    def pair_grads(t):
        part_cross[t, rest] = inner_rows(enc_all[:, t], dpair_two[...]).astype(low_type)

    loop_cols(width, BLOCK, pair_grads)
    comm.spend(4.0)
    local.wait(dq_at, rows_two_at, back_at)

    def query_grads(t):
        part_cross[t, second] = inner_rows(rows_two[:, t], dq_two[...]).astype(low_type)

    loop_cols(width, BLOCK, query_grads)
    comm.spend(1.5)
    comm.begin()
    rows_one_at = local.start(rows_one_in, rows_one)
    local.wait(query_at)
    over = exchange_rows(
        place, copies, n, sent.at[0], landed.at[0], lambda r: outer_cols(dq_two[r], query_w[...])
    )
    total[...] = outer_cols(dq_two[mine], query_w[...])
    comm.spend(2.2)
    local.wait(pair_w_at)

    def enc_rows(xx, cc):
        return pl.ds(pl.multiple_of((xx * 2 + cc) * e, LANES), e)

    def enc_term(xx, cc):
        return outer_cols(dpair_two[enc_rows(xx, cc)], pair_w[...])

    enc_sent[0] = enc_term(x, 1 - c).astype(low_type)
    enc_sent[1] = enc_term(1 - x, 1 - c).astype(low_type)
    enc_over = copies.start(place, enc_sent.at[pl.ds(0, 2)], enc_landed.at[pl.ds(0, 2)], "c")
    comm.spend(1.6)
    local.wait(grad_at, res_at)
    over.wait_recv()

    def norm_part(tile, rows_here):
        incoming = total[tile] + landed[0, tile].astype(f32)
        after = grad[tile] + norm_back_tile(small, 1, incoming, residual[tile], gains[1:2])
        grad[tile] = after
        g_one[rows_here] = after.astype(low_type)

    own_tiles(place, n, norm_part)
    g_over = copies.start(place, g_one.at[mine], g_one.at[mine], "c")
    comm.spend(4.0)
    enc_over.wait_recv()
    enc_sent[2] = (enc_term(1 - x, c) + enc_landed[1].astype(f32)).astype(low_type)
    enc_far = copies.start(place, enc_sent.at[2], enc_landed.at[2], "x")
    enc_total[...] = enc_term(x, c) + enc_landed[0].astype(f32)
    qkv_at = local.start(qkv_in, qkv_w)
    comm.spend(2.0)
    local.wait(con_at, out_w_at)
    g_over.wait_recv()
    loop_rows(2 * n, BLOCK, lambda r: store(grad_context, r, matmul(g_one[r], out_w[...])))

    def out_grads(t):
        part_out[t] = inner_rows(g_one[:, t], context[...]).astype(low_type)

    loop_cols(width, BLOCK, out_grads)
    comm.spend(2.6)
    comm.begin()
    local.wait(q_at, pair_at)
    n_pairs = heads_width // PAIR

    def self_back(pairs):
        attention_back(
            place, comm, q_one, pair_one, lambda block: bias[block], context, grad_context, lse_one, window,
            dk_sum, dv_sum, pairs,
        )

    chip_rows = pl.ds(pl.multiple_of(x * 2 * n, LANES), 2 * n)

    def self_grads(which):
        spots = [k * cols + which * half for k in range(2)]
        dq = jnp.concatenate([q_one[:, at : at + half] for at in spots], axis=1)
        dpair = jnp.concatenate(
            [pair_one[:, at : at + half] for at in spots + [heads_width + at for at in spots]], axis=1
        )

        def tile(t):
            part_half[which, t, pl.ds(0, cols)] = inner_rows(rows_one[chip_rows, t], dq).astype(low_type)
            part_half[which, t, pl.ds(cols, 2 * cols)] = inner_rows(rows_one[:, t], dpair).astype(low_type)

        loop_cols(width, BLOCK, tile)

    halves = [[p for p in range(n_pairs) if p * PAIR % cols // half == which] for which in range(2)]
    self_back(halves[0])
    local.wait(rows_one_at)
    self_grads(0)
    comm.spend(3.0)
    comm.begin()
    self_back(halves[1])
    enc_far.wait_recv()
    enc_total[...] += enc_landed[2].astype(f32)
    local.start(enc_total, enc_grad)
    local.wait(qkv_at)
    q_lanes, kv_lanes = pl.ds(0, heads_width), pl.ds(heads_width, 2 * heads_width)

    def key_term(xx, local_rows):
        at = pl.ds(pl.multiple_of(xx * 2 * n + local_rows.start, LANES), local_rows.size)
        return outer_cols(pair_one[at], qkv_w[:, kv_lanes])

    def query_term(local_rows):
        return outer_cols(q_one[local_rows], qkv_w[:, q_lanes])

    far_over = exchange_rows(
        place, copies, n, sent.at[1], landed.at[1], lambda r: key_term(1 - x, r)
    )
    near_over = exchange_rows(
        place, copies, n, sent.at[2], landed.at[2], lambda r: key_term(x, r) + query_term(r)
    )
    comm.spend(4.0)
    far_over.wait_recv()
    sent[3] = (key_term(1 - x, mine) + landed[1].astype(f32)).astype(low_type)
    chip_over = copies.start(place, sent.at[3], landed.at[3], "x")
    comm.spend(1.5)
    self_grads(1)
    comm.spend(3.0)
    comm.begin()
    total[...] = key_term(x, mine) + query_term(mine)
    comm.spend(2.0)
    local.wait(tokens_at)
    near_over.wait_recv()
    chip_over.wait_recv()

    def last_part(tile, rows_here):
        incoming = total[tile] + landed[2, tile].astype(f32) + landed[3, tile].astype(f32)
        grad[tile] += norm_back_tile(small, 0, incoming, tokens[tile].astype(f32), gains[0:1])

    own_tiles(place, n, last_part)
    local.start(grad, in_grad)
    comm.begin()
    comm.drain()
    local.finish()
    copies.finish()


def back_two(segment, gains, lse_one, small, hbm, rows, cols, window, enc_rows):
    grad, q_one, pair_one = hbm[7], hbm[11], hbm[12]
    n, width = grad.shape
    heads_width = q_one.shape[1]

    def sums(k):
        return wide(k, rows, cols)

    out_shape = [
        sums(1), sums(1), sums(2), sums(1), sums(3), wide(6, 8, width), wide(n, width), wide(enc_rows, width),
    ]
    n_copies = 11 * 15 + 8 + 5
    held = hbm[:2] + hbm[7:13] + hbm[15:16]
    held_rows = max(enc_rows * 4 + 2 * n, hbm[13].shape[0])
    return pl.pallas_call(
        functools.partial(back_two_kernel, (rows, cols), window),
        out_shape=out_shape,
        in_specs=[VMEM_SPEC] * 4 + [ANY_SPEC] * len(hbm),
        out_specs=[VMEM_SPEC] * 6 + [ANY_SPEC] * 2,
        scratch_shapes=scratch_like(held)
        + scratch_like(
            [
                low(held_rows, width), low(*hbm[14].shape),
                low(width, 4 * heads_width), low(width, heads_width), low(2, width, 3 * cols), low(8, rows * 15, cols),
                low(4, n, width), low(4, n, width), wide(n, width), low(2 * n, width),
                low(2 * n, heads_width), wide(pair_one.shape[0], PAIR), wide(pair_one.shape[0], PAIR),
                low(3, enc_rows, width), low(3, enc_rows, width), wide(enc_rows, width), wide(5, 8, width),
                wide(2 * n // BLOCK, window, BLOCK),
            ]
        )
        + [
            pltpu.SemaphoreType.DMA((n_copies,)),
            pltpu.SemaphoreType.DMA((n_copies,)),
            pltpu.SemaphoreType.DMA((len(hbm) + 2,)),
        ],
        compiler_params=pltpu.CompilerParams(
            collective_id=3, has_side_effects=True, vmem_limit_bytes=62 * MIB
        ),
        name="back_two",
    )(segment, gains, lse_one, small, *hbm)


BLOCK = 256


def split_heads(values_in):
    lane = lax.broadcasted_iota(jnp.int32, values_in.shape, 1)
    zero = jnp.zeros_like(values_in)
    return jnp.concatenate(
        [jnp.where(lane < HD, values_in, zero), jnp.where(lane >= HD, values_in, zero)], axis=0
    )


def key_scores(queries, keys, bias):
    return outer_cols(keys, queries) + jnp.concatenate([bias, bias], axis=1)


def attend_step(q_block, keys, values, bias):
    rows = q_block.shape[0]
    queries = split_heads(q_block * jnp.asarray(HD**-0.5, low_type))
    scores = key_scores(queries, keys, bias)
    peak = jnp.max(scores, axis=0, keepdims=True)
    probs = jnp.exp(scores - peak)
    total = jnp.sum(probs, axis=0, keepdims=True)
    context = inner_rows(values, probs.astype(low_type)) / total
    pair = jnp.concatenate([context[:HD, :rows], context[HD:, rows:]], axis=0)
    return pair.T.astype(low_type), peak + jnp.log(total)


def attend_back_step(q_block, keys, values, bias, context, grad_context, lse):
    rows = q_block.shape[0]
    queries = split_heads(q_block * jnp.asarray(HD**-0.5, low_type))
    grads = split_heads(grad_context)
    scores = key_scores(queries, keys, bias)
    probs = jnp.exp(scores - lse)
    grad_probs = outer_cols(values, grads)
    product = (grad_context.astype(f32) * context.astype(f32)).T
    inner = jnp.concatenate(
        [
            jnp.sum(product[:HD], axis=0, keepdims=True),
            jnp.sum(product[HD:], axis=0, keepdims=True),
        ],
        axis=1,
    )
    grad_scores = (probs * (grad_probs - inner)).astype(low_type)
    dv = matmul(probs.astype(low_type), grads)
    dk = matmul(grad_scores, queries)
    grad_queries = inner_rows(keys, grad_scores) * HD**-0.5
    pair = jnp.concatenate([grad_queries[:HD, :rows], grad_queries[HD:, rows:]], axis=0)
    return pair.T.astype(low_type), dk, dv


def finish_kernel(n_parts, *refs):
    parts, outs, held, sems = refs[:n_parts], refs[n_parts:-1 - n_parts], refs[-1 - n_parts : -1], refs[-1]
    local = Locals(sems)
    for src, dst in zip(parts, held):
        local.start(src, dst)
    local.finish()
    tokens_in, in_grad_in, enc_in, small, up, down, back, query, pair, out, qkv = held
    tokens_out, in_grad, enc_grad, qkv_out, out_out, query_out, pair_out, back_out, up_out, down_out, gain, bias = outs
    cols = up.shape[2]
    tokens_out[...] = tokens_in[...]
    in_grad[...] = in_grad_in[...]
    enc_grad[0] = enc_in[...]
    qkv_out[...] = qkv[...]
    out_out[...] = out[0].T
    query_out[...] = query[0]
    pair_out[...] = pair[...]
    back_out[...] = back[0].T
    for unit in range(up.shape[0]):
        up_out[:, unit * cols : (unit + 1) * cols] = up[unit]
    for unit in range(down.shape[0]):
        down_out[unit * cols : (unit + 1) * cols] = down[unit].T
    gain[...] = small[small.shape[0] - 1, 0:3]
    bias[...] = small[small.shape[0] - 1, 3:6]


def finish(*parts):
    tokens, in_grad, enc_grad, small, up, down, back, query, pair, out, qkv = parts
    rows, cols = up.shape[1:]
    width = small.shape[2]
    hidden = cols * down.shape[0]
    out_shape = [
        low(*tokens.shape), wide(*in_grad.shape), wide(1, *enc_grad.shape), wide(*qkv.shape), wide(cols, rows),
        wide(rows, cols), wide(*pair.shape), wide(cols, rows), wide(rows, hidden), wide(hidden, rows),
        wide(3, width), wide(3, width),
    ]
    return pl.pallas_call(
        functools.partial(finish_kernel, len(parts)),
        out_shape=out_shape,
        in_specs=[ANY_SPEC] * len(parts),
        out_specs=[VMEM_SPEC] * len(out_shape),
        scratch_shapes=scratch_like(parts) + [pltpu.SemaphoreType.DMA((len(parts),))],
        compiler_params=pltpu.CompilerParams(vmem_limit_bytes=62 * MIB),
        name="finish",
    )(*parts)


def width_orders(outer, width):
    def spread(values_in):
        if outer == 1:
            return values_in
        parts = values_in.reshape(values_in.shape[:-1] + (outer, RING * 2, -1))
        return jnp.swapaxes(parts, -3, -2).reshape(values_in.shape)

    def back(values_in):
        if outer == 1:
            return values_in
        parts = values_in.reshape(values_in.shape[:-1] + (RING * 2, outer, -1))
        return jnp.swapaxes(parts, -3, -2).reshape(values_in.shape)

    return spread, back


def on_device(
    tokens,
    encoder,
    seg_ids,
    enc_lens,
    attn_qkv,
    attn_out,
    cross_q,
    cross_kv,
    cross_out,
    ffn_in,
    ffn_out,
    norm_gains,
    norm_biases,
    out_grad,
):
    outer = lax.axis_size("o")
    spread, gathered_back = width_orders(outer, tokens.shape[1])
    tokens, encoder, out_grad = spread(tokens), spread(encoder[0]), spread(out_grad)
    norm_gains, norm_biases = spread(norm_gains), spread(norm_biases)
    seq_len = seg_ids.shape[1]
    cols = cross_q.shape[1]
    width = tokens.shape[1]

    def units(block):
        k = block.shape[-1] // cols
        return block.reshape(block.shape[0], k, cols).transpose(1, 0, 2)

    masters = [attn_qkv, attn_out, cross_q, cross_kv, cross_out, ffn_in, ffn_out]
    if outer > 1:
        masters = [
            attn_qkv, attn_out.T[None], cross_q[None], cross_kv, cross_out.T[None], units(ffn_in), units(ffn_out.T)
        ]
        masters = [lax.all_gather(m.astype(low_type), "o", axis=1, tiled=True) for m in masters]
    rows = cross_q.shape[0] * outer
    units_of = (3, 1, 1, 2, 1, ffn_in.shape[1] // cols, ffn_in.shape[1] // cols)
    window = min(seq_len, seq_len // 2 + BLOCK)
    (
        grads_three, qkv_w, out_w, query_w, pair_w, back_w, up_w, down_w, rows_one, enc_full, queries_one, pair_one,
        context_one, lse_one, residual_one, rows_two, queries_two, pair_two, context_two, lse_two, residual_two,
        rows_three, active, slope,
    ) = forward(
        seg_ids, norm_gains, norm_biases, enc_lens, tokens, out_grad, encoder, masters, (rows, cols, units_of), window
    )
    down_sum, up_sum, small, out_tokens, grad_two, back_grad, grad_queries, grad_pair = back_one(
        enc_lens, norm_gains, lse_two, down_w, up_w, active, slope, grads_three, rows_three, residual_two,
        queries_two, pair_two, context_two, back_w, rows, cols,
    )
    back_sum, query_sum, pair_sum, out_sum, qkv_sum, small, in_grad, enc_grad = back_two(
        seg_ids, norm_gains, lse_one, small,
        [
            grad_queries, grad_pair, rows_two, enc_full, query_w, pair_w, back_grad, grad_two, residual_one,
            context_one, out_w, queries_one, pair_one, rows_one, qkv_w, tokens,
        ],
        rows, cols, window, encoder.shape[0],
    )
    if outer == 1:
        return tuple(
            finish(
                out_tokens, in_grad, enc_grad, small, up_sum, down_sum, back_sum, query_sum, pair_sum,
                out_sum, qkv_sum,
            )
        )
    enc_grad = enc_grad[None]
    sums = [up_sum, down_sum, back_sum, query_sum, pair_sum, out_sum, qkv_sum]
    small = small[-1]
    small = lax.psum(small, "o")
    sums = [lax.psum_scatter(s, "o", scatter_dimension=1, tiled=True) for s in sums]
    up_sum, down_sum, back_sum, query_sum, pair_sum, out_sum, qkv_sum = sums

    def joined(block):
        return block.transpose(1, 0, 2).reshape(block.shape[1], -1)

    return (
        gathered_back(out_tokens),
        gathered_back(in_grad),
        gathered_back(enc_grad),
        qkv_sum,
        out_sum[0].T,
        query_sum[0],
        pair_sum,
        back_sum[0].T,
        joined(up_sum),
        joined(down_sum).T,
        gathered_back(small[:3]),
        gathered_back(small[3:6]),
    )


def solution(mesh):
    count, tensor = mesh.devices.shape
    outer = count // (RING * 2)
    fine = Mesh(
        mesh.devices.reshape(outer, RING, 2, tensor // 2, 2), ("o", "z", "y", "x", "c")
    )
    dp, tp = ("o", "z", "y"), ("x", "c")
    in_specs = (
        P(dp + tp, None),
        P(dp, tp, None),
        P(dp, None),
        P(dp),
        P(None, dp, tp),
        P(tp, dp),
        P(dp, tp),
        P(None, dp, tp),
        P(tp, dp),
        P(dp, tp),
        P(tp, dp),
        P(),
        P(),
        P(dp + tp, None),
    )
    out_specs = (
        P(dp + tp, None),
        P(dp + tp, None),
        P(dp, tp, None),
        P(None, dp, tp),
        P(tp, dp),
        P(dp, tp),
        P(None, dp, tp),
        P(tp, dp),
        P(dp, tp),
        P(tp, dp),
        P(),
        P(),
    )
    return jax.shard_map(
        on_device, mesh=fine, in_specs=in_specs, out_specs=out_specs, check_vma=False
    )
```

```python
import functools

import jax
import jax.numpy as jnp
from jax import lax
from jax.experimental import pallas as pl
from jax.experimental.pallas import tpu as pltpu
from jax.sharding import Mesh
from jax.sharding import PartitionSpec as P

HD = 64
DOCS = 4
LANES = 128
PAIR = 2 * HD
RING = 4
epsilon = 1e-05
masked_score = -1e30
MESH = pl.DeviceIdType.MESH
low_type = jnp.bfloat16
f32 = jnp.float32
MIB = 1 << 20


def matmul(left, right):
    return jnp.dot(left, right, preferred_element_type=f32)


def inner_rows(left, right):
    return lax.dot_general(left, right, (((0,), (0,)), ((), ())), preferred_element_type=f32)


def outer_cols(left, right):
    return lax.dot_general(left, right, (((1,), (1,)), ((), ())), preferred_element_type=f32)


def norm_forward(values_in, gain_row, bias_row):
    average = jnp.mean(values_in, axis=-1, keepdims=True)
    centred = values_in - average
    inverse = lax.rsqrt(jnp.mean(centred * centred, axis=-1, keepdims=True) + epsilon)
    unit_rows = centred * inverse
    return (unit_rows * gain_row + bias_row, unit_rows, inverse)


def norm_backward(incoming, unit_rows, inverse, gain_row):
    scaled = incoming * gain_row
    first_mean = jnp.mean(scaled, axis=-1, keepdims=True)
    second_mean = jnp.mean(scaled * unit_rows, axis=-1, keepdims=True)
    result = inverse * (scaled - first_mean - unit_rows * second_mean)
    return (result, jnp.sum(incoming * unit_rows, axis=0), jnp.sum(incoming, axis=0))


class Place:
    def __init__(self):
        self.z = lax.axis_index("z")
        self.y = lax.axis_index("y")
        self.x = lax.axis_index("x")
        self.c = lax.axis_index("c")

    def to(self, which):
        if which == "x":
            return {"x": 1 - self.x}
        if which == "y":
            return {"y": 1 - self.y}
        if which == "c":
            return {"c": 1 - self.c}
        if which == "z1":
            return {"z": self.z + 1 - 2 * lax.rem(self.z, 2)}
        if which == "z2":
            return {"z": lax.rem(self.z + 2, RING)}
        if which == "down":
            return {"z": lax.rem(self.z + RING - 1, RING)}
        return {"z": lax.rem(self.z + 1, RING)}

    def ring(self, step):
        return lax.rem(self.z + step, RING)


def greet(place, names):
    barrier = pltpu.get_barrier_semaphore()
    for name in names:
        pl.semaphore_signal(barrier, inc=1, device_id=place.to(name), device_id_type=MESH)
    pl.semaphore_wait(barrier, len(names))


class Copies:
    def __init__(self, send_sems, recv_sems):
        self.send_sems, self.recv_sems = send_sems, recv_sems
        self.made = []

    def start(self, place, src, dst, which):
        at = len(self.made)
        copy = pltpu.make_async_remote_copy(
            src_ref=src,
            dst_ref=dst,
            send_sem=self.send_sems.at[at],
            recv_sem=self.recv_sems.at[at],
            device_id=place.to(which),
            device_id_type=MESH,
        )
        copy.start()
        self.made.append(copy)
        return copy

    def finish(self):
        for copy in self.made:
            copy.wait_send()


FORWARD_ORDERS = (
    "yzx", "zxy", "yzx", "xzy",
    "xzy", "yzx", "yzx", "zxy",
    "zy", "zy", "zy", "yz",
    "zy", "zy", "zy", "zy",
)


def gather_unit(order, place, whole, base, rows, cols, copies):
    x, y = place.x, place.y

    def at(step, both_y, both_x):
        first = place.ring(step) * 2
        row = first * rows if both_y else (first + y) * rows
        col = base if both_x else base + x * cols
        return whole.at[
            pl.ds(pl.multiple_of(row, rows), rows * (2 if both_y else 1)),
            pl.ds(pl.multiple_of(col, LANES), cols * (2 if both_x else 1)),
        ]

    def send(where, which):
        return copies.start(place, where, where, which)

    if len(order) == 2:
        yield from gather_flat(order, place, whole, base, rows, cols, send)
        return
    mine = at(0, False, False)
    if order in ("xzy", "yzx"):
        axis, last = order[0], order[2]
        wide = dict(both_y=axis == "y", both_x=axis == "x")
        first = send(mine, axis)
        yield
        first.wait_recv()
        hop = send(at(0, **wide), "down")
        ends = [send(at(0, **wide), last)]
        yield
        for step in range(1, RING):
            hop.wait_recv()
            if step < RING - 1:
                hop = send(at(step, **wide), "down")
            ends.append(send(at(step, **wide), last))
            yield
        for copy in ends:
            copy.wait_recv()
    else:
        mid, last = order[1], order[2]
        wide = dict(both_y=mid == "y", both_x=mid == "x")
        hop = send(mine, "down")
        mids = [send(mine, mid)]
        ends = []
        yield
        for step in range(1, RING + 1):
            if step < RING:
                hop.wait_recv()
                if step < RING - 1:
                    hop = send(at(step, False, False), "down")
                mids.append(send(at(step, False, False), mid))
            mids[step - 1].wait_recv()
            ends.append(send(at(step - 1, **wide), last))
            yield
        for copy in ends:
            copy.wait_recv()


class Paced:
    def __init__(self, groups, pace):
        self.groups, self.pace = [list(g) for g in groups], pace
        self.live, self.budget = [], 0.0

    def advance(self):
        unit = self.live.pop(0)
        try:
            next(unit)
            self.live.append(unit)
        except StopIteration:
            pass

    def begin(self):
        for unit in self.groups.pop(0):
            next(unit)
            self.live.append(unit)

    def spend(self, time):
        self.budget += time
        while self.budget >= self.pace:
            self.budget -= self.pace
            if self.live:
                self.advance()

    def drain(self):
        while self.live:
            self.advance()


PACE = 3.2
FLAT_PACE = 1.4
FLOW_PACE = 1.5
DEPTH = 6


class Flow:
    def __init__(self, units, pace, depth):
        self.waiting, self.pace, self.depth = list(units), pace, depth
        self.live, self.budget, self.done = [], 0.0, []

    def fill(self):
        while self.waiting and len(self.live) < self.depth:
            unit = self.waiting.pop(0)
            next(unit)
            self.live.append(unit)

    def advance(self):
        self.fill()
        unit = self.live.pop(0)
        try:
            next(unit)
            self.live.append(unit)
        except StopIteration:
            self.done.append(unit)
            self.fill()

    def spend(self, time):
        self.budget += time
        while self.budget >= self.pace:
            self.budget -= self.pace
            if self.live or self.waiting:
                self.advance()

    def until(self, units):
        while any(all(u is not d for d in self.done) for u in units):
            self.advance()

    def drain(self):
        while self.live or self.waiting:
            self.advance()


class Locals:
    def __init__(self, sems):
        self.sems, self.made = sems, []

    def start(self, src, dst):
        copy = pltpu.make_async_copy(src, dst, self.sems.at[len(self.made)])
        copy.start()
        self.made.append(copy)
        return len(self.made) - 1

    def wait(self, *which):
        for at in which:
            if self.made[at] is not None:
                self.made[at].wait()
                self.made[at] = None

    def finish(self):
        self.wait(*range(len(self.made)))


def gather_flat(order, place, whole, base, rows, cols, send):
    def at(step, both_y):
        first = place.ring(step) * 2
        row = first * rows if both_y else (first + place.y) * rows
        return whole.at[
            pl.ds(pl.multiple_of(row, rows), rows * (2 if both_y else 1)), pl.ds(base, cols)
        ]

    both, ends = order == "yz", []
    if both:
        first = send(at(0, False), "y")
        yield
        first.wait_recv()
    for step in range(RING):
        if step:
            hop.wait_recv()
        if step < RING - 1:
            hop = send(at(step, both), "down")
        if not both:
            ends.append(send(at(step, False), "y"))
        yield
    for copy in ends:
        copy.wait_recv()


def is_flat(which):
    return which >= 5


def own_block(place, which, whole, unit, rows, cols):
    col = unit * cols if is_flat(which) else unit * 2 * cols + place.x * cols
    return whole.at[
        pl.ds(pl.multiple_of((place.z * 2 + place.y) * rows, rows), rows),
        pl.ds(pl.multiple_of(col, LANES), cols),
    ]


def gather_groups(place, sizes, whole, copies, orders):
    rows, cols, units_of = sizes
    units = [
        gather_unit(
            order, place, whole[which], unit * cols * (1 if is_flat(which) else 2), rows, cols, copies
        )
        for (which, unit), order in zip(
            ((w, u) for w, count in enumerate(units_of) for u in range(count)), orders, strict=True
        )
    ]
    return [units[k : k + 4] for k in range(0, len(units), 4)]


def place_own(place, sizes, which, master, whole):
    rows, cols, units_of = sizes
    for unit in range(units_of[which]):
        if len(master.shape) == 3:
            block = master[unit]
        elif master.shape[0] == rows:
            block = master[:, unit * cols : (unit + 1) * cols]
        else:
            block = master[unit * cols : (unit + 1) * cols].T
        own_block(place, which, whole, unit, rows, cols)[...] = block.astype(low_type)


ANY_SPEC = pl.BlockSpec(memory_space=pl.ANY)
VMEM_SPEC = pl.BlockSpec(memory_space=pltpu.VMEM)


def norm_rows(values_in, gain_row, bias_row):
    return norm_forward(values_in, gain_row, bias_row)[0]


def loop_rows(count, tile, body):
    @pl.loop(0, count // tile)
    def _(i):
        body(pl.ds(pl.multiple_of(i * tile, tile), tile))


def exchange_rows(place, copies, n, sent, landed, make):
    theirs = pl.ds(pl.multiple_of((1 - place.c) * n, LANES), n)
    sent[...] = make(theirs).astype(low_type)
    return copies.start(place, sent, landed, "c")


def own_tiles(place, n, body):
    @pl.loop(0, n // LANES)
    def _(i):
        tile = pl.ds(pl.multiple_of(i * LANES, LANES), LANES)
        body(tile, pl.ds(pl.multiple_of(place.c * n + i * LANES, LANES), LANES))


def blocks_of(place, rows_count, pair_count, span):
    def at(block):
        rows = pl.ds(pl.multiple_of(block * BLOCK, BLOCK), BLOCK)
        if span == pair_count:
            return rows, 0
        ends = (place.x * (rows_count // BLOCK) + block + 1) * BLOCK
        return rows, pl.multiple_of(jnp.maximum(ends - span, 0), BLOCK)

    return at


def fill_biases(place, bias, segment, span):
    count = segment.shape[1]
    ids = segment[...].astype(f32)
    half = count // 2
    for block in range(bias.shape[0]):
        first = place.x * half + block * BLOCK
        mine = segment[:, pl.ds(pl.multiple_of(first, BLOCK), BLOCK)].astype(f32)
        lows = jnp.zeros(mine.shape, f32)
        for doc in range(DOCS - 1):
            size = jnp.sum(jnp.where(ids == doc, 1.0, 0.0), axis=1, keepdims=True)
            lows += jnp.where(mine > doc, size, 0.0)
        start = jnp.maximum(first + BLOCK - span, 0)
        keys = lax.broadcasted_iota(jnp.int32, bias.shape[1:], 0)
        rows = first - start + lax.broadcasted_iota(jnp.int32, bias.shape[1:], 1)
        seen = (keys.astype(f32) >= lows - start.astype(f32)) & (keys <= rows)
        bias[block] = jnp.where(seen, 0.0, masked_score)


def fill_enc_bias(bias, length):
    keys = lax.broadcasted_iota(jnp.int32, bias.shape, 0)
    bias[...] = jnp.where(keys < length, 0.0, masked_score)


def forward_kernel(sizes, window, n_out, *refs):
    n_weights = len(sizes[2])
    segment, gains, biases, enc_length, tokens_in, g_own, enc_own, *master_in = refs[: 7 + n_weights]
    at = 7 + n_weights
    g_all, *outs = refs[at : at + n_out]
    at += n_out
    held = refs[at : at + n_out - 1]
    at += n_out - 1
    masters = refs[at : at + n_weights]
    tokens, sent, landed, bias_one, bias_two, send_sems, recv_sems, local_sems = refs[at + n_weights :]
    whole = held[:n_weights]
    (
        rows_one, enc_all, q_one, pair_one, context_one, lse_one, residual_one, rows_two, q_two, pair_two,
        context_two, lse_two, residual_two, rows_three, active, slope,
    ) = held[n_weights:]
    qkv_w, out_w, query_w, pair_w, back_w, up_w, _ = whole
    place = Place()
    copies = Copies(send_sems, recv_sems)
    local = Locals(local_sems)
    x, c = place.x, place.c
    n, e = tokens.shape[0], enc_own.shape[0]
    heads_width = q_one.shape[1]
    mine = pl.ds(pl.multiple_of(c * n, 16), n)
    tokens_at = local.start(tokens_in, tokens)
    masters_at = [local.start(src, dst) for src, dst in zip(master_in, masters)]

    def flush(*names):
        for ref in names:
            local.start(ref, outs[[h is ref for h in held].index(True)])

    def part_of(ref, xx, cc, size):
        return ref.at[pl.ds(pl.multiple_of((xx * 2 + cc) * size, 16), size)]

    enc_at = local.start(enc_own, part_of(enc_all, x, c, e))
    local.start(g_own, part_of(g_all, x, c, n))
    greet(place, ("x", "y", "c", "down", "up"))
    local.wait(tokens_at)
    h_own = part_of(rows_one, x, c, n)

    @pl.loop(0, n // LANES)
    def _(i):
        tile = pl.ds(pl.multiple_of(i * LANES, LANES), LANES)
        normed = norm_rows(tokens[tile].astype(f32), gains[0:1], biases[0:1])
        rows_one[pl.ds(pl.multiple_of((x * 2 + c) * n + i * LANES, LANES), LANES)] = normed.astype(low_type)

    hx = copies.start(place, h_own, h_own, "x")
    hc = copies.start(place, h_own, h_own, "c")
    orders = FORWARD_ORDERS
    groups = gather_groups(place, sizes, whole, copies, orders)

    def rows_unit(own_x, own_c, ref, size, also):
        yield
        yield
        own_x.wait_recv()
        far = part_of(ref, 1 - x, c, size)
        over = copies.start(place, far, far, "c")
        yield
        yield
        for copy in (own_c, over, *also):
            copy.wait_recv()

    groups[0].append(rows_unit(hx, hc, rows_one, n, ()))
    for which in range(n_weights):
        local.wait(masters_at[which])
        place_own(place, sizes, which, masters[which], whole[which])
        if which == 1:
            comm = Flow(groups[0], FLOW_PACE, len(groups[0]))
            comm.fill()
    local.wait(enc_at)
    e_own = part_of(enc_all, x, c, e)
    ex = copies.start(place, e_own, e_own, "x")
    ec = copies.start(place, e_own, e_own, "c")

    groups[1].append(rows_unit(ex, ec, enc_all, e, ()))
    comm.waiting.extend(groups[1] + groups[2] + groups[3])
    comm.depth = DEPTH
    fill_biases(place, bias_one, segment, window)
    fill_enc_bias(bias_two, enc_length[0])

    def attention(q_ref, pair_ref, bias_of, o_ref, lse_ref, span):
        block_at = blocks_of(place, q_ref.shape[0], pair_ref.shape[0], span)
        for pair in range(heads_width // PAIR):
            comm.spend(4.0)
            lanes = pl.ds(pair * PAIR, PAIR)
            value_lanes = pl.ds(heads_width + pair * PAIR, PAIR)

            @pl.loop(0, q_ref.shape[0] // BLOCK)
            def _(block):
                rows, start = block_at(block)
                here = pl.ds(start, span)
                o_ref[rows, lanes], lse_ref[pair, block] = attend_step(
                    q_ref[rows, lanes],
                    pair_ref[here, lanes],
                    pair_ref[here, value_lanes],
                    bias_of(block),
                )

    def branch(at, context, weight, before, after, gain_at, rows_ref):
        over = exchange_rows(
            place, copies, n, sent.at[at], landed.at[at],
            lambda rows: outer_cols(context[rows], weight[...]),
        )

        after[...] = before[...].astype(f32) + outer_cols(context[mine], weight[...])
        over.wait_recv()

        def rest(tile, rows):
            total = after[tile] + landed[at, tile].astype(f32)
            after[tile] = total
            rows_ref[rows] = norm_rows(
                total, gains[gain_at : gain_at + 1], biases[gain_at : gain_at + 1]
            ).astype(low_type)

        own_tiles(place, n, rest)
        return copies.start(place, rows_ref.at[mine], rows_ref.at[mine], "c")

    comm.until(groups[0])
    flush(rows_one, qkv_w, out_w)

    def project(rows):
        first = pl.ds(pl.multiple_of(x * 2 * n + rows.start, BLOCK), rows.size)
        q_one[rows] = matmul(rows_one[first], qkv_w[:, :heads_width]).astype(low_type)

    loop_rows(2 * n, BLOCK, project)
    comm.spend(2.0)
    loop_rows(
        4 * n, BLOCK, lambda r: store(pair_one, r, matmul(rows_one[r], qkv_w[:, heads_width:]))
    )
    flush(q_one, pair_one)
    comm.spend(4.0)
    attention(q_one, pair_one, lambda block: bias_one[block], context_one, lse_one, window)
    over = branch(0, context_one, out_w, tokens, residual_one, 1, rows_two)
    flush(context_one, lse_one, residual_one)
    comm.spend(5.0)
    comm.until(groups[1])
    g_mine = part_of(g_all, x, c, n)
    gx = copies.start(place, g_own, g_mine, "x")
    gc = copies.start(place, g_own, g_mine, "c")
    loop_rows(
        enc_all.shape[0], BLOCK, lambda r: store(pair_two, r, matmul(enc_all[r], pair_w[...]))
    )
    flush(query_w, pair_w, back_w, enc_all, pair_two)
    over.wait_recv()
    comm.spend(3.0)
    loop_rows(2 * n, BLOCK, lambda r: store(q_two, r, matmul(rows_two[r], query_w[...])))
    flush(rows_two, q_two)
    attention(
        q_two, pair_two, lambda block: bias_two[...], context_two, lse_two, enc_all.shape[0]
    )
    chip = rows_three.at[pl.ds(pl.multiple_of(x * 2 * n, BLOCK), 2 * n)]
    over = branch(1, context_two, back_w, residual_one, residual_two, 2, chip)
    h_three = part_of(rows_three, x, c, n)
    far_over = copies.start(place, h_three, h_three, "x")
    flush(context_two, lse_two, residual_two)
    comm.spend(5.0)
    over.wait_recv()
    comm.until(groups[2])

    def up(chip_at, rows):
        here = pl.ds(pl.multiple_of(chip_at * 2 * n + rows.start, BLOCK), rows.size)
        inner = matmul(rows_three[here], up_w[...])
        gate = 1.0 / (1.0 + jnp.exp(-inner))
        active[here] = (inner * gate).astype(low_type)
        slope[here] = (gate * (1.0 + inner * (1.0 - gate))).astype(low_type)

    loop_rows(2 * n, BLOCK, lambda rows: up(x, rows))
    gx.wait_recv()
    g_far = part_of(g_all, 1 - x, c, n)
    gxc = copies.start(place, g_far, g_far, "c")
    far_over.wait_recv()
    far = part_of(rows_three, 1 - x, c, n)
    over = copies.start(place, far, far, "c")
    comm.spend(3.0)
    over.wait_recv()
    flush(rows_three, up_w)
    loop_rows(2 * n, BLOCK, lambda rows: up(1 - x, rows))
    flush(active, slope)
    gc.wait_recv()
    gxc.wait_recv()
    comm.drain()
    flush(whole[-1])
    local.finish()
    copies.finish()


def store(ref, rows, values_in):
    ref[rows] = values_in.astype(ref.dtype)


def low(*shape):
    return jax.ShapeDtypeStruct(shape, low_type)


def wide(*shape):
    return jax.ShapeDtypeStruct(shape, f32)


def scratch_like(shapes):
    return [pltpu.VMEM(s.shape, s.dtype) for s in shapes]


def forward(segment, gains, biases, enc_lens, tokens, g_own, enc_own, masters, sizes, window):
    rows, cols, units_of = sizes
    n, width = tokens.shape
    e = enc_own.shape[0]
    hidden = cols * units_of[-1]
    heads_width = 2 * cols
    n_units = sum(units_of)
    n_copies = 16 + n_units * 11
    lse = wide(heads_width // PAIR, 2 * n // BLOCK, 1, 2 * BLOCK)
    held = [low(width, cols * k * (1 if is_flat(w) else 2)) for w, k in enumerate(units_of)] + [
        low(4 * n, width), low(4 * e, width),
        low(2 * n, heads_width), low(4 * n, 2 * heads_width), low(2 * n, heads_width), lse, wide(n, width),
        low(2 * n, width), low(2 * n, heads_width), low(4 * e, 2 * heads_width), low(2 * n, heads_width), lse,
        wide(n, width), low(4 * n, width), low(4 * n, hidden), low(4 * n, hidden),
    ]
    out_shape = [low(4 * n, width)] + held
    return pl.pallas_call(
        functools.partial(forward_kernel, sizes, window, len(out_shape)),
        out_shape=out_shape,
        in_specs=[VMEM_SPEC] * 3
        + [pl.BlockSpec(memory_space=pltpu.SMEM)]
        + [ANY_SPEC] * (3 + len(masters)),
        out_specs=[ANY_SPEC] * len(out_shape),
        scratch_shapes=scratch_like(held + masters + [tokens])
        + scratch_like([low(2, n, width)] * 2)
        + scratch_like([wide(2 * n // BLOCK, window, BLOCK), wide(4 * e, BLOCK)])
        + [
            pltpu.SemaphoreType.DMA((n_copies,)),
            pltpu.SemaphoreType.DMA((n_copies,)),
            pltpu.SemaphoreType.DMA((3 + len(masters) + len(held),)),
        ],
        compiler_params=pltpu.CompilerParams(
            collective_id=2, has_side_effects=True, vmem_limit_bytes=62 * MIB
        ),
        name="forward",
    )(segment, gains, biases, enc_lens, tokens, g_own, enc_own, *masters)


REDUCE_ORDERS = ("xyz", "xzy", "yxz", "yzx")
CHUNK_ORDER = tuple(range(1, RING)) + (0,)


def reduce_unit(order, place, part, base, rows, cols, recv, out, copies):
    x, y = place.x, place.y

    def at(step, row_of, col_of):
        first = place.ring(step) * 2
        row = first * rows if row_of is None else (first + row_of) * rows
        col = base if col_of is None else base + col_of * cols
        return part.at[
            pl.ds(pl.multiple_of(row, rows), rows * (2 if row_of is None else 1)),
            pl.ds(pl.multiple_of(col, LANES), cols * (2 if col_of is None else 1)),
        ]

    used = [0]

    def landing(shape):
        height = shape[0] * (shape[1] // cols)
        where = [
            recv.at[pl.ds(used[0] + k * shape[0], shape[0])] for k in range(shape[1] // cols)
        ]
        used[0] += height
        return where

    def add(target, source):
        target[...] = target[...] + source[...]

    def exchange(step, which, mid):
        sent = []
        if which == "x":
            if mid:
                spots = [(at(step, y, 1 - x), at(step, y, x))]
            else:
                spots = [(at(step, None, 1 - x), at(step, None, x))]
        else:
            if mid:
                spots = [(at(step, 1 - y, x), at(step, y, x))]
            else:
                spots = [(at(step, 1 - y, k), at(step, y, k)) for k in range(2)]
        for src, keep_at in spots:
            (land,) = landing((src.shape[0], cols))
            sent.append((copies.start(place, src, land, which), keep_at, land))
        return sent

    def take(sent):
        for copy, keep_at, land in sent:
            copy.wait_recv()
            add(keep_at, land)

    def ring_hop(step, spots, ready, arrived):
        if step in ready:
            take(ready[step])
        for (copy, land), spot in zip(arrived or [], spots):
            copy.wait_recv()
            add(spot, land)
        sent = []
        if step != 0:
            for spot in spots:
                (land,) = landing((spot.shape[0], cols))
                sent.append((copies.start(place, spot, land, "down"), land))
        return sent

    first, middle, last = order
    outer, inner = {}, {}
    for step in CHUNK_ORDER[:2]:
        outer[step] = exchange(step, first, False)
    yield
    hop = None
    for k, step in enumerate(CHUNK_ORDER):
        take(outer[step])
        if k + 2 < RING:
            outer[CHUNK_ORDER[k + 2]] = exchange(CHUNK_ORDER[k + 2], first, False)
        if last == "z":
            inner[step] = exchange(step, middle, True)
            if k > 0:
                hop = ring_hop(CHUNK_ORDER[k - 1], [at(CHUNK_ORDER[k - 1], y, x)], inner, hop)
        else:
            if first == "x":
                spots = [at(step, None, x)]
            else:
                spots = [at(step, y, half) for half in range(2)]
            hop = ring_hop(step, spots, {}, hop)
        yield
    if last == "z":
        take(inner[0])
        ((copy, land),) = hop
    else:
        src = at(0, 1 - y, x) if last == "y" else at(0, y, 1 - x)
        (land,) = landing((rows, cols))
        copy = copies.start(place, src, land, last)
        yield
    copy.wait_recv()
    out[...] = at(0, y, x)[...].astype(f32) + land[...].astype(f32)


def reduce_flat(order, place, part, base, rows, cols, recv, out, copies):
    y = place.y

    def at(step, both_y, row_of=y):
        first = place.ring(step) * 2
        row = first * rows if both_y else (first + row_of) * rows
        return part.at[
            pl.ds(pl.multiple_of(row, rows), rows * (2 if both_y else 1)), pl.ds(base, cols)
        ]

    used = [0]

    def send(src, which):
        land = recv.at[pl.ds(used[0], src.shape[0])]
        used[0] += src.shape[0]
        return copies.start(place, src, land, which), land

    def add(target, sent):
        copy, land = sent
        copy.wait_recv()
        target[...] = target[...] + land[...]

    both = order == "zy"
    outer, hop = {}, None
    if not both:
        for step in CHUNK_ORDER[:2]:
            outer[step] = send(at(step, False, 1 - y), "y")
        yield
    for k, step in enumerate(CHUNK_ORDER):
        spot = at(step, both)
        if not both:
            add(spot, outer[step])
            if k + 2 < RING:
                ahead = CHUNK_ORDER[k + 2]
                outer[ahead] = send(at(ahead, False, 1 - y), "y")
        if step != 0:
            if hop is not None:
                add(spot, hop)
            hop = send(spot, "down")
            yield
    if both:
        add(at(0, True), hop)
        hop = send(at(0, False, 1 - y), "y")
        yield
    copy, land = hop
    copy.wait_recv()
    out[...] = at(0, False)[...].astype(f32) + land[...].astype(f32)


def flat_group(place, rows, cols, part, recv, outs, copies, first, orders):
    return [
        reduce_flat(order, place, part, unit * cols, rows, cols, recv.at[first + unit], outs[unit], copies)
        for unit, order in enumerate(orders)
    ]


def reduce_group(place, rows, cols, part, recv, outs, copies, first, orders):
    return [
        reduce_unit(
            order, place, part, unit * 2 * cols, rows, cols, recv.at[first + unit], outs[unit], copies
        )
        for unit, order in enumerate(orders)
    ]


def attention_back(place, comm, q_ref, pair_ref, bias_of, o_ref, do_ref, lse_ref, span, dk_sum, dv_sum, pairs):
    heads_width = q_ref.shape[1]
    block_at = blocks_of(place, q_ref.shape[0], pair_ref.shape[0], span)
    for pair in pairs:
        lanes = pl.ds(pair * PAIR, PAIR)
        value_lanes = pl.ds(heads_width + pair * PAIR, PAIR)
        dk_sum[...] = jnp.zeros_like(dk_sum)
        dv_sum[...] = jnp.zeros_like(dv_sum)

        @pl.loop(0, q_ref.shape[0] // BLOCK)
        def _(block):
            rows, start = block_at(block)
            here = pl.ds(start, span)
            dq, dk, dv = attend_back_step(
                q_ref[rows, lanes],
                pair_ref[here, lanes],
                pair_ref[here, value_lanes],
                bias_of(block),
                o_ref[rows, lanes],
                do_ref[rows, lanes],
                lse_ref[pair, block],
            )
            q_ref[rows, lanes] = dq
            dk_sum[here] += dk
            dv_sum[here] += dv

        pair_ref[:, lanes] = dk_sum[...].astype(low_type)
        pair_ref[:, value_lanes] = dv_sum[...].astype(low_type)
        comm.spend(6.0)


def loop_cols(count, tile, body):
    loop_rows(count, tile, body)


def norm_back_tile(small, at, incoming, before, gain_row):
    _, unit_rows, inverse = norm_forward(before, jnp.ones_like(gain_row), jnp.zeros_like(gain_row))
    result, gain_sum, bias_sum = norm_backward(incoming, unit_rows, inverse, gain_row)
    small[at : at + 1] += gain_sum[None]
    small[at + 3 : at + 4] += bias_sum[None]
    return result


def back_one_kernel(sizes, *refs):
    rows, cols = sizes
    (
        enc_length, gains, lse_two,
        down_in, up_in, active_in, slope_in, g_in, rows_in, residual_in, q_in, pair_in, context_in, back_in,
        down_sum, up_sum, small, out_tokens, grad_out, back_out, dq_out, dpair_out,
        down_w, up_w, active, slope, g_all, rows_three, residual, q_two, pair_two, context, back_w,
        part_down, part_up, recv, sent, landed, grad, g_two, back_part, grad_context, tokens_out, dk_sum, dv_sum,
        bias, out_total, send_sems, recv_sems, local_sems,
    ) = refs
    place = Place()
    copies = Copies(send_sems, recv_sems)
    local = Locals(local_sems)
    x, c = place.x, place.c
    g_at, active_at, down_at, slope_at, rows_at, up_at, res_at, con_at, back_at, q_at, pair_at = [
        local.start(src, dst)
        for src, dst in (
            (g_in, g_all), (active_in, active), (down_in, down_w), (slope_in, slope), (rows_in, rows_three),
            (up_in, up_w), (residual_in, residual), (context_in, context), (back_in, back_w),
            (q_in, q_two), (pair_in, pair_two),
        )
    ]
    greet(place, ("x", "y", "c", "down", "up"))
    n, width = residual.shape
    mine = pl.ds(pl.multiple_of(c * n, 16), n)
    comm = Paced(
        [
            flat_group(
                place, rows, cols, part_down, recv, [down_sum.at[k] for k in range(4)], copies, 0,
                ("yz", "zy", "yz", "yz"),
            ),
            flat_group(
                place, rows, cols, part_up, recv, [up_sum.at[k] for k in range(4)], copies, 4,
                ("yz", "yz", "zy", "yz"),
            ),
        ],
        FLAT_PACE,
    )
    small[...] = jnp.zeros_like(small)
    fill_enc_bias(bias, enc_length[0])

    def on_chip(chip, local_rows):
        return pl.ds(pl.multiple_of(chip * 2 * n + local_rows.start, LANES), local_rows.size)

    local.wait(g_at, down_at, slope_at)

    def inner(tile):
        slope[tile] = (matmul(g_all[tile], down_w[...]) * slope[tile].astype(f32)).astype(low_type)

    loop_rows(4 * n, BLOCK, inner)
    local.wait(up_at)

    def up_term(chip, local_rows):
        return outer_cols(slope[on_chip(chip, local_rows)], up_w[...])

    def down_term(chip, local_rows):
        return outer_cols(active[on_chip(chip, local_rows)], down_w[...])

    far_over = exchange_rows(
        place, copies, n, sent.at[0], landed.at[0], lambda r: up_term(1 - x, r)
    )
    near_over = exchange_rows(place, copies, n, sent.at[1], landed.at[1], lambda r: up_term(x, r))
    grad[...] = up_term(x, mine)
    far_over.wait_recv()
    sent[2] = (up_term(1 - x, mine) + landed[0].astype(f32)).astype(low_type)
    chip_over = copies.start(place, sent.at[2], landed.at[2], "x")
    local.wait(active_at)
    loop_cols(width, BLOCK, lambda t: store(part_down, t, inner_rows(g_all[:, t], active[...])))
    comm.begin()
    local.wait(rows_at)
    loop_cols(width, BLOCK, lambda t: store(part_up, t, inner_rows(rows_three[:, t], slope[...])))
    comm.spend(4.8)
    comm.begin()
    out_far = exchange_rows(
        place, copies, n, sent.at[3], landed.at[3], lambda r: down_term(1 - x, r)
    )
    out_near = exchange_rows(place, copies, n, sent.at[4], landed.at[4], lambda r: down_term(x, r))
    local.wait(res_at)
    out_total[...] = residual[...] + down_term(x, mine)
    comm.spend(3.0)
    out_far.wait_recv()
    sent[5] = (down_term(1 - x, mine) + landed[3].astype(f32)).astype(low_type)
    out_chip = copies.start(place, sent.at[5], landed.at[5], "x")
    comm.spend(1.5)
    near_over.wait_recv()
    chip_over.wait_recv()

    def norm_part(tile, rows_here):
        incoming = grad[tile] + landed[1, tile].astype(f32) + landed[2, tile].astype(f32)
        total = g_all[on_chip(x, rows_here)].astype(f32) + norm_back_tile(
            small, 2, incoming, residual[tile], gains[2:3]
        )
        grad[tile] = total
        g_two[rows_here] = total.astype(low_type)

    own_tiles(place, n, norm_part)
    g_over = copies.start(place, g_two.at[mine], g_two.at[mine], "c")
    local.start(grad, grad_out)
    comm.spend(5.5)
    local.wait(con_at, back_at)
    g_over.wait_recv()
    loop_rows(2 * n, BLOCK, lambda r: store(grad_context, r, matmul(g_two[r], back_w[...])))
    loop_cols(width, BLOCK, lambda t: store(back_part, t, inner_rows(g_two[:, t], context[...])))
    local.start(back_part, back_out)
    comm.spend(3.0)
    local.wait(q_at, pair_at)
    attention_back(
        place, comm, q_two, pair_two, lambda block: bias[...], context, grad_context, lse_two, pair_two.shape[0], dk_sum, dv_sum, range(q_two.shape[1] // PAIR),
    )
    local.start(q_two, dq_out)
    local.start(pair_two, dpair_out)
    out_near.wait_recv()
    out_chip.wait_recv()
    tokens_out[...] = (out_total[...] + landed[4].astype(f32) + landed[5].astype(f32)).astype(low_type)
    local.start(tokens_out, out_tokens)
    comm.drain()
    local.finish()
    copies.finish()


def back_one(enc_lens, gains, lse_two, down_w, up_w, active, slope, g_all, rows_three, residual, q_two, pair_two, context, back_w, rows, cols):
    n, width = residual.shape
    heads_width = q_two.shape[1]
    hbm = [down_w, up_w, active, slope, g_all, rows_three, residual, q_two, pair_two, context, back_w]
    out_shape = [
        wide(4, rows, cols), wide(4, rows, cols), wide(8, width), low(n, width), wide(n, width),
        low(width, heads_width), low(2 * n, heads_width), low(*pair_two.shape),
    ]
    n_copies = 8 * 7 + 8
    return pl.pallas_call(
        functools.partial(back_one_kernel, (rows, cols)),
        out_shape=out_shape,
        in_specs=[pl.BlockSpec(memory_space=pltpu.SMEM)] + [VMEM_SPEC] * 2 + [ANY_SPEC] * len(hbm),
        out_specs=[VMEM_SPEC] * 3 + [ANY_SPEC] * 5,
        scratch_shapes=scratch_like(hbm)
        + scratch_like(
            [
                low(*down_w.shape), low(*up_w.shape), low(8, rows * 7, cols), low(6, n, width),
                low(6, n, width), wide(n, width), low(2 * n, width), low(width, heads_width),
                low(2 * n, heads_width), low(n, width), wide(pair_two.shape[0], PAIR), wide(pair_two.shape[0], PAIR),
                wide(pair_two.shape[0], BLOCK), wide(n, width),
            ]
        )
        + [
            pltpu.SemaphoreType.DMA((n_copies,)),
            pltpu.SemaphoreType.DMA((n_copies,)),
            pltpu.SemaphoreType.DMA((len(hbm) + 5,)),
        ],
        compiler_params=pltpu.CompilerParams(
            collective_id=1, has_side_effects=True, vmem_limit_bytes=60 * MIB
        ),
        name="back_one",
    )(enc_lens, gains, lse_two, *hbm)


def back_two_kernel(sizes, window, *refs):
    rows, cols = sizes
    (
        segment, gains, lse_one, small_in,
        dq_in, dpair_in, rows_two_in, enc_in, query_in, pair_w_in, back_in, grad_in, residual_in, context_in,
        out_w_in, q_in, pair_in, rows_one_in, qkv_in, tokens_in,
        back_sum, query_sum, pair_sum, out_sum, qkv_sum, small_out, in_grad, enc_grad,
        dq_two, dpair_two, grad, residual, context, out_w, q_one, pair_one, tokens,
        rows_held, qkv_w, part_cross, part_out, part_half, recv, sent, landed, total, g_one, grad_context, dk_sum, dv_sum,
        enc_sent, enc_landed, enc_total, small_recv, bias, send_sems, recv_sems, local_sems,
    ) = refs
    place = Place()
    copies = Copies(send_sems, recv_sems)
    local = Locals(local_sems)
    x, c = place.x, place.c
    n, width = residual.shape
    heads_width = q_one.shape[1]
    e = enc_grad.shape[0]
    enc_all = rows_held.at[pl.ds(0, enc_in.shape[0])]
    rows_two = rows_held.at[pl.ds(enc_in.shape[0], 2 * n)]
    rows_one = rows_held.at[pl.ds(0, rows_one_in.shape[0])]
    query_w = qkv_w.at[:, pl.ds(0, heads_width)]
    pair_w = qkv_w.at[:, pl.ds(heads_width, 2 * heads_width)]
    (
        dpair_at, enc_at, dq_at, rows_two_at, back_at, query_at, pair_w_at, grad_at, res_at, con_at,
        out_w_at, q_at, pair_at, tokens_at,
    ) = [
        local.start(src, dst)
        for src, dst in (
            (dpair_in, dpair_two), (enc_in, enc_all), (dq_in, dq_two),
            (rows_two_in, rows_two), (back_in, part_cross.at[:, pl.ds(0, heads_width)]), (query_in, query_w),
            (pair_w_in, pair_w), (grad_in, grad), (residual_in, residual), (context_in, context),
            (out_w_in, out_w), (q_in, q_one), (pair_in, pair_one), (tokens_in, tokens),
        )
    ]
    greet(place, ("x", "y", "c", "down", "up", "z2"))
    mine = pl.ds(pl.multiple_of(c * n, 16), n)

    def small_unit():
        for at, which in enumerate(("c", "x", "y", "z1", "z2")):
            copy = copies.start(place, small_out.at[at], small_recv.at[at], which)
            yield
            copy.wait_recv()
            small_out[at + 1] = small_out[at] + small_recv[at]

    cross_sums = [back_sum.at[0], query_sum.at[0], pair_sum.at[0], pair_sum.at[1]]
    half = cols // 2

    def half_group(which, orders):
        lanes = pl.ds(which * half, half)
        return [
            reduce_unit(
                order, place, part_half.at[which], unit * cols, rows, half, recv.at[5 + unit, :, lanes],
                qkv_sum.at[unit, :, lanes], copies,
            )
            for unit, order in enumerate(orders)
        ]

    comm = Paced(
        [
            reduce_group(
                place, rows, cols, part_cross, recv, cross_sums, copies, 0, ("yxz", "yzx", "xzy", "yzx")
            ),
            reduce_group(place, rows, cols, part_out, recv, [out_sum.at[0]], copies, 4, ("yzx",)),
            half_group(0, ("yzx", "yzx", "xzy")),
            half_group(1, ("yxz", "yzx", "xzy")),
            [small_unit()],
        ],
        PACE,
    )
    small = small_out.at[0]
    small[...] = small_in[...]
    second = pl.ds(heads_width, heads_width)
    rest = pl.ds(2 * heads_width, 2 * heads_width)
    fill_biases(place, bias, segment, window)
    local.wait(dpair_at, enc_at)

    def pair_grads(t):
        part_cross[t, rest] = inner_rows(enc_all[:, t], dpair_two[...]).astype(low_type)

    loop_cols(width, BLOCK, pair_grads)
    comm.spend(4.0)
    local.wait(dq_at, rows_two_at, back_at)

    def query_grads(t):
        part_cross[t, second] = inner_rows(rows_two[:, t], dq_two[...]).astype(low_type)

    loop_cols(width, BLOCK, query_grads)
    comm.spend(1.5)
    comm.begin()
    rows_one_at = local.start(rows_one_in, rows_one)
    local.wait(query_at)
    over = exchange_rows(
        place, copies, n, sent.at[0], landed.at[0], lambda r: outer_cols(dq_two[r], query_w[...])
    )
    total[...] = outer_cols(dq_two[mine], query_w[...])
    comm.spend(2.2)
    local.wait(pair_w_at)

    def enc_rows(xx, cc):
        return pl.ds(pl.multiple_of((xx * 2 + cc) * e, LANES), e)

    def enc_term(xx, cc):
        return outer_cols(dpair_two[enc_rows(xx, cc)], pair_w[...])

    enc_sent[0] = enc_term(x, 1 - c).astype(low_type)
    enc_sent[1] = enc_term(1 - x, 1 - c).astype(low_type)
    enc_over = copies.start(place, enc_sent.at[pl.ds(0, 2)], enc_landed.at[pl.ds(0, 2)], "c")
    comm.spend(1.6)
    local.wait(grad_at, res_at)
    over.wait_recv()

    def norm_part(tile, rows_here):
        incoming = total[tile] + landed[0, tile].astype(f32)
        after = grad[tile] + norm_back_tile(small, 1, incoming, residual[tile], gains[1:2])
        grad[tile] = after
        g_one[rows_here] = after.astype(low_type)

    own_tiles(place, n, norm_part)
    g_over = copies.start(place, g_one.at[mine], g_one.at[mine], "c")
    comm.spend(4.0)
    enc_over.wait_recv()
    enc_sent[2] = (enc_term(1 - x, c) + enc_landed[1].astype(f32)).astype(low_type)
    enc_far = copies.start(place, enc_sent.at[2], enc_landed.at[2], "x")
    enc_total[...] = enc_term(x, c) + enc_landed[0].astype(f32)
    qkv_at = local.start(qkv_in, qkv_w)
    comm.spend(2.0)
    local.wait(con_at, out_w_at)
    g_over.wait_recv()
    loop_rows(2 * n, BLOCK, lambda r: store(grad_context, r, matmul(g_one[r], out_w[...])))

    def out_grads(t):
        part_out[t] = inner_rows(g_one[:, t], context[...]).astype(low_type)

    loop_cols(width, BLOCK, out_grads)
    comm.spend(2.6)
    comm.begin()
    local.wait(q_at, pair_at)
    n_pairs = heads_width // PAIR

    def self_back(pairs):
        attention_back(
            place, comm, q_one, pair_one, lambda block: bias[block], context, grad_context, lse_one, window,
            dk_sum, dv_sum, pairs,
        )

    chip_rows = pl.ds(pl.multiple_of(x * 2 * n, LANES), 2 * n)

    def self_grads(which):
        spots = [k * cols + which * half for k in range(2)]
        dq = jnp.concatenate([q_one[:, at : at + half] for at in spots], axis=1)
        dpair = jnp.concatenate(
            [pair_one[:, at : at + half] for at in spots + [heads_width + at for at in spots]], axis=1
        )

        def tile(t):
            part_half[which, t, pl.ds(0, cols)] = inner_rows(rows_one[chip_rows, t], dq).astype(low_type)
            part_half[which, t, pl.ds(cols, 2 * cols)] = inner_rows(rows_one[:, t], dpair).astype(low_type)

        loop_cols(width, BLOCK, tile)

    halves = [[p for p in range(n_pairs) if p * PAIR % cols // half == which] for which in range(2)]
    self_back(halves[0])
    local.wait(rows_one_at)
    self_grads(0)
    comm.spend(3.0)
    comm.begin()
    self_back(halves[1])
    enc_far.wait_recv()
    enc_total[...] += enc_landed[2].astype(f32)
    local.start(enc_total, enc_grad)
    local.wait(qkv_at)
    q_lanes, kv_lanes = pl.ds(0, heads_width), pl.ds(heads_width, 2 * heads_width)

    def key_term(xx, local_rows):
        at = pl.ds(pl.multiple_of(xx * 2 * n + local_rows.start, LANES), local_rows.size)
        return outer_cols(pair_one[at], qkv_w[:, kv_lanes])

    def query_term(local_rows):
        return outer_cols(q_one[local_rows], qkv_w[:, q_lanes])

    far_over = exchange_rows(
        place, copies, n, sent.at[1], landed.at[1], lambda r: key_term(1 - x, r)
    )
    near_over = exchange_rows(
        place, copies, n, sent.at[2], landed.at[2], lambda r: key_term(x, r) + query_term(r)
    )
    comm.spend(4.0)
    far_over.wait_recv()
    sent[3] = (key_term(1 - x, mine) + landed[1].astype(f32)).astype(low_type)
    chip_over = copies.start(place, sent.at[3], landed.at[3], "x")
    comm.spend(1.5)
    self_grads(1)
    comm.spend(3.0)
    comm.begin()
    total[...] = key_term(x, mine) + query_term(mine)
    comm.spend(2.0)
    local.wait(tokens_at)
    near_over.wait_recv()
    chip_over.wait_recv()

    def last_part(tile, rows_here):
        incoming = total[tile] + landed[2, tile].astype(f32) + landed[3, tile].astype(f32)
        grad[tile] += norm_back_tile(small, 0, incoming, tokens[tile].astype(f32), gains[0:1])

    own_tiles(place, n, last_part)
    local.start(grad, in_grad)
    comm.begin()
    comm.drain()
    local.finish()
    copies.finish()


def back_two(segment, gains, lse_one, small, hbm, rows, cols, window, enc_rows):
    grad, q_one, pair_one = hbm[7], hbm[11], hbm[12]
    n, width = grad.shape
    heads_width = q_one.shape[1]

    def sums(k):
        return wide(k, rows, cols)

    out_shape = [
        sums(1), sums(1), sums(2), sums(1), sums(3), wide(6, 8, width), wide(n, width), wide(enc_rows, width),
    ]
    n_copies = 11 * 15 + 8 + 5
    held = hbm[:2] + hbm[7:13] + hbm[15:16]
    held_rows = max(enc_rows * 4 + 2 * n, hbm[13].shape[0])
    return pl.pallas_call(
        functools.partial(back_two_kernel, (rows, cols), window),
        out_shape=out_shape,
        in_specs=[VMEM_SPEC] * 4 + [ANY_SPEC] * len(hbm),
        out_specs=[VMEM_SPEC] * 6 + [ANY_SPEC] * 2,
        scratch_shapes=scratch_like(held)
        + scratch_like(
            [
                low(held_rows, width), low(*hbm[14].shape),
                low(width, 4 * heads_width), low(width, heads_width), low(2, width, 3 * cols), low(8, rows * 15, cols),
                low(4, n, width), low(4, n, width), wide(n, width), low(2 * n, width),
                low(2 * n, heads_width), wide(pair_one.shape[0], PAIR), wide(pair_one.shape[0], PAIR),
                low(3, enc_rows, width), low(3, enc_rows, width), wide(enc_rows, width), wide(5, 8, width),
                wide(2 * n // BLOCK, window, BLOCK),
            ]
        )
        + [
            pltpu.SemaphoreType.DMA((n_copies,)),
            pltpu.SemaphoreType.DMA((n_copies,)),
            pltpu.SemaphoreType.DMA((len(hbm) + 2,)),
        ],
        compiler_params=pltpu.CompilerParams(
            collective_id=3, has_side_effects=True, vmem_limit_bytes=62 * MIB
        ),
        name="back_two",
    )(segment, gains, lse_one, small, *hbm)


BLOCK = 256


def split_heads(values_in):
    lane = lax.broadcasted_iota(jnp.int32, values_in.shape, 1)
    zero = jnp.zeros_like(values_in)
    return jnp.concatenate(
        [jnp.where(lane < HD, values_in, zero), jnp.where(lane >= HD, values_in, zero)], axis=0
    )


def key_scores(queries, keys, bias):
    return outer_cols(keys, queries) + jnp.concatenate([bias, bias], axis=1)


def attend_step(q_block, keys, values, bias):
    rows = q_block.shape[0]
    queries = split_heads(q_block * jnp.asarray(HD**-0.5, low_type))
    scores = key_scores(queries, keys, bias)
    peak = jnp.max(scores, axis=0, keepdims=True)
    probs = jnp.exp(scores - peak)
    total = jnp.sum(probs, axis=0, keepdims=True)
    context = inner_rows(values, probs.astype(low_type)) / total
    pair = jnp.concatenate([context[:HD, :rows], context[HD:, rows:]], axis=0)
    return pair.T.astype(low_type), peak + jnp.log(total)


def attend_back_step(q_block, keys, values, bias, context, grad_context, lse):
    rows = q_block.shape[0]
    queries = split_heads(q_block * jnp.asarray(HD**-0.5, low_type))
    grads = split_heads(grad_context)
    scores = key_scores(queries, keys, bias)
    probs = jnp.exp(scores - lse)
    grad_probs = outer_cols(values, grads)
    product = (grad_context.astype(f32) * context.astype(f32)).T
    inner = jnp.concatenate(
        [
            jnp.sum(product[:HD], axis=0, keepdims=True),
            jnp.sum(product[HD:], axis=0, keepdims=True),
        ],
        axis=1,
    )
    grad_scores = (probs * (grad_probs - inner)).astype(low_type)
    dv = matmul(probs.astype(low_type), grads)
    dk = matmul(grad_scores, queries)
    grad_queries = inner_rows(keys, grad_scores) * HD**-0.5
    pair = jnp.concatenate([grad_queries[:HD, :rows], grad_queries[HD:, rows:]], axis=0)
    return pair.T.astype(low_type), dk, dv


def finish_kernel(n_parts, *refs):
    parts, outs, held, sems = refs[:n_parts], refs[n_parts:-1 - n_parts], refs[-1 - n_parts : -1], refs[-1]
    local = Locals(sems)
    for src, dst in zip(parts, held):
        local.start(src, dst)
    local.finish()
    tokens_in, in_grad_in, enc_in, small, up, down, back, query, pair, out, qkv = held
    tokens_out, in_grad, enc_grad, qkv_out, out_out, query_out, pair_out, back_out, up_out, down_out, gain, bias = outs
    cols = up.shape[2]
    tokens_out[...] = tokens_in[...]
    in_grad[...] = in_grad_in[...]
    enc_grad[0] = enc_in[...]
    qkv_out[...] = qkv[...]
    out_out[...] = out[0].T
    query_out[...] = query[0]
    pair_out[...] = pair[...]
    back_out[...] = back[0].T
    for unit in range(up.shape[0]):
        up_out[:, unit * cols : (unit + 1) * cols] = up[unit]
    for unit in range(down.shape[0]):
        down_out[unit * cols : (unit + 1) * cols] = down[unit].T
    gain[...] = small[small.shape[0] - 1, 0:3]
    bias[...] = small[small.shape[0] - 1, 3:6]


def finish(*parts):
    tokens, in_grad, enc_grad, small, up, down, back, query, pair, out, qkv = parts
    rows, cols = up.shape[1:]
    width = small.shape[2]
    hidden = cols * down.shape[0]
    out_shape = [
        low(*tokens.shape), wide(*in_grad.shape), wide(1, *enc_grad.shape), wide(*qkv.shape), wide(cols, rows),
        wide(rows, cols), wide(*pair.shape), wide(cols, rows), wide(rows, hidden), wide(hidden, rows),
        wide(3, width), wide(3, width),
    ]
    return pl.pallas_call(
        functools.partial(finish_kernel, len(parts)),
        out_shape=out_shape,
        in_specs=[ANY_SPEC] * len(parts),
        out_specs=[VMEM_SPEC] * len(out_shape),
        scratch_shapes=scratch_like(parts) + [pltpu.SemaphoreType.DMA((len(parts),))],
        compiler_params=pltpu.CompilerParams(vmem_limit_bytes=62 * MIB),
        name="finish",
    )(*parts)


def width_orders(outer, width):
    def spread(values_in):
        if outer == 1:
            return values_in
        parts = values_in.reshape(values_in.shape[:-1] + (outer, RING * 2, -1))
        return jnp.swapaxes(parts, -3, -2).reshape(values_in.shape)

    def back(values_in):
        if outer == 1:
            return values_in
        parts = values_in.reshape(values_in.shape[:-1] + (RING * 2, outer, -1))
        return jnp.swapaxes(parts, -3, -2).reshape(values_in.shape)

    return spread, back


def on_device(
    tokens,
    encoder,
    seg_ids,
    enc_lens,
    attn_qkv,
    attn_out,
    cross_q,
    cross_kv,
    cross_out,
    ffn_in,
    ffn_out,
    norm_gains,
    norm_biases,
    out_grad,
):
    outer = lax.axis_size("o")
    spread, gathered_back = width_orders(outer, tokens.shape[1])
    tokens, encoder, out_grad = spread(tokens), spread(encoder[0]), spread(out_grad)
    norm_gains, norm_biases = spread(norm_gains), spread(norm_biases)
    seq_len = seg_ids.shape[1]
    cols = cross_q.shape[1]
    width = tokens.shape[1]

    def units(block):
        k = block.shape[-1] // cols
        return block.reshape(block.shape[0], k, cols).transpose(1, 0, 2)

    masters = [attn_qkv, attn_out, cross_q, cross_kv, cross_out, ffn_in, ffn_out]
    if outer > 1:
        masters = [
            attn_qkv, attn_out.T[None], cross_q[None], cross_kv, cross_out.T[None], units(ffn_in), units(ffn_out.T)
        ]
        masters = [lax.all_gather(m.astype(low_type), "o", axis=1, tiled=True) for m in masters]
    rows = cross_q.shape[0] * outer
    units_of = (3, 1, 1, 2, 1, ffn_in.shape[1] // cols, ffn_in.shape[1] // cols)
    window = min(seq_len, seq_len // 2 + BLOCK)
    (
        grads_three, qkv_w, out_w, query_w, pair_w, back_w, up_w, down_w, rows_one, enc_full, queries_one, pair_one,
        context_one, lse_one, residual_one, rows_two, queries_two, pair_two, context_two, lse_two, residual_two,
        rows_three, active, slope,
    ) = forward(
        seg_ids, norm_gains, norm_biases, enc_lens, tokens, out_grad, encoder, masters, (rows, cols, units_of), window
    )
    down_sum, up_sum, small, out_tokens, grad_two, back_grad, grad_queries, grad_pair = back_one(
        enc_lens, norm_gains, lse_two, down_w, up_w, active, slope, grads_three, rows_three, residual_two,
        queries_two, pair_two, context_two, back_w, rows, cols,
    )
    back_sum, query_sum, pair_sum, out_sum, qkv_sum, small, in_grad, enc_grad = back_two(
        seg_ids, norm_gains, lse_one, small,
        [
            grad_queries, grad_pair, rows_two, enc_full, query_w, pair_w, back_grad, grad_two, residual_one,
            context_one, out_w, queries_one, pair_one, rows_one, qkv_w, tokens,
        ],
        rows, cols, window, encoder.shape[0],
    )
    if outer == 1:
        return tuple(
            finish(
                out_tokens, in_grad, enc_grad, small, up_sum, down_sum, back_sum, query_sum, pair_sum,
                out_sum, qkv_sum,
            )
        )
    enc_grad = enc_grad[None]
    sums = [up_sum, down_sum, back_sum, query_sum, pair_sum, out_sum, qkv_sum]
    small = small[-1]
    small = lax.psum(small, "o")
    sums = [lax.psum_scatter(s, "o", scatter_dimension=1, tiled=True) for s in sums]
    up_sum, down_sum, back_sum, query_sum, pair_sum, out_sum, qkv_sum = sums

    def joined(block):
        return block.transpose(1, 0, 2).reshape(block.shape[1], -1)

    return (
        gathered_back(out_tokens),
        gathered_back(in_grad),
        gathered_back(enc_grad),
        qkv_sum,
        out_sum[0].T,
        query_sum[0],
        pair_sum,
        back_sum[0].T,
        joined(up_sum),
        joined(down_sum).T,
        gathered_back(small[:3]),
        gathered_back(small[3:6]),
    )


def solution(mesh):
    count, tensor = mesh.devices.shape
    outer = count // (RING * 2)
    fine = Mesh(
        mesh.devices.reshape(outer, RING, 2, tensor // 2, 2), ("o", "z", "y", "x", "c")
    )
    dp, tp = ("o", "z", "y"), ("x", "c")
    in_specs = (
        P(dp + tp, None),
        P(dp, tp, None),
        P(dp, None),
        P(dp),
        P(None, dp, tp),
        P(tp, dp),
        P(dp, tp),
        P(None, dp, tp),
        P(tp, dp),
        P(dp, tp),
        P(tp, dp),
        P(),
        P(),
        P(dp + tp, None),
    )
    out_specs = (
        P(dp + tp, None),
        P(dp + tp, None),
        P(dp, tp, None),
        P(None, dp, tp),
        P(tp, dp),
        P(dp, tp),
        P(None, dp, tp),
        P(tp, dp),
        P(dp, tp),
        P(tp, dp),
        P(),
        P(),
    )
    return jax.shard_map(
        on_device, mesh=fine, in_specs=in_specs, out_specs=out_specs, check_vma=False
    )
```
